32 devices in a mesh: sub: 16 (over z, y, core), smp: 2 (over x).
Axes of the slice: x: 2, y: 2, z: 4, core: 2. Of those that a mesh axis runs over, the one named last changes fastest.
Arguments:
- trial: bfloat16 [16, 2, 3, 16, 768], P('sub', None, None, 'smp'), may hold values from -6 to 6
- stiff_lam: bfloat16 [768, 768], replicated
- stiff_mu: bfloat16 [768, 768], replicated
- log_modes: float32 [2, 16, 2, 3, 15], P(None, 'sub'), may hold values from -0.6 to 0.6
- nodes: float32 [16, 15], replicated, may hold values from -1 to 1
- quad_weights: float32 [16], replicated
- chaos_index: int32 [816, 15], replicated, may hold values from 0 to 3, as said below
- bonds: int32 [3, 16, 2, 3], replicated, may hold values 0 or 1
- face_map: int32 [16, 2, 3, 128], P('sub'), may hold values from 0 to 127, each once within a row
Outputs:
- coefficients: bfloat16 [16, 2, 3, 768, 816], P('sub', None, None, 'smp')
The draws below stay inside these ranges and needn't reach their ends.
Inputs may be any that keep to these rules, and one draw needn't show every extreme that they name: Each row of chaos_index has entries summing to at most 3.
All inputs are finite; a program needn't handle non-finite values.
Results may differ from the reference program's by a relative error of at most 0.0063.
Values may be sent and summed in bfloat16 or wider, within the bound.
No kernel may reach another device: no remote copies, remote signals or barrier semaphores. Data moves between devices by JAX's collectives and lax.ppermute only.
A program may use at most 64 MiB of HBM per device.

```python
import jax
import jax.numpy as jnp
from jax import lax

FACE = 128
G = 768
P_SIZE = 816
K = 15
LX = 3
LY = 2
NZ = 16
Q = 16


def make_stiffness(key):
    first_key, second_key = jax.random.split(key)
    diagonal = jnp.exp(jax.random.uniform(first_key, (G,), jnp.float32, jnp.log(0.3), jnp.log(0.9)))
    noise = jax.random.normal(second_key, (G, G), jnp.float32)
    symmetric = (noise + noise.T) * (0.3 / jnp.sqrt(2.0 * G))
    return (jnp.diag(diagonal) + symmetric).astype(jnp.bfloat16)


def draw_stiff_lam(key, part):
    return make_stiffness(jax.random.fold_in(key, 11))


def draw_stiff_mu(key, part):
    return make_stiffness(jax.random.fold_in(key, 23))


def draw_quad_weights(key, part):
    inner = jax.random.fold_in(key, 37)
    values = jnp.exp(jax.random.uniform(inner, (Q,), jnp.float32, jnp.log(0.5), jnp.log(2.0)))
    return (values * 8.0 / Q).astype(jnp.float32)


def draw_chaos_index(key, part):
    inner = jax.random.fold_in(key, 51)
    pick_key, active_key = jax.random.split(inner)
    picks = jax.random.randint(pick_key, (P_SIZE, 3), 0, K)
    active = jax.random.randint(active_key, (P_SIZE, 3), 0, 2)
    picks = picks.at[0].set(picks[0, 0])
    active = active.at[0].set(1)
    columns = jnp.arange(K, dtype=jnp.int32)
    hits = (picks[:, :, None] == columns[None, None, :]).astype(jnp.int32) * active[:, :, None]
    return jnp.sum(hits, axis=1).astype(jnp.int32)


def plant(entries, stream_key, smallest, high):
    longest = entries.shape.index(max(entries.shape))
    spots = []
    for shift in (0, 1):
        where = [jax.random.randint(jax.random.fold_in(stream_key, axis), (), 0, length) for axis, length in enumerate(entries.shape)]
        where[longest] = (where[longest] + shift) % entries.shape[longest]
        spots.append(tuple(where))
    return entries.at[spots[0]].set(smallest).at[spots[1]].set(high)


def shard_levels(own_key, dims, cuts, least, high):
    loudness = 1.0
    for dim, blocks in cuts:
        heights = jax.random.uniform(jax.random.fold_in(jax.random.fold_in(own_key, 6), dim), (blocks,), jnp.float32, least / len(cuts), high / len(cuts))
        loudness = loudness * jnp.repeat(jnp.exp(heights), dims[dim] // blocks).reshape((-1,) + (1,) * (len(dims) - 1 - dim))
    return loudness


def centred(key, extent, deviation, reach, cuts=(), held_as=jnp.bfloat16):
    entries = deviation * jax.random.normal(key, extent, jnp.float32)
    if cuts:
        entries = entries * shard_levels(key, extent, cuts, -0.22, 0.18)
    return jnp.clip(entries, -reach, reach).astype(held_as)


def setup_inputs(seed: int = 0) -> dict:
    splits = jax.random.split(jax.random.key(seed), 10)
    trial = centred(splits[0], (NZ, LY, LX, Q, G), 1.0, 6.0, ((0, 16), (3, 2)))
    stiff_lam = draw_stiff_lam(jax.random.fold_in(splits[9], 71), 0)
    stiff_mu = draw_stiff_mu(jax.random.fold_in(splits[9], 71), 0)
    log_modes = centred(splits[3], (2, NZ, LY, LX, K), 0.15, 0.6, ((1, 16),), jnp.float32)
    nodes = jnp.clip(jax.random.uniform(splits[4], (Q, K), jnp.float32, -1.0, 1.0), -1.0, 1.0)
    quad_weights = draw_quad_weights(jax.random.fold_in(splits[9], 71), 0)
    chaos_index = draw_chaos_index(jax.random.fold_in(splits[9], 71), 0)
    bonds = plant((jax.random.randint(splits[7], (3, NZ, LY, LX), 0, 8) < 7).astype(jnp.int32), jax.random.fold_in(splits[7], 1), 0, 1)
    face_map = jax.vmap(lambda own: jax.random.permutation(own, FACE))(jax.random.split(splits[8], NZ * LY * LX)).reshape((NZ, LY, LX, FACE)).astype(jnp.int32)
    return dict(trial=trial, stiff_lam=stiff_lam, stiff_mu=stiff_mu, log_modes=log_modes, nodes=nodes, quad_weights=quad_weights, chaos_index=chaos_index, bonds=bonds, face_map=face_map)


def legendre(points):
    second = jnp.sqrt(5.0) * (1.5 * points * points - 0.5)
    third = jnp.sqrt(7.0) * (2.5 * points * points * points - 1.5 * points)
    return [jnp.ones_like(points), jnp.sqrt(3.0) * points, second, third]

def chaos_basis(nodes, chaos_index, quad_weights):
    table = jnp.stack(legendre(nodes), axis=-1).reshape(nodes.shape[0], -1)
    columns = jnp.arange(chaos_index.shape[1], dtype=jnp.int32)[:, None] * 4 + chaos_index.T.astype(jnp.int32)
    picked = jnp.take(table, columns, axis=1)
    total = jnp.prod(picked, axis=1)
    return (quad_weights[:, None] * total).astype(jnp.bfloat16)

def schur(field, lame_first, lame_shear, stiff_lam, stiff_mu):

    def one_layer(pieces):
        block, first_layer, shear_layer = pieces
        flattened = block.reshape(-1, block.shape[-1])
        part_one = jnp.dot(flattened, stiff_lam, preferred_element_type=jnp.float32).reshape(block.shape)
        part_two = jnp.dot(flattened, stiff_mu, preferred_element_type=jnp.float32).reshape(block.shape)
        return first_layer[..., None] * part_one + shear_layer[..., None] * part_two
    return lax.map(one_layer, (field, lame_first, lame_shear))

def face_jumps(field, bonds, face_map):
    layers, height, breadth, samples, width = field.shape
    size = width // 6
    faces = field.reshape(layers, height, breadth, samples, 6, size)
    minus_x, plus_x = (faces[..., 0, :], faces[..., 1, :])
    minus_y, plus_y = (faces[..., 2, :], faces[..., 3, :])
    minus_z, plus_z = (faces[..., 4, :], faces[..., 5, :])
    bond = bonds.astype(jnp.float32)[..., None, None]
    bond_x, bond_y, bond_z = (bond[0], bond[1], bond[2])
    jump_mx = jnp.roll(bond_x, 1, axis=2) * (minus_x - jnp.roll(plus_x, 1, axis=2))
    jump_px = bond_x * (plus_x - jnp.roll(minus_x, -1, axis=2))
    jump_my = jnp.roll(bond_y, 1, axis=1) * (minus_y - jnp.roll(plus_y, 1, axis=1))
    jump_py = bond_y * (plus_y - jnp.roll(minus_y, -1, axis=1))
    index = jnp.broadcast_to(face_map[:, :, :, None, :], minus_z.shape)
    inverse = jnp.argsort(face_map, axis=-1).astype(jnp.int32)
    reverse = jnp.broadcast_to(inverse[:, :, :, None, :], minus_z.shape)
    zero_layer = jnp.zeros_like(minus_z[:1])
    above = jnp.concatenate([minus_z[1:], zero_layer], axis=0)
    jump_pz = bond_z * (plus_z - jnp.take_along_axis(above, index, axis=-1))
    pushed = jnp.take_along_axis(plus_z, reverse, axis=-1)
    below = jnp.concatenate([zero_layer, pushed[:-1]], axis=0)
    bond_under = jnp.concatenate([jnp.zeros_like(bond_z[:1]), bond_z[:-1]], axis=0)
    jump_mz = bond_under * (minus_z - below)
    stacked = jnp.stack([jump_mx, jump_px, jump_my, jump_py, jump_mz, jump_pz], axis=4)
    return stacked.reshape(field.shape)

def reference(trial, stiff_lam, stiff_mu, log_modes, nodes, quad_weights, chaos_index, bonds, face_map):
    moduli = jnp.exp(jnp.einsum('czyxk,qk->czyxq', log_modes, nodes, precision=lax.Precision.HIGHEST))
    first = schur(trial, moduli[0], moduli[1], stiff_lam, stiff_mu)
    jump_one = face_jumps(first, bonds, face_map).astype(jnp.bfloat16)
    second = schur(jump_one, moduli[0], moduli[1], stiff_lam, stiff_mu)
    jump_two = face_jumps(second, bonds, face_map).astype(jnp.bfloat16)
    basis = chaos_basis(nodes, chaos_index, quad_weights)

    def project(block):
        return jnp.einsum('yxqg,qp->yxgp', block.astype(jnp.float32), basis.astype(jnp.float32)).astype(jnp.bfloat16)
    return lax.map(project, jump_two)
```

```python
import functools

import jax
import jax.numpy as jnp
from jax import lax
from jax.experimental import pallas as pl
from jax.experimental.pallas import tpu as pltpu
from jax.sharding import PartitionSpec as P

F32 = jnp.float32
BF16 = jnp.bfloat16
VMEM = pl.BlockSpec(memory_space=pltpu.VMEM)
SMEM = pl.BlockSpec(memory_space=pltpu.SMEM)
ANY = pl.BlockSpec(memory_space=pl.ANY)


def shaped(shape, dtype=F32):
    return jax.ShapeDtypeStruct(shape, dtype)


def call(body, outs, specs, args, flops=0, scratch=(), out_specs=None):
    return pl.pallas_call(
        body,
        out_shape=outs,
        in_specs=specs,
        out_specs=[VMEM] * len(outs) if out_specs is None else out_specs,
        scratch_shapes=list(scratch),
        cost_estimate=pl.CostEstimate(flops=flops, bytes_accessed=0, transcendentals=0),
        compiler_params=pltpu.CompilerParams(vmem_limit_bytes=24 << 20),
    )(*args)


def dot(a, b):
    return jnp.dot(a, b, preferred_element_type=F32)


def wide(column, width):
    return jnp.concatenate([column] * (width // 128), axis=1)


def schur(rows, lam, mu, mod_lam, mod_mu):
    width = lam.shape[1]
    return wide(mod_lam, width) * dot(rows, lam) + wide(mod_mu, width) * dot(rows, mu)


class Sizes:
    def __init__(self, trial, basis_size, parts):
        _, self.height, self.breadth, self.here, self.width = trial.shape
        self.face = self.width // 6
        self.subs = self.height * self.breadth
        self.parts = parts
        self.samples = self.here * parts
        self.rows = self.subs * self.samples
        self.plane = 4 * self.face
        self.terms = basis_size
        self.share = self.width // parts

    def own(self, n, part):
        return pl.ds(pl.multiple_of(n * self.samples + part * self.here, 8), self.here)

    def block(self, n):
        return slice(n * self.samples, (n + 1) * self.samples)

    def group(self, n):
        return slice(n * self.here, (n + 1) * self.here)


def prepare(
    d, trial, lam, mu, modes, nodes, weights, chaos, faces, mod, maps, basis, plane, zed
):
    points = nodes[...]
    for c in range(2):
        for n in range(d.subs):
            row = modes[c, 0, n // d.breadth, pl.ds(n % d.breadth, 1), :]
            total = jnp.exp(jnp.sum(points * row, axis=1, keepdims=True))
            mod[c, d.block(n), :] = jnp.broadcast_to(total, (d.samples, 128))
    target = lax.broadcasted_iota(jnp.int32, (d.face, d.face), 0)
    source = lax.broadcasted_iota(jnp.int32, (8, d.face), 1).astype(F32).astype(BF16)
    for n in range(d.subs):
        row = faces[0, n // d.breadth, pl.ds(n % d.breadth, 1), :]
        hit = jnp.where(row == target, 1.0, 0.0).astype(BF16)
        back = lax.dot_general(
            source, hit, (((1,), (1,)), ((), ())), preferred_element_type=F32
        )
        maps[0, n] = jnp.broadcast_to(row, (8, d.face))
        maps[1, n] = back.astype(jnp.int32)
    count = points.shape[1]
    same = lax.broadcasted_iota(jnp.int32, (16, count), 0) == lax.broadcasted_iota(
        jnp.int32, (16, count), 1
    )
    degree = lax.dot_general(
        jnp.where(same, 1.0, 0.0).astype(BF16),
        chaos[...].astype(F32).astype(BF16),
        (((1,), (1,)), ((), ())),
        preferred_element_type=F32,
    )
    one = jnp.sqrt(3.0) * points
    two = jnp.sqrt(5.0) * (1.5 * points * points - 0.5)
    three = jnp.sqrt(7.0) * (2.5 * points * points * points - 1.5 * points)
    total = jnp.ones((d.samples, d.terms), F32)
    for k in range(count):
        c = degree[k : k + 1, :]
        high = jnp.where(c > 2.5, three[:, k : k + 1], two[:, k : k + 1])
        low = jnp.where(c > 0.5, one[:, k : k + 1], 1.0)
        total = total * jnp.where(c > 1.5, high, low)
    square = (d.samples, d.samples)
    diagonal = lax.broadcasted_iota(jnp.int32, square, 0) == lax.broadcasted_iota(
        jnp.int32, square, 1
    )
    column = jnp.sum(jnp.where(diagonal, weights[...], 0.0), axis=1, keepdims=True)
    table = (column * total).astype(BF16)
    for n in range(d.subs):
        basis[n] = jnp.zeros((d.rows, d.terms), BF16)
        basis[n, d.block(n), :] = table
    part = lax.axis_index("smp")
    field = trial[...]
    first = dot(field, lam[...])
    second = dot(field, mu[...])
    for n in range(d.subs):
        own = d.own(n, part)
        value = (
            wide(mod[0, own, :], d.width) * first[d.group(n)]
            + wide(mod[1, own, :], d.width) * second[d.group(n)]
        )
        plane[d.group(n), :] = value[:, : d.plane]
        zed[d.group(n), :] = value[:, d.plane :]


def payloads(d, low, high, maps, on_chip, off_chip):
    even = lax.rem(lax.axis_index("sub"), 2) == 0
    for n in range(d.subs):
        back = maps[1, n]
        for start in range(n * d.samples, (n + 1) * d.samples, 8):
            rows = slice(start, start + 8)
            minus = low[rows]
            pushed = jnp.take_along_axis(high[rows], back, axis=1, mode="promise_in_bounds")
            on_chip[rows, :] = jnp.where(even, pushed, minus)
            off_chip[rows, :] = jnp.where(even, minus, pushed)


def part_of(d, shift):
    here = lax.axis_index("smp")
    return lax.rem(here - shift + d.parts, d.parts)


def first_z(d, *refs):
    others = refs[: d.parts - 1]
    lam, mu, mod, maps, zed, field, on_chip, off_chip = refs[d.parts - 1 :]
    part = lax.axis_index("smp")
    for n in range(d.subs):
        field[d.own(n, part), :] = zed[d.group(n), :]
    for shift, other in enumerate(others, 1):
        part = part_of(d, shift)
        rows = other[...]
        first = dot(rows, lam[:, d.plane :])
        second = dot(rows, mu[:, d.plane :])
        for n in range(d.subs):
            own = d.own(n, part)
            field[own, :] = (
                wide(mod[0, own, :], 2 * d.face) * first[d.group(n)]
                + wide(mod[1, own, :], 2 * d.face) * second[d.group(n)]
            )
    payloads(d, field[:, : d.face], field[:, d.face :], maps, on_chip, off_chip)


def plane_jumps(d, field, bonds, out):
    layer = lax.axis_index("sub")

    def bond(axis, n):
        return bonds[axis, layer, n // d.breadth, n % d.breadth].astype(F32)

    for n in range(d.subs):
        y, x = divmod(n, d.breadth)
        left = y * d.breadth + (x - 1) % d.breadth
        right = y * d.breadth + (x + 1) % d.breadth
        front = (y - 1) % d.height * d.breadth + x
        behind = (y + 1) % d.height * d.breadth + x

        def face(which, m):
            return field[d.block(m), which * d.face : (which + 1) * d.face]

        out(0, n, bond(0, left) * (face(0, n) - face(1, left)))
        out(1, n, bond(0, n) * (face(1, n) - face(0, right)))
        out(2, n, bond(1, front) * (face(2, n) - face(3, front)))
        out(3, n, bond(1, n) * (face(3, n) - face(2, behind)))


def z_jumps(d, field, from_chip, from_off, maps, bonds, out):
    layer = lax.axis_index("sub")
    even = lax.rem(layer, 2) == 0
    under = jnp.maximum(layer - 1, 0)
    for n in range(d.subs):
        y, x = divmod(n, d.breadth)
        bond_up = bonds[2, layer, y, x].astype(F32)
        bond_down = jnp.where(layer > 0, bonds[2, under, y, x].astype(F32), 0.0)
        for start in range(n * d.samples, (n + 1) * d.samples, 8):
            rows = slice(start, start + 8)
            near, far = from_chip[rows, :], from_off[rows, :]
            above = jnp.where(even, near, far)
            below = jnp.where(even, far, near)
            matched = jnp.take_along_axis(above, maps[0, n], axis=1, mode="promise_in_bounds")
            out(0, rows, bond_down * (field[rows, : d.face] - below))
            out(1, rows, bond_up * (field[rows, d.face :] - matched))


def first_plane(d, *refs):
    others = refs[: d.parts - 1]
    lam, mu, mod, plane, bonds, jumps, part_lam, part_mu, field = refs[d.parts - 1 :]
    part = lax.axis_index("smp")
    for n in range(d.subs):
        field[d.own(n, part), :] = plane[d.group(n), :]
    for shift, other in enumerate(others, 1):
        part = part_of(d, shift)
        rows = other[...]
        first = dot(rows, lam[:, : d.plane])
        second = dot(rows, mu[:, : d.plane])
        for n in range(d.subs):
            own = d.own(n, part)
            field[own, :] = (
                wide(mod[0, own, :], d.plane) * first[d.group(n)]
                + wide(mod[1, own, :], d.plane) * second[d.group(n)]
            )

    def put(which, n, value):
        jumps[d.block(n), which * d.face : (which + 1) * d.face] = value.astype(BF16)

    plane_jumps(d, field, bonds, put)
    part_lam[...] = dot(jumps[...], lam[: d.plane, d.plane :])
    part_mu[...] = dot(jumps[...], mu[: d.plane, d.plane :])


def second_z(
    d, field, from_chip, from_off, maps, bonds, mod, lam, mu, part_lam, part_mu,
    jumps, result, on_chip, off_chip, held,
):
    def put(which, rows, value):
        held[rows, which * d.face : (which + 1) * d.face] = value

    z_jumps(d, field, from_chip, from_off, maps, bonds, put)
    rounded = held[...].astype(BF16)
    jumps[...] = rounded
    one = part_lam[...] + dot(rounded, lam[d.plane :, d.plane :])
    two = part_mu[...] + dot(rounded, mu[d.plane :, d.plane :])
    result[...] = wide(mod[0], 2 * d.face) * one + wide(mod[1], 2 * d.face) * two
    payloads(d, result[:, : d.face], result[:, d.face :], maps, on_chip, off_chip)


def second_plane(d, plane, zed, lam, mu, mod, bonds, turned, held):
    one = dot(plane[...], lam[: d.plane, : d.plane]) + dot(zed[...], lam[d.plane :, : d.plane])
    two = dot(plane[...], mu[: d.plane, : d.plane]) + dot(zed[...], mu[d.plane :, : d.plane])
    field = wide(mod[0], d.plane) * one + wide(mod[1], d.plane) * two

    def put(which, n, value):
        held[which, d.block(n), :] = value

    plane_jumps(d, field, bonds, put)
    for which in range(4):
        turned[which * d.face : (which + 1) * d.face, :] = held[which].T.astype(BF16)


def project(d, field, from_chip, from_off, maps, bonds, plane, basis, out, held, turned, rows_out, sems):
    def put(which, rows, value):
        held[which, rows, :] = value

    z_jumps(d, field, from_chip, from_off, maps, bonds, put)
    turned[: d.plane, :] = plane[...]
    for which in range(2):
        start = d.plane + which * d.face
        turned[start : start + d.face, :] = held[which].T.astype(BF16)
    start = pl.multiple_of(lax.axis_index("smp") * d.share, 16)
    left = turned[pl.ds(start, d.share), :]
    copies = []
    for n in range(d.subs):
        rows_out[n] = dot(left, basis[n]).astype(BF16)
        copy = pltpu.make_async_copy(
            rows_out.at[n], out.at[0, n // d.breadth, n % d.breadth], sems.at[n]
        )
        copy.start()
        copies.append(copy)
    for copy in copies:
        copy.wait()


def per_device(
    trial, stiff_lam, stiff_mu, log_modes, nodes, quad_weights, chaos_index, bonds, face_map
):
    parts = lax.axis_size("smp")
    layers = lax.axis_size("sub")
    d = Sizes(trial, chaos_index.shape[0], parts)
    rows, face = d.rows, d.face
    own = trial.reshape(d.subs * d.here, d.width)
    others = [
        lax.ppermute(own, "smp", [(i, (i + shift) % parts) for i in range(parts)])
        for shift in range(1, parts)
    ]
    pairs = [(i, i ^ 1) for i in range(layers)]
    ends = [(i, i + 1) for i in range(1, layers - 1, 2)]
    ends = ends + [(j, i) for i, j in ends]

    def exchange(on_chip, off_chip):
        return lax.ppermute(on_chip, "sub", pairs), lax.ppermute(off_chip, "sub", ends)

    def run(body, *args, **options):
        return call(functools.partial(body, d), *args, **options)

    mod, maps, basis, plane, zed = run(
        prepare,
        [
            shaped((2, rows, 128)),
            shaped((2, d.subs, 8, face), jnp.int32),
            shaped((d.subs, rows, d.terms), BF16),
            shaped((d.subs * d.here, d.plane)),
            shaped((d.subs * d.here, 2 * face)),
        ],
        [VMEM] * 8,
        [
            own, stiff_lam, stiff_mu, log_modes, nodes,
            quad_weights.reshape(1, -1), chaos_index, face_map,
        ],
    )
    field, on_chip, off_chip = run(
        first_z,
        [shaped((rows, 2 * face)), shaped((rows, face)), shaped((rows, face))],
        [VMEM] * (parts + 4),
        [*others, stiff_lam, stiff_mu, mod, maps, zed],
    )
    near, far = exchange(on_chip, off_chip)
    jumps_plane, part_lam, part_mu = run(
        first_plane,
        [shaped((rows, d.plane), BF16), shaped((rows, 2 * face)), shaped((rows, 2 * face))],
        [VMEM] * (parts + 3) + [SMEM],
        [*others, stiff_lam, stiff_mu, mod, plane, bonds],
        scratch=[pltpu.VMEM((rows, d.plane), F32)],
    )
    jumps_z, field, on_chip, off_chip = run(
        second_z,
        [
            shaped((rows, 2 * face), BF16),
            shaped((rows, 2 * face)),
            shaped((rows, face)),
            shaped((rows, face)),
        ],
        [VMEM] * 4 + [SMEM] + [VMEM] * 5,
        [field, near, far, maps, bonds, mod, stiff_lam, stiff_mu, part_lam, part_mu],
        scratch=[pltpu.VMEM((rows, 2 * face), F32)],
    )
    near, far = exchange(on_chip, off_chip)
    (turned,) = run(
        second_plane,
        [shaped((d.plane, rows), BF16)],
        [VMEM] * 5 + [SMEM],
        [jumps_plane, jumps_z, stiff_lam, stiff_mu, mod, bonds],
        scratch=[pltpu.VMEM((4, rows, face), F32)],
    )
    (out,) = run(
        project,
        [shaped((1, d.height, d.breadth, d.share, d.terms), BF16)],
        [VMEM] * 4 + [SMEM] + [VMEM] * 2,
        [field, near, far, maps, bonds, turned, basis],
        out_specs=[ANY],
        scratch=[
            pltpu.VMEM((2, rows, face), F32),
            pltpu.VMEM((d.width, rows), BF16),
            pltpu.VMEM((d.subs, d.share, d.terms), BF16),
            pltpu.SemaphoreType.DMA((d.subs,)),
        ],
    )
    return out


def solution(mesh):
    return jax.shard_map(
        per_device,
        mesh=mesh,
        in_specs=(
            P("sub", None, None, "smp", None),
            P(),
            P(),
            P(None, "sub", None, None, None),
            P(),
            P(),
            P(),
            P(),
            P("sub", None, None, None),
        ),
        out_specs=P("sub", None, None, "smp", None),
        check_vma=False,
    )
```

```python
import functools

import jax
import jax.numpy as jnp
from jax import lax
from jax.experimental import pallas as pl
from jax.experimental.pallas import tpu as pltpu
from jax.sharding import PartitionSpec as P

F32 = jnp.float32
BF16 = jnp.bfloat16
VMEM = pl.BlockSpec(memory_space=pltpu.VMEM)
CHUNKS = 3
HBM = pl.BlockSpec(memory_space=pltpu.HBM)


def shaped(shape, dtype=F32):
    return jax.ShapeDtypeStruct(shape, dtype)


def call(body, outs, specs, args, flops=0, scratch=(), out_specs=None, grant=24 << 20, aliases=None):
    return pl.pallas_call(
        body,
        out_shape=outs,
        in_specs=specs,
        out_specs=[VMEM] * len(outs) if out_specs is None else out_specs,
        scratch_shapes=list(scratch),
        input_output_aliases=aliases or {},
        cost_estimate=pl.CostEstimate(flops=flops, bytes_accessed=0, transcendentals=0),
        compiler_params=pltpu.CompilerParams(vmem_limit_bytes=grant),
    )(*args)


def dot(a, b):
    return jnp.dot(a, b, preferred_element_type=F32)


def wide(column, width):
    return jnp.concatenate([column] * (width // 128), axis=1)


class Sizes:
    def __init__(self, trial, basis_size, parts):
        _, self.height, self.breadth, self.here, self.width = trial.shape
        self.face = self.width // 6
        self.subs = self.height * self.breadth
        self.parts = parts
        self.samples = self.here * parts
        self.rows = self.subs * self.samples
        self.plane = 4 * self.face
        self.terms = basis_size
        self.share = self.width // parts

    def own(self, n, part):
        return pl.ds(pl.multiple_of(n * self.samples + part * self.here, 8), self.here)

    def block(self, n):
        return slice(n * self.samples, (n + 1) * self.samples)

    def group(self, n):
        return slice(n * self.here, (n + 1) * self.here)


def load(d, lam, mu, lam_here, mu_here, sems):
    copies = [
        pltpu.make_async_copy(lam, lam_here, sems.at[0]),
        pltpu.make_async_copy(mu, mu_here, sems.at[1]),
    ]
    for copy in copies:
        copy.start()
    for copy in copies:
        copy.wait()


def prepare(d, trial, lam, mu, modes, nodes, faces, mod, maps, first, second):
    first[...] = dot(trial[...], lam[...])
    second[...] = dot(trial[...], mu[...])
    points = nodes[...]
    for c in range(2):
        for n in range(d.subs):
            row = modes[c, 0, n % d.breadth, pl.ds(n // d.breadth, 1), :]
            total = jnp.exp(jnp.sum(points * row, axis=1, keepdims=True))
            mod[c, d.block(n), :] = jnp.broadcast_to(total, (d.samples, 128))
    target = lax.broadcasted_iota(jnp.int32, (d.face, d.face), 0)
    source = lax.broadcasted_iota(jnp.int32, (8, d.face), 1).astype(F32).astype(BF16)
    for n in range(d.subs):
        row = faces[0, n % d.breadth, pl.ds(n // d.breadth, 1), :]
        hit = jnp.where(row == target, 1.0, 0.0).astype(BF16)
        back = lax.dot_general(
            source, hit, (((1,), (1,)), ((), ())), preferred_element_type=F32
        )
        maps[0, n] = jnp.broadcast_to(row, (8, d.face))
        maps[1, n] = back.astype(jnp.int32)


def tables(d, nodes, weights, chaos, bonds, basis, masks):
    points = nodes[...]
    layer = lax.axis_index("sub")
    lane = lax.broadcasted_iota(jnp.int32, (d.height, bonds.shape[-1]), 1)

    def at(axis, x, z):
        picked = jnp.where(lane == z, bonds[axis, x].astype(F32), 0.0)
        return jnp.sum(picked, axis=1, keepdims=True)

    along = [[at(axis, x, layer) for x in range(d.breadth)] for axis in range(3)]
    under = [at(2, x, layer - 1) for x in range(d.breadth)]
    for n in range(d.subs):
        y, x = divmod(n, d.breadth)
        columns = [
            (along[0][(x - 1) % d.breadth], y),
            (along[0][x], y),
            (along[1][x], (y - 1) % d.height),
            (along[1][x], y),
            (under[x], y),
            (along[2][x], y),
        ]
        for which, (column, at_y) in enumerate(columns):
            masks[which, n] = jnp.broadcast_to(column[at_y : at_y + 1], (8, 128))
    one = jnp.sqrt(3.0) * points
    two = jnp.sqrt(5.0) * (1.5 * points * points - 0.5)
    three = jnp.sqrt(7.0) * (2.5 * points * points * points - 1.5 * points)
    total = jnp.ones((d.samples, d.terms), F32)
    for k in range(points.shape[1]):
        c = chaos[k : k + 1, :]
        high = jnp.where(c == 3, three[:, k : k + 1], two[:, k : k + 1])
        low = jnp.where(c == 1, one[:, k : k + 1], 1.0)
        total = total * jnp.where(c >= 2, high, low)
    square = (d.samples, d.samples)
    diagonal = lax.broadcasted_iota(jnp.int32, square, 0) == lax.broadcasted_iota(
        jnp.int32, square, 1
    )
    column = jnp.sum(jnp.where(diagonal, weights[...], 0.0), axis=1, keepdims=True)
    basis[...] = (column * total).T.astype(BF16)


def payloads(d, low, high, maps, on_chip, off_chip):
    even = lax.rem(lax.axis_index("sub"), 2) == 0
    for n in range(d.subs):
        back = maps[1, n]
        for start in range(n * d.samples, (n + 1) * d.samples, 8):
            rows = slice(start, start + 8)
            minus = low[rows]
            pushed = jnp.take_along_axis(high[rows], back, axis=1, mode="promise_in_bounds")
            on_chip[rows, :] = jnp.where(even, pushed, minus)
            off_chip[rows, :] = jnp.where(even, minus, pushed)


def part_of(d, shift):
    here = lax.axis_index("smp")
    return lax.rem(here - shift + d.parts, d.parts)


def combine(d, mod, part, first, second, field):
    width = field.shape[1]
    for n in range(d.subs):
        own = d.own(n, part)
        field[own, :] = (
            wide(mod[0, own, :], width) * first[d.group(n), :]
            + wide(mod[1, own, :], width) * second[d.group(n), :]
        )


def first_z(d, *refs):
    others = refs[: d.parts - 1]
    lam, mu, mod, maps, own_lam, own_mu, field, on_chip, off_chip = refs[d.parts - 1 :]
    at = slice(d.plane, d.width)
    combine(d, mod, lax.axis_index("smp"), own_lam.at[:, at], own_mu.at[:, at], field)
    for shift, other in enumerate(others, 1):
        rows = other[...]
        combine(d, mod, part_of(d, shift), dot(rows, lam[:, at]), dot(rows, mu[:, at]), field)
    payloads(d, field[:, : d.face], field[:, d.face :], maps, on_chip, off_chip)


def plane_jumps(d, field, masks, out):
    def mask(which, n):
        return jnp.concatenate([masks[which, n]] * (d.samples // 8), axis=0)

    for n in range(d.subs):
        y, x = divmod(n, d.breadth)
        left = y * d.breadth + (x - 1) % d.breadth
        right = y * d.breadth + (x + 1) % d.breadth
        front = (y - 1) % d.height * d.breadth + x
        behind = (y + 1) % d.height * d.breadth + x

        def face(which, m):
            return field[d.block(m), which * d.face : (which + 1) * d.face]

        out(0, n, mask(0, n) * (face(0, n) - face(1, left)))
        out(1, n, mask(1, n) * (face(1, n) - face(0, right)))
        out(2, n, mask(2, n) * (face(2, n) - face(3, front)))
        out(3, n, mask(3, n) * (face(3, n) - face(2, behind)))


def z_jumps(d, field, from_chip, from_off, maps, masks, out):
    even = lax.rem(lax.axis_index("sub"), 2) == 0
    for n in range(d.subs):
        for start in range(n * d.samples, (n + 1) * d.samples, 8):
            rows = slice(start, start + 8)
            near, far = from_chip[rows, :], from_off[rows, :]
            above = jnp.where(even, near, far)
            below = jnp.where(even, far, near)
            matched = jnp.take_along_axis(above, maps[0, n], axis=1, mode="promise_in_bounds")
            out(0, rows, masks[4, n] * (field[rows, : d.face] - below))
            out(1, rows, masks[5, n] * (field[rows, d.face :] - matched))


def first_plane(d, *refs):
    others = refs[: d.parts - 1]
    lam, mu, mod, own_lam, own_mu, masks, jumps, part_lam, part_mu, field = refs[d.parts - 1 :]
    at = slice(0, d.plane)
    combine(d, mod, lax.axis_index("smp"), own_lam.at[:, at], own_mu.at[:, at], field)
    for shift, other in enumerate(others, 1):
        rows = other[...]
        combine(d, mod, part_of(d, shift), dot(rows, lam[:, at]), dot(rows, mu[:, at]), field)

    def put(which, n, value):
        jumps[d.block(n), which * d.face : (which + 1) * d.face] = value.astype(BF16)

    plane_jumps(d, field, masks, put)
    part_lam[...] = dot(jumps[...], lam[: d.plane, d.plane :])
    part_mu[...] = dot(jumps[...], mu[: d.plane, d.plane :])


def second_z(
    d, field, from_chip, from_off, maps, masks, mod, lam, mu, part_lam, part_mu,
    jumps, result, on_chip, off_chip, held,
):
    def put(which, rows, value):
        held[rows, which * d.face : (which + 1) * d.face] = value

    z_jumps(d, field, from_chip, from_off, maps, masks, put)
    rounded = held[...].astype(BF16)
    jumps[...] = rounded
    one = part_lam[...] + dot(rounded, lam[d.plane :, d.plane :])
    two = part_mu[...] + dot(rounded, mu[d.plane :, d.plane :])
    result[...] = wide(mod[0], 2 * d.face) * one + wide(mod[1], 2 * d.face) * two
    payloads(d, result[:, : d.face], result[:, d.face :], maps, on_chip, off_chip)


def second_plane(d, plane, zed, lam, mu, mod, masks, jumps):
    one = dot(plane[...], lam[: d.plane, : d.plane]) + dot(zed[...], lam[d.plane :, : d.plane])
    two = dot(plane[...], mu[: d.plane, : d.plane]) + dot(zed[...], mu[d.plane :, : d.plane])
    field = wide(mod[0], d.plane) * one + wide(mod[1], d.plane) * two

    def put(which, n, value):
        jumps[d.block(n), which * d.face : (which + 1) * d.face] = value.astype(BF16)

    plane_jumps(d, field, masks, put)


def last_z(d, field, from_chip, from_off, maps, masks, plane, jumps, held):
    def put(which, rows, value):
        held[rows, which * d.face : (which + 1) * d.face] = value

    z_jumps(d, field, from_chip, from_off, maps, masks, put)
    jumps[:, : d.plane] = plane[...]
    jumps[:, d.plane :] = held[...].astype(BF16)


def project_rows(d, picks, lanes, basis, out, rows_out, sems):
    width = lanes.stop - lanes.start
    group = max(g for g in (1, 2, 3, 6) if d.subs % g == 0 and g * width <= 768)
    chunk = d.terms // CHUNKS
    copies = []
    for n in range(0, d.subs, group):
        right = picks[n : n + group]
        right = right[0] if group == 1 else jnp.concatenate(right, axis=1)
        for c in range(CHUNKS):
            rows = slice(c * chunk, (c + 1) * chunk)
            value = dot(basis[rows, :], right)
            for m in range(group):
                rows_out[n + m, rows, :] = value[:, m * width : (m + 1) * width].astype(BF16)
                y, x = divmod(n + m, d.breadth)
                copy = pltpu.make_async_copy(
                    rows_out.at[n + m, rows, :],
                    out.at[0, y, x, rows, lanes],
                    sems.at[n + m, c],
                )
                copy.start()
                copies.append(copy)
    for copy in copies:
        copy.wait()


def project_early(d, plane, basis, out, rows_out, sems):
    start = pl.multiple_of(lax.axis_index("smp") * d.share, 128)
    picks = [plane[d.block(n), pl.ds(start, d.face)] for n in range(d.subs)]
    project_rows(d, picks, slice(0, d.face), basis, out, rows_out, sems)


def project_late(
    d, field, from_chip, from_off, maps, masks, plane, basis, early, out, held, jumps, rows_out, sems
):
    last_z(d, field, from_chip, from_off, maps, masks, plane, jumps, held)
    width = d.share - d.face
    start = pl.multiple_of(lax.axis_index("smp") * d.share + d.face, 128)
    picks = [jumps[d.block(n), pl.ds(start, width)] for n in range(d.subs)]
    project_rows(d, picks, slice(d.face, d.share), basis, out, rows_out, sems)


def project_share(d, jumps, basis, out, rows_out, sems):
    picks = [jumps[d.block(n), :] for n in range(d.subs)]
    project_rows(d, picks, slice(0, d.share), basis, out, rows_out, sems)


def per_device(
    trial, stiff_lam, stiff_mu, log_modes, nodes, quad_weights, chaos_index, bonds, face_map
):
    parts = lax.axis_size("smp")
    layers = lax.axis_size("sub")
    d = Sizes(trial, chaos_index.shape[0], parts)
    rows, face = d.rows, d.face
    own = trial.reshape(d.subs * d.here, d.width)
    others = [
        lax.ppermute(own, "smp", [(i, (i + shift) % parts) for i in range(parts)])
        for shift in range(1, parts)
    ]
    pairs = [(i, i ^ 1) for i in range(layers)]
    ends = [(i, i + 1) for i in range(1, layers - 1, 2)]
    ends = ends + [(j, i) for i, j in ends]

    def exchange(on_chip, off_chip):
        far = lax.ppermute(off_chip, "sub", ends)
        return lax.ppermute(on_chip, "sub", pairs), far

    def run(body, *args, **options):
        return call(functools.partial(body, d), *args, **options)

    product = shaped((d.subs * d.here, d.width))
    lam, mu = run(
        load,
        [shaped(stiff_lam.shape, BF16), shaped(stiff_mu.shape, BF16)],
        [HBM] * 2,
        [stiff_lam, stiff_mu],
        scratch=[pltpu.SemaphoreType.DMA((2,))],
        grant=51 << 20,
    )
    mod, maps, own_lam, own_mu = run(
        prepare,
        [shaped((2, rows, 128)), shaped((2, d.subs, 8, face), jnp.int32), product, product],
        [VMEM] * 6,
        [
            own, lam, mu,
            log_modes.transpose(0, 1, 3, 2, 4), nodes, face_map.transpose(0, 2, 1, 3),
        ],
    )
    field, on_chip, off_chip = run(
        first_z,
        [shaped((rows, 2 * face)), shaped((rows, face)), shaped((rows, face))],
        [VMEM] * (parts + 5),
        [*others, lam, mu, mod, maps, own_lam, own_mu],
    )
    near, far = exchange(on_chip, off_chip)
    basis, masks = run(
        tables,
        [shaped((d.terms, d.samples), BF16), shaped((6, d.subs, 8, 128))],
        [VMEM] * 4,
        [nodes, quad_weights.reshape(1, -1), chaos_index.T, bonds.transpose(0, 3, 2, 1)],
    )
    jumps_plane, part_lam, part_mu = run(
        first_plane,
        [shaped((rows, d.plane), BF16), shaped((rows, 2 * face)), shaped((rows, 2 * face))],
        [VMEM] * (parts + 5),
        [*others, lam, mu, mod, own_lam, own_mu, masks],
        scratch=[pltpu.VMEM((rows, d.plane), F32)],
    )
    jumps_z, field, on_chip, off_chip = run(
        second_z,
        [
            shaped((rows, 2 * face), BF16),
            shaped((rows, 2 * face)),
            shaped((rows, face)),
            shaped((rows, face)),
        ],
        [VMEM] * 10,
        [field, near, far, maps, masks, mod, lam, mu, part_lam, part_mu],
        scratch=[pltpu.VMEM((rows, 2 * face), F32)],
    )
    near, far = exchange(on_chip, off_chip)
    (plane,) = run(
        second_plane,
        [shaped((rows, d.plane), BF16)],
        [VMEM] * 6,
        [jumps_plane, jumps_z, lam, mu, mod, masks],
    )
    last = [field, near, far, maps, masks, plane]
    held = pltpu.VMEM((rows, 2 * face), F32)
    result = [shaped((1, d.height, d.breadth, d.terms, d.share), BF16)]

    def buffers(width):
        return [
            pltpu.VMEM((d.subs, d.terms, width), BF16),
            pltpu.SemaphoreType.DMA((d.subs, CHUNKS)),
        ]

    if d.share == 3 * face:
        (early,) = run(
            project_early,
            result,
            [VMEM] * 2,
            [plane, basis],
            out_specs=[HBM],
            scratch=buffers(face),
        )
        (out,) = run(
            project_late,
            result,
            [VMEM] * 7 + [HBM],
            [*last, basis, early],
            out_specs=[HBM],
            scratch=[held, pltpu.VMEM((rows, d.width), BF16)] + buffers(2 * face),
            aliases={7: 0},
        )
    else:
        (jumps,) = run(last_z, [shaped((rows, d.width), BF16)], [VMEM] * 6, last, scratch=[held])
        start = lax.axis_index("smp") * d.share
        jumps = lax.dynamic_slice_in_dim(jumps, start, d.share, 1)
        (out,) = run(
            project_share, result, [VMEM] * 2, [jumps, basis], out_specs=[HBM], scratch=buffers(d.share)
        )
    return jnp.swapaxes(out, -1, -2)


def solution(mesh):
    return jax.shard_map(
        per_device,
        mesh=mesh,
        in_specs=(
            P("sub", None, None, "smp", None),
            P(),
            P(),
            P(None, "sub", None, None, None),
            P(),
            P(),
            P(),
            P(),
            P("sub", None, None, None),
        ),
        out_specs=P("sub", None, None, "smp", None),
        check_vma=False,
    )
```

```python
import functools

import jax
import jax.numpy as jnp
from jax import lax
from jax.experimental import pallas as pl
from jax.experimental.pallas import tpu as pltpu
from jax.sharding import PartitionSpec as P

F32 = jnp.float32
BF16 = jnp.bfloat16
VMEM = pl.BlockSpec(memory_space=pltpu.VMEM)
CHUNKS = 3
HBM = pl.BlockSpec(memory_space=pltpu.HBM)


def shaped(shape, dtype=F32):
    return jax.ShapeDtypeStruct(shape, dtype)


def call(body, outs, specs, args, flops=0, scratch=(), out_specs=None, grant=24 << 20, aliases=None):
    return pl.pallas_call(
        body,
        out_shape=outs,
        in_specs=specs,
        out_specs=[VMEM] * len(outs) if out_specs is None else out_specs,
        scratch_shapes=list(scratch),
        input_output_aliases=aliases or {},
        cost_estimate=pl.CostEstimate(flops=flops, bytes_accessed=0, transcendentals=0),
        compiler_params=pltpu.CompilerParams(vmem_limit_bytes=grant),
    )(*args)


def dot(a, b):
    return jnp.dot(a, b, preferred_element_type=F32)


def wide(column, width):
    return jnp.concatenate([column] * (width // 128), axis=1)


class Sizes:
    def __init__(self, trial, basis_size, parts):
        _, self.height, self.breadth, self.here, self.width = trial.shape
        self.face = self.width // 6
        self.subs = self.height * self.breadth
        self.parts = parts
        self.samples = self.here * parts
        self.rows = self.subs * self.samples
        self.plane = 4 * self.face
        self.terms = basis_size
        self.share = self.width // parts

    def own(self, n, part):
        return pl.ds(pl.multiple_of(n * self.samples + part * self.here, 8), self.here)

    def block(self, n):
        return slice(n * self.samples, (n + 1) * self.samples)

    def group(self, n):
        return slice(n * self.here, (n + 1) * self.here)


def load(d, lam, mu, lam_here, mu_here, sems):
    copies = [
        pltpu.make_async_copy(lam, lam_here, sems.at[0]),
        pltpu.make_async_copy(mu, mu_here, sems.at[1]),
    ]
    for copy in copies:
        copy.start()
    for copy in copies:
        copy.wait()


def prepare(d, trial, lam, mu, modes, nodes, faces, mod, maps, first, second):
    first[...] = dot(trial[...], lam[...])
    second[...] = dot(trial[...], mu[...])
    points = nodes[...]
    for c in range(2):
        for n in range(d.subs):
            row = modes[c, 0, n % d.breadth, pl.ds(n // d.breadth, 1), :]
            total = jnp.exp(jnp.sum(points * row, axis=1, keepdims=True))
            mod[c, d.block(n), :] = jnp.broadcast_to(total, (d.samples, 128))
    target = lax.broadcasted_iota(jnp.int32, (d.face, d.face), 0)
    source = lax.broadcasted_iota(jnp.int32, (8, d.face), 1).astype(F32).astype(BF16)
    for n in range(d.subs):
        row = faces[0, n % d.breadth, pl.ds(n // d.breadth, 1), :]
        hit = jnp.where(row == target, 1.0, 0.0).astype(BF16)
        back = lax.dot_general(
            source, hit, (((1,), (1,)), ((), ())), preferred_element_type=F32
        )
        maps[0, n] = jnp.broadcast_to(row, (8, d.face))
        maps[1, n] = back.astype(jnp.int32)


def tables(d, nodes, weights, chaos, bonds, basis, masks):
    points = nodes[...]
    layer = lax.axis_index("sub")
    lane = lax.broadcasted_iota(jnp.int32, (d.height, bonds.shape[-1]), 1)

    def at(axis, x, z):
        picked = jnp.where(lane == z, bonds[axis, x].astype(F32), 0.0)
        return jnp.sum(picked, axis=1, keepdims=True)

    along = [[at(axis, x, layer) for x in range(d.breadth)] for axis in range(3)]
    under = [at(2, x, layer - 1) for x in range(d.breadth)]
    for n in range(d.subs):
        y, x = divmod(n, d.breadth)
        columns = [
            (along[0][(x - 1) % d.breadth], y),
            (along[0][x], y),
            (along[1][x], (y - 1) % d.height),
            (along[1][x], y),
            (under[x], y),
            (along[2][x], y),
        ]
        for which, (column, at_y) in enumerate(columns):
            masks[which, n] = jnp.broadcast_to(column[at_y : at_y + 1], (8, 128))
    one = jnp.sqrt(3.0) * points
    two = jnp.sqrt(5.0) * (1.5 * points * points - 0.5)
    three = jnp.sqrt(7.0) * (2.5 * points * points * points - 1.5 * points)
    total = jnp.ones((d.samples, d.terms), F32)
    for k in range(points.shape[1]):
        c = chaos[k : k + 1, :]
        high = jnp.where(c == 3, three[:, k : k + 1], two[:, k : k + 1])
        low = jnp.where(c == 1, one[:, k : k + 1], 1.0)
        total = total * jnp.where(c >= 2, high, low)
    square = (d.samples, d.samples)
    diagonal = lax.broadcasted_iota(jnp.int32, square, 0) == lax.broadcasted_iota(
        jnp.int32, square, 1
    )
    column = jnp.sum(jnp.where(diagonal, weights[...], 0.0), axis=1, keepdims=True)
    basis[...] = (column * total).T.astype(BF16)


def payloads(d, low, high, maps, on_chip, off_chip):
    even = lax.rem(lax.axis_index("sub"), 2) == 0
    for n in range(d.subs):
        back = maps[1, n]
        for start in range(n * d.samples, (n + 1) * d.samples, 8):
            rows = slice(start, start + 8)
            minus = low[rows]
            pushed = jnp.take_along_axis(high[rows], back, axis=1, mode="promise_in_bounds")
            on_chip[rows, :] = jnp.where(even, pushed, minus)
            off_chip[rows, :] = jnp.where(even, minus, pushed)


def part_of(d, shift):
    here = lax.axis_index("smp")
    return lax.rem(here - shift + d.parts, d.parts)


def combine(d, mod, part, first, second, field):
    width = field.shape[1]
    for n in range(d.subs):
        own = d.own(n, part)
        field[own, :] = (
            wide(mod[0, own, :], width) * first[d.group(n), :]
            + wide(mod[1, own, :], width) * second[d.group(n), :]
        )


def first_z(d, *refs):
    others = refs[: d.parts - 1]
    lam, mu, mod, maps, own_lam, own_mu, field, on_chip, off_chip = refs[d.parts - 1 :]
    at = slice(d.plane, d.width)
    combine(d, mod, lax.axis_index("smp"), own_lam.at[:, at], own_mu.at[:, at], field)
    for shift, other in enumerate(others, 1):
        rows = other[...]
        combine(d, mod, part_of(d, shift), dot(rows, lam[:, at]), dot(rows, mu[:, at]), field)
    payloads(d, field[:, : d.face], field[:, d.face :], maps, on_chip, off_chip)


def plane_jumps(d, field, masks, out):
    def mask(which, n):
        return jnp.concatenate([masks[which, n]] * (d.samples // 8), axis=0)

    for n in range(d.subs):
        y, x = divmod(n, d.breadth)
        left = y * d.breadth + (x - 1) % d.breadth
        right = y * d.breadth + (x + 1) % d.breadth
        front = (y - 1) % d.height * d.breadth + x
        behind = (y + 1) % d.height * d.breadth + x

        def face(which, m):
            return field[d.block(m), which * d.face : (which + 1) * d.face]

        out(0, n, mask(0, n) * (face(0, n) - face(1, left)))
        out(1, n, mask(1, n) * (face(1, n) - face(0, right)))
        out(2, n, mask(2, n) * (face(2, n) - face(3, front)))
        out(3, n, mask(3, n) * (face(3, n) - face(2, behind)))


def z_jumps(d, field, from_off, from_chip, maps, masks, out):
    even = lax.rem(lax.axis_index("sub"), 2) == 0
    for n in range(d.subs):
        for start in range(n * d.samples, (n + 1) * d.samples, 8):
            rows = slice(start, start + 8)
            near, far = from_chip[rows, :], from_off[rows, :]
            above = jnp.where(even, near, far)
            below = jnp.where(even, far, near)
            matched = jnp.take_along_axis(above, maps[0, n], axis=1, mode="promise_in_bounds")
            out(0, rows, masks[4, n] * (field[rows, : d.face] - below))
            out(1, rows, masks[5, n] * (field[rows, d.face :] - matched))


def first_plane(d, *refs):
    others = refs[: d.parts - 1]
    lam, mu, mod, own_lam, own_mu, masks, jumps, part_lam, part_mu, field = refs[d.parts - 1 :]
    at = slice(0, d.plane)
    combine(d, mod, lax.axis_index("smp"), own_lam.at[:, at], own_mu.at[:, at], field)
    for shift, other in enumerate(others, 1):
        rows = other[...]
        combine(d, mod, part_of(d, shift), dot(rows, lam[:, at]), dot(rows, mu[:, at]), field)

    def put(which, n, value):
        jumps[d.block(n), which * d.face : (which + 1) * d.face] = value.astype(BF16)

    plane_jumps(d, field, masks, put)
    part_lam[...] = dot(jumps[...], lam[: d.plane, d.plane :])
    part_mu[...] = dot(jumps[...], mu[: d.plane, d.plane :])


def second_z(
    d, field, from_off, from_chip, maps, masks, mod, lam, mu, part_lam, part_mu,
    jumps, result, on_chip, off_chip, held,
):
    def put(which, rows, value):
        held[rows, which * d.face : (which + 1) * d.face] = value

    z_jumps(d, field, from_off, from_chip, maps, masks, put)
    rounded = held[...].astype(BF16)
    jumps[...] = rounded
    one = part_lam[...] + dot(rounded, lam[d.plane :, d.plane :])
    two = part_mu[...] + dot(rounded, mu[d.plane :, d.plane :])
    result[...] = wide(mod[0], 2 * d.face) * one + wide(mod[1], 2 * d.face) * two
    payloads(d, result[:, : d.face], result[:, d.face :], maps, on_chip, off_chip)


def second_plane(d, plane, zed, lam, mu, mod, masks, jumps):
    one = dot(plane[...], lam[: d.plane, : d.plane]) + dot(zed[...], lam[d.plane :, : d.plane])
    two = dot(plane[...], mu[: d.plane, : d.plane]) + dot(zed[...], mu[d.plane :, : d.plane])
    field = wide(mod[0], d.plane) * one + wide(mod[1], d.plane) * two

    def put(which, n, value):
        jumps[d.block(n), which * d.face : (which + 1) * d.face] = value.astype(BF16)

    plane_jumps(d, field, masks, put)


def last_z(d, field, from_off, from_chip, maps, masks, plane, jumps, held):
    def put(which, rows, value):
        held[rows, which * d.face : (which + 1) * d.face] = value

    z_jumps(d, field, from_off, from_chip, maps, masks, put)
    jumps[:, : d.plane] = plane[...]
    jumps[:, d.plane :] = held[...].astype(BF16)


def project_rows(d, picks, lanes, basis, out, rows_out, sems):
    width = lanes.stop - lanes.start
    group = max(g for g in (1, 2, 3, 6) if d.subs % g == 0 and g * width <= 768)
    chunk = d.terms // CHUNKS
    copies = []
    for n in range(0, d.subs, group):
        right = picks[n : n + group]
        right = right[0] if group == 1 else jnp.concatenate(right, axis=1)
        for c in range(CHUNKS):
            rows = slice(c * chunk, (c + 1) * chunk)
            value = dot(basis[rows, :], right)
            for m in range(group):
                rows_out[n + m, rows, :] = value[:, m * width : (m + 1) * width].astype(BF16)
                y, x = divmod(n + m, d.breadth)
                copy = pltpu.make_async_copy(
                    rows_out.at[n + m, rows, :],
                    out.at[0, y, x, rows, lanes],
                    sems.at[n + m, c],
                )
                copy.start()
                copies.append(copy)
    for copy in copies:
        copy.wait()


def project_early(d, plane, basis, out, rows_out, sems):
    start = pl.multiple_of(lax.axis_index("smp") * d.share, 128)
    picks = [plane[d.block(n), pl.ds(start, d.face)] for n in range(d.subs)]
    project_rows(d, picks, slice(0, d.face), basis, out, rows_out, sems)


def project_late(
    d, field, from_off, from_chip, maps, masks, plane, basis, early, out, held, jumps, rows_out, sems
):
    last_z(d, field, from_off, from_chip, maps, masks, plane, jumps, held)
    width = d.share - d.face
    start = pl.multiple_of(lax.axis_index("smp") * d.share + d.face, 128)
    picks = [jumps[d.block(n), pl.ds(start, width)] for n in range(d.subs)]
    project_rows(d, picks, slice(d.face, d.share), basis, out, rows_out, sems)


def project_share(d, jumps, basis, out, rows_out, sems):
    picks = [jumps[d.block(n), :] for n in range(d.subs)]
    project_rows(d, picks, slice(0, d.share), basis, out, rows_out, sems)


def per_device(
    trial, stiff_lam, stiff_mu, log_modes, nodes, quad_weights, chaos_index, bonds, face_map
):
    parts = lax.axis_size("smp")
    layers = lax.axis_size("sub")
    d = Sizes(trial, chaos_index.shape[0], parts)
    rows, face = d.rows, d.face
    own = trial.reshape(d.subs * d.here, d.width)
    others = [
        lax.ppermute(own, "smp", [(i, (i + shift) % parts) for i in range(parts)])
        for shift in range(1, parts)
    ]
    pairs = [(i, i ^ 1) for i in range(layers)]
    ends = [(i, i + 1) for i in range(1, layers - 1, 2)]
    ends = ends + [(j, i) for i, j in ends]

    def exchange(on_chip, off_chip):
        far = lax.ppermute(off_chip, "sub", ends)
        return lax.ppermute(on_chip, "sub", pairs), far

    def run(body, *args, **options):
        return call(functools.partial(body, d), *args, **options)

    product = shaped((d.subs * d.here, d.width))
    lam, mu = run(
        load,
        [shaped(stiff_lam.shape, BF16), shaped(stiff_mu.shape, BF16)],
        [HBM] * 2,
        [stiff_lam, stiff_mu],
        scratch=[pltpu.SemaphoreType.DMA((2,))],
        grant=51 << 20,
    )
    mod, maps, own_lam, own_mu = run(
        prepare,
        [shaped((2, rows, 128)), shaped((2, d.subs, 8, face), jnp.int32), product, product],
        [VMEM] * 6,
        [
            own, lam, mu,
            log_modes.transpose(0, 1, 3, 2, 4), nodes, face_map.transpose(0, 2, 1, 3),
        ],
    )
    field, on_chip, off_chip = run(
        first_z,
        [shaped((rows, 2 * face)), shaped((rows, face)), shaped((rows, face))],
        [VMEM] * (parts + 5),
        [*others, lam, mu, mod, maps, own_lam, own_mu],
    )
    near, far = exchange(on_chip, off_chip)
    basis, masks = run(
        tables,
        [shaped((d.terms, d.samples), BF16), shaped((6, d.subs, 8, 128))],
        [VMEM] * 4,
        [nodes, quad_weights.reshape(1, -1), chaos_index.T, bonds.transpose(0, 3, 2, 1)],
    )
    jumps_plane, part_lam, part_mu = run(
        first_plane,
        [shaped((rows, d.plane), BF16), shaped((rows, 2 * face)), shaped((rows, 2 * face))],
        [VMEM] * (parts + 5),
        [*others, lam, mu, mod, own_lam, own_mu, masks],
        scratch=[pltpu.VMEM((rows, d.plane), F32)],
    )
    jumps_z, field, on_chip, off_chip = run(
        second_z,
        [
            shaped((rows, 2 * face), BF16),
            shaped((rows, 2 * face)),
            shaped((rows, face)),
            shaped((rows, face)),
        ],
        [VMEM] * 10,
        [field, far, near, maps, masks, mod, lam, mu, part_lam, part_mu],
        scratch=[pltpu.VMEM((rows, 2 * face), F32)],
    )
    near, far = exchange(on_chip, off_chip)
    (plane,) = run(
        second_plane,
        [shaped((rows, d.plane), BF16)],
        [VMEM] * 6,
        [jumps_plane, jumps_z, lam, mu, mod, masks],
    )
    last = [field, far, near, maps, masks, plane]
    held = pltpu.VMEM((rows, 2 * face), F32)
    result = [shaped((1, d.height, d.breadth, d.terms, d.share), BF16)]

    def buffers(width):
        return [
            pltpu.VMEM((d.subs, d.terms, width), BF16),
            pltpu.SemaphoreType.DMA((d.subs, CHUNKS)),
        ]

    if d.share == 3 * face:
        (early,) = run(
            project_early,
            result,
            [VMEM] * 2,
            [plane, basis],
            out_specs=[HBM],
            scratch=buffers(face),
        )
        (out,) = run(
            project_late,
            result,
            [VMEM] * 7 + [HBM],
            [*last, basis, early],
            out_specs=[HBM],
            scratch=[held, pltpu.VMEM((rows, d.width), BF16)] + buffers(2 * face),
            aliases={7: 0},
        )
    else:
        (jumps,) = run(last_z, [shaped((rows, d.width), BF16)], [VMEM] * 6, last, scratch=[held])
        start = lax.axis_index("smp") * d.share
        jumps = lax.dynamic_slice_in_dim(jumps, start, d.share, 1)
        (out,) = run(
            project_share, result, [VMEM] * 2, [jumps, basis], out_specs=[HBM], scratch=buffers(d.share)
        )
    return jnp.swapaxes(out, -1, -2)


def solution(mesh):
    return jax.shard_map(
        per_device,
        mesh=mesh,
        in_specs=(
            P("sub", None, None, "smp", None),
            P(),
            P(),
            P(None, "sub", None, None, None),
            P(),
            P(),
            P(),
            P(),
            P("sub", None, None, None),
        ),
        out_specs=P("sub", None, None, "smp", None),
        check_vma=False,
    )
```

```python
import functools

import jax
import jax.numpy as jnp
from jax import lax
from jax.experimental import pallas as pl
from jax.experimental.pallas import tpu as pltpu
from jax.sharding import PartitionSpec as P

F32 = jnp.float32
BF16 = jnp.bfloat16
VMEM = pl.BlockSpec(memory_space=pltpu.VMEM)
CHUNKS = 3
HBM = pl.BlockSpec(memory_space=pltpu.HBM)


def shaped(shape, dtype=F32):
    return jax.ShapeDtypeStruct(shape, dtype)


def call(body, outs, specs, args, flops=0, scratch=(), out_specs=None, grant=24 << 20, aliases=None):
    return pl.pallas_call(
        body,
        out_shape=outs,
        in_specs=specs,
        out_specs=[VMEM] * len(outs) if out_specs is None else out_specs,
        scratch_shapes=list(scratch),
        input_output_aliases=aliases or {},
        cost_estimate=pl.CostEstimate(flops=flops, bytes_accessed=0, transcendentals=0),
        compiler_params=pltpu.CompilerParams(vmem_limit_bytes=grant),
    )(*args)


def dot(a, b):
    return jnp.dot(a, b, preferred_element_type=F32)


def wide(column, width):
    return jnp.concatenate([column] * (width // 128), axis=1)


class Sizes:
    def __init__(self, trial, basis_size, parts):
        _, self.height, self.breadth, self.here, self.width = trial.shape
        self.face = self.width // 6
        self.subs = self.height * self.breadth
        self.parts = parts
        self.samples = self.here * parts
        self.rows = self.subs * self.samples
        self.plane = 4 * self.face
        self.terms = basis_size
        self.share = self.width // parts

    def own(self, n, part):
        return pl.ds(pl.multiple_of(n * self.samples + part * self.here, 8), self.here)

    def block(self, n):
        return slice(n * self.samples, (n + 1) * self.samples)

    def group(self, n):
        return slice(n * self.here, (n + 1) * self.here)


def load(d, lam, mu, lam_here, mu_here, sems):
    copies = [
        pltpu.make_async_copy(lam, lam_here, sems.at[0]),
        pltpu.make_async_copy(mu, mu_here, sems.at[1]),
    ]
    for copy in copies:
        copy.start()
    for copy in copies:
        copy.wait()


def prepare(d, trial, lam, mu, modes, nodes, faces, mod, maps, first, second):
    first[...] = dot(trial[...], lam[...])
    second[...] = dot(trial[...], mu[...])
    points = nodes[...]
    for c in range(2):
        for n in range(d.subs):
            row = modes[c, 0, n % d.breadth, pl.ds(n // d.breadth, 1), :]
            total = jnp.exp(jnp.sum(points * row, axis=1, keepdims=True))
            mod[c, d.block(n), :] = jnp.broadcast_to(total, (d.samples, 128))
    target = lax.broadcasted_iota(jnp.int32, (d.face, d.face), 0)
    source = lax.broadcasted_iota(jnp.int32, (8, d.face), 1).astype(F32).astype(BF16)
    for n in range(d.subs):
        row = faces[0, n % d.breadth, pl.ds(n // d.breadth, 1), :]
        hit = jnp.where(row == target, 1.0, 0.0).astype(BF16)
        back = lax.dot_general(
            source, hit, (((1,), (1,)), ((), ())), preferred_element_type=F32
        )
        maps[0, n] = jnp.broadcast_to(row, (8, d.face))
        maps[1, n] = back.astype(jnp.int32)


def tables(d, nodes, weights, chaos, bonds, basis, masks):
    points = nodes[...]
    layer = lax.axis_index("sub")
    lane = lax.broadcasted_iota(jnp.int32, (d.height, bonds.shape[-1]), 1)

    def at(axis, x, z):
        picked = jnp.where(lane == z, bonds[axis, x].astype(F32), 0.0)
        return jnp.sum(picked, axis=1, keepdims=True)

    along = [[at(axis, x, layer) for x in range(d.breadth)] for axis in range(3)]
    under = [at(2, x, layer - 1) for x in range(d.breadth)]
    for n in range(d.subs):
        y, x = divmod(n, d.breadth)
        columns = [
            (along[0][(x - 1) % d.breadth], y),
            (along[0][x], y),
            (along[1][x], (y - 1) % d.height),
            (along[1][x], y),
            (under[x], y),
            (along[2][x], y),
        ]
        for which, (column, at_y) in enumerate(columns):
            masks[which, n] = jnp.broadcast_to(column[at_y : at_y + 1], (8, 128))
    one = jnp.sqrt(3.0) * points
    two = jnp.sqrt(5.0) * (1.5 * points * points - 0.5)
    three = jnp.sqrt(7.0) * (2.5 * points * points * points - 1.5 * points)
    total = jnp.ones((d.samples, d.terms), F32)
    for k in range(points.shape[1]):
        c = chaos[k : k + 1, :]
        high = jnp.where(c == 3, three[:, k : k + 1], two[:, k : k + 1])
        low = jnp.where(c == 1, one[:, k : k + 1], 1.0)
        total = total * jnp.where(c >= 2, high, low)
    square = (d.samples, d.samples)
    diagonal = lax.broadcasted_iota(jnp.int32, square, 0) == lax.broadcasted_iota(
        jnp.int32, square, 1
    )
    column = jnp.sum(jnp.where(diagonal, weights[...], 0.0), axis=1, keepdims=True)
    basis[...] = (column * total).T.astype(BF16)


def payloads(d, low, high, maps, on_chip, off_chip):
    even = lax.rem(lax.axis_index("sub"), 2) == 0
    for n in range(d.subs):
        back = maps[1, n]
        for start in range(n * d.samples, (n + 1) * d.samples, 8):
            rows = slice(start, start + 8)
            minus = low[rows]
            pushed = jnp.take_along_axis(high[rows], back, axis=1, mode="promise_in_bounds")
            on_chip[rows, :] = jnp.where(even, pushed, minus)
            off_chip[rows, :] = jnp.where(even, minus, pushed)


def part_of(d, shift):
    here = lax.axis_index("smp")
    return lax.rem(here - shift + d.parts, d.parts)


def combine(d, mod, part, first, second, field):
    width = field.shape[1]
    for n in range(d.subs):
        own = d.own(n, part)
        field[own, :] = (
            wide(mod[0, own, :], width) * first[d.group(n), :]
            + wide(mod[1, own, :], width) * second[d.group(n), :]
        )


def first_z(d, *refs):
    others = refs[: d.parts - 1]
    lam, mu, mod, maps, own_lam, own_mu, field, on_chip, off_chip = refs[d.parts - 1 :]
    at = slice(d.plane, d.width)
    combine(d, mod, lax.axis_index("smp"), own_lam.at[:, at], own_mu.at[:, at], field)
    for shift, other in enumerate(others, 1):
        rows = other[...]
        combine(d, mod, part_of(d, shift), dot(rows, lam[:, at]), dot(rows, mu[:, at]), field)
    payloads(d, field[:, : d.face], field[:, d.face :], maps, on_chip, off_chip)


def plane_jumps(d, field, masks, out):
    def mask(which, n):
        return jnp.concatenate([masks[which, n]] * (d.samples // 8), axis=0)

    for n in range(d.subs):
        y, x = divmod(n, d.breadth)
        left = y * d.breadth + (x - 1) % d.breadth
        right = y * d.breadth + (x + 1) % d.breadth
        front = (y - 1) % d.height * d.breadth + x
        behind = (y + 1) % d.height * d.breadth + x

        def face(which, m):
            return field[d.block(m), which * d.face : (which + 1) * d.face]

        out(0, n, mask(0, n) * (face(0, n) - face(1, left)))
        out(1, n, mask(1, n) * (face(1, n) - face(0, right)))
        out(2, n, mask(2, n) * (face(2, n) - face(3, front)))
        out(3, n, mask(3, n) * (face(3, n) - face(2, behind)))


def z_jumps(d, field, from_off, from_chip, maps, masks, out):
    layer = lax.axis_index("sub")
    even = lax.rem(layer, 2) == 0
    inside = jnp.logical_and(layer > 0, layer < lax.axis_size("sub") - 1)
    for n in range(d.subs):
        for start in range(n * d.samples, (n + 1) * d.samples, 8):
            rows = slice(start, start + 8)
            near, far = from_chip[rows, :], jnp.where(inside, from_off[rows, :], 0.0)
            above = jnp.where(even, near, far)
            below = jnp.where(even, far, near)
            matched = jnp.take_along_axis(above, maps[0, n], axis=1, mode="promise_in_bounds")
            out(0, rows, masks[4, n] * (field[rows, : d.face] - below))
            out(1, rows, masks[5, n] * (field[rows, d.face :] - matched))


def first_plane(d, *refs):
    others = refs[: d.parts - 1]
    lam, mu, mod, own_lam, own_mu, masks, jumps, part_lam, part_mu, field = refs[d.parts - 1 :]
    at = slice(0, d.plane)
    combine(d, mod, lax.axis_index("smp"), own_lam.at[:, at], own_mu.at[:, at], field)
    for shift, other in enumerate(others, 1):
        rows = other[...]
        combine(d, mod, part_of(d, shift), dot(rows, lam[:, at]), dot(rows, mu[:, at]), field)

    def put(which, n, value):
        jumps[d.block(n), which * d.face : (which + 1) * d.face] = value.astype(BF16)

    plane_jumps(d, field, masks, put)
    part_lam[...] = dot(jumps[...], lam[: d.plane, d.plane :])
    part_mu[...] = dot(jumps[...], mu[: d.plane, d.plane :])


def second_z(
    d, field, from_off, from_chip, maps, masks, mod, lam, mu, part_lam, part_mu,
    jumps, result, on_chip, off_chip, held,
):
    def put(which, rows, value):
        held[rows, which * d.face : (which + 1) * d.face] = value

    z_jumps(d, field, from_off, from_chip, maps, masks, put)
    rounded = held[...].astype(BF16)
    jumps[...] = rounded
    one = part_lam[...] + dot(rounded, lam[d.plane :, d.plane :])
    two = part_mu[...] + dot(rounded, mu[d.plane :, d.plane :])
    result[...] = wide(mod[0], 2 * d.face) * one + wide(mod[1], 2 * d.face) * two
    payloads(d, result[:, : d.face], result[:, d.face :], maps, on_chip, off_chip)


def second_plane(d, plane, zed, lam, mu, mod, masks, jumps):
    one = dot(plane[...], lam[: d.plane, : d.plane]) + dot(zed[...], lam[d.plane :, : d.plane])
    two = dot(plane[...], mu[: d.plane, : d.plane]) + dot(zed[...], mu[d.plane :, : d.plane])
    field = wide(mod[0], d.plane) * one + wide(mod[1], d.plane) * two

    def put(which, n, value):
        jumps[d.block(n), which * d.face : (which + 1) * d.face] = value.astype(BF16)

    plane_jumps(d, field, masks, put)


def last_z(d, field, from_off, from_chip, maps, masks, plane, jumps, held):
    def put(which, rows, value):
        held[rows, which * d.face : (which + 1) * d.face] = value

    z_jumps(d, field, from_off, from_chip, maps, masks, put)
    jumps[:, : d.plane] = plane[...]
    jumps[:, d.plane :] = held[...].astype(BF16)


def project_rows(d, picks, lanes, basis, out, rows_out, sems):
    width = lanes.stop - lanes.start
    group = max(g for g in (1, 2, 3, 6) if d.subs % g == 0 and g * width <= 768)
    chunk = d.terms // CHUNKS
    copies = []
    for n in range(0, d.subs, group):
        right = picks[n : n + group]
        right = right[0] if group == 1 else jnp.concatenate(right, axis=1)
        for c in range(CHUNKS):
            rows = slice(c * chunk, (c + 1) * chunk)
            value = dot(basis[rows, :], right)
            for m in range(group):
                rows_out[n + m, rows, :] = value[:, m * width : (m + 1) * width].astype(BF16)
                y, x = divmod(n + m, d.breadth)
                copy = pltpu.make_async_copy(
                    rows_out.at[n + m, rows, :],
                    out.at[0, y, x, rows, lanes],
                    sems.at[n + m, c],
                )
                copy.start()
                copies.append(copy)
    for copy in copies:
        copy.wait()


def project_early(d, plane, basis, out, rows_out, sems):
    start = pl.multiple_of(lax.axis_index("smp") * d.share, 128)
    picks = [plane[d.block(n), pl.ds(start, d.face)] for n in range(d.subs)]
    project_rows(d, picks, slice(0, d.face), basis, out, rows_out, sems)


def project_late(
    d, field, from_off, from_chip, maps, masks, plane, basis, early, out, held, jumps, rows_out, sems
):
    last_z(d, field, from_off, from_chip, maps, masks, plane, jumps, held)
    width = d.share - d.face
    start = pl.multiple_of(lax.axis_index("smp") * d.share + d.face, 128)
    picks = [jumps[d.block(n), pl.ds(start, width)] for n in range(d.subs)]
    project_rows(d, picks, slice(d.face, d.share), basis, out, rows_out, sems)


def project_share(d, jumps, basis, out, rows_out, sems):
    picks = [jumps[d.block(n), :] for n in range(d.subs)]
    project_rows(d, picks, slice(0, d.share), basis, out, rows_out, sems)


def per_device(
    trial, stiff_lam, stiff_mu, log_modes, nodes, quad_weights, chaos_index, bonds, face_map
):
    parts = lax.axis_size("smp")
    layers = lax.axis_size("sub")
    d = Sizes(trial, chaos_index.shape[0], parts)
    rows, face = d.rows, d.face
    own = trial.reshape(d.subs * d.here, d.width)
    others = [
        lax.ppermute(own, "smp", [(i, (i + shift) % parts) for i in range(parts)])
        for shift in range(1, parts)
    ]
    pairs = [(i, i ^ 1) for i in range(layers)]
    partner = {i: i + 1 if i % 2 else i - 1 for i in range(1, layers - 1)}
    across = [
        (i * parts + s, partner[i] * parts + s if i in partner else i * parts + (s + 1) % parts)
        for i in range(layers)
        for s in range(parts)
    ]

    def exchange(on_chip, off_chip):
        far = lax.ppermute(off_chip, ("sub", "smp"), across)
        return lax.ppermute(on_chip, "sub", pairs), far

    def run(body, *args, **options):
        return call(functools.partial(body, d), *args, **options)

    product = shaped((d.subs * d.here, d.width))
    lam, mu = run(
        load,
        [shaped(stiff_lam.shape, BF16), shaped(stiff_mu.shape, BF16)],
        [HBM] * 2,
        [stiff_lam, stiff_mu],
        scratch=[pltpu.SemaphoreType.DMA((2,))],
        grant=51 << 20,
    )
    mod, maps, own_lam, own_mu = run(
        prepare,
        [shaped((2, rows, 128)), shaped((2, d.subs, 8, face), jnp.int32), product, product],
        [VMEM] * 6,
        [
            own, lam, mu,
            log_modes.transpose(0, 1, 3, 2, 4), nodes, face_map.transpose(0, 2, 1, 3),
        ],
    )
    field, on_chip, off_chip = run(
        first_z,
        [shaped((rows, 2 * face)), shaped((rows, face)), shaped((rows, face))],
        [VMEM] * (parts + 5),
        [*others, lam, mu, mod, maps, own_lam, own_mu],
    )
    near, far = exchange(on_chip, off_chip)
    basis, masks = run(
        tables,
        [shaped((d.terms, d.samples), BF16), shaped((6, d.subs, 8, 128))],
        [VMEM] * 4,
        [nodes, quad_weights.reshape(1, -1), chaos_index.T, bonds.transpose(0, 3, 2, 1)],
    )
    jumps_plane, part_lam, part_mu = run(
        first_plane,
        [shaped((rows, d.plane), BF16), shaped((rows, 2 * face)), shaped((rows, 2 * face))],
        [VMEM] * (parts + 5),
        [*others, lam, mu, mod, own_lam, own_mu, masks],
        scratch=[pltpu.VMEM((rows, d.plane), F32)],
    )
    jumps_z, field, on_chip, off_chip = run(
        second_z,
        [
            shaped((rows, 2 * face), BF16),
            shaped((rows, 2 * face)),
            shaped((rows, face)),
            shaped((rows, face)),
        ],
        [VMEM] * 10,
        [field, far, near, maps, masks, mod, lam, mu, part_lam, part_mu],
        scratch=[pltpu.VMEM((rows, 2 * face), F32)],
    )
    near, far = exchange(on_chip, off_chip)
    (plane,) = run(
        second_plane,
        [shaped((rows, d.plane), BF16)],
        [VMEM] * 6,
        [jumps_plane, jumps_z, lam, mu, mod, masks],
    )
    last = [field, far, near, maps, masks, plane]
    held = pltpu.VMEM((rows, 2 * face), F32)
    result = [shaped((1, d.height, d.breadth, d.terms, d.share), BF16)]

    def buffers(width):
        return [
            pltpu.VMEM((d.subs, d.terms, width), BF16),
            pltpu.SemaphoreType.DMA((d.subs, CHUNKS)),
        ]

    if d.share == 3 * face:
        (early,) = run(
            project_early,
            result,
            [VMEM] * 2,
            [plane, basis],
            out_specs=[HBM],
            scratch=buffers(face),
        )
        (out,) = run(
            project_late,
            result,
            [VMEM] * 7 + [HBM],
            [*last, basis, early],
            out_specs=[HBM],
            scratch=[held, pltpu.VMEM((rows, d.width), BF16)] + buffers(2 * face),
            aliases={7: 0},
        )
    else:
        (jumps,) = run(last_z, [shaped((rows, d.width), BF16)], [VMEM] * 6, last, scratch=[held])
        start = lax.axis_index("smp") * d.share
        jumps = lax.dynamic_slice_in_dim(jumps, start, d.share, 1)
        (out,) = run(
            project_share, result, [VMEM] * 2, [jumps, basis], out_specs=[HBM], scratch=buffers(d.share)
        )
    return jnp.swapaxes(out, -1, -2)


def solution(mesh):
    return jax.shard_map(
        per_device,
        mesh=mesh,
        in_specs=(
            P("sub", None, None, "smp", None),
            P(),
            P(),
            P(None, "sub", None, None, None),
            P(),
            P(),
            P(),
            P(),
            P("sub", None, None, None),
        ),
        out_specs=P("sub", None, None, "smp", None),
        check_vma=False,
    )
```

```python
import functools

import jax
import jax.numpy as jnp
from jax import lax
from jax.experimental import pallas as pl
from jax.experimental.pallas import tpu as pltpu
from jax.sharding import PartitionSpec as P

F32 = jnp.float32
BF16 = jnp.bfloat16
VMEM = pl.BlockSpec(memory_space=pltpu.VMEM)
CHUNK = 144
HBM = pl.BlockSpec(memory_space=pltpu.HBM)


def shaped(shape, dtype=F32):
    return jax.ShapeDtypeStruct(shape, dtype)


def call(body, outs, specs, args, flops=0, scratch=(), out_specs=None, grant=24 << 20, aliases=None):
    return pl.pallas_call(
        body,
        out_shape=outs,
        in_specs=specs,
        out_specs=[VMEM] * len(outs) if out_specs is None else out_specs,
        scratch_shapes=list(scratch),
        input_output_aliases=aliases or {},
        cost_estimate=pl.CostEstimate(flops=flops, bytes_accessed=0, transcendentals=0),
        compiler_params=pltpu.CompilerParams(vmem_limit_bytes=grant),
    )(*args)


def dot(a, b):
    return jnp.dot(a, b, preferred_element_type=F32)


def wide(column, width):
    return jnp.concatenate([column] * (width // 128), axis=1)


class Sizes:
    def __init__(self, trial, basis_size, parts):
        _, self.height, self.breadth, self.here, self.width = trial.shape
        self.face = self.width // 6
        self.subs = self.height * self.breadth
        self.parts = parts
        self.samples = self.here * parts
        self.rows = self.subs * self.samples
        self.plane = 4 * self.face
        self.terms = basis_size
        self.share = self.width // parts

    def own(self, n, part):
        return pl.ds(pl.multiple_of(n * self.samples + part * self.here, 8), self.here)

    def block(self, n):
        return slice(n * self.samples, (n + 1) * self.samples)

    def group(self, n):
        return slice(n * self.here, (n + 1) * self.here)


def load(d, lam, mu, lam_here, mu_here, sems):
    copies = [
        pltpu.make_async_copy(lam, lam_here, sems.at[0]),
        pltpu.make_async_copy(mu, mu_here, sems.at[1]),
    ]
    for copy in copies:
        copy.start()
    for copy in copies:
        copy.wait()


def prepare(d, trial, lam, mu, modes, nodes, faces, mod, maps, first, second):
    first[...] = dot(trial[...], lam[...])
    second[...] = dot(trial[...], mu[...])
    points = nodes[...]
    for c in range(2):
        for n in range(d.subs):
            row = modes[c, 0, n % d.breadth, pl.ds(n // d.breadth, 1), :]
            total = jnp.exp(jnp.sum(points * row, axis=1, keepdims=True))
            mod[c, d.block(n), :] = jnp.broadcast_to(total, (d.samples, 128))
    target = lax.broadcasted_iota(jnp.int32, (d.face, d.face), 0)
    source = lax.broadcasted_iota(jnp.int32, (8, d.face), 1).astype(F32).astype(BF16)
    for n in range(d.subs):
        row = faces[0, n % d.breadth, pl.ds(n // d.breadth, 1), :]
        hit = jnp.where(row == target, 1.0, 0.0).astype(BF16)
        back = lax.dot_general(
            source, hit, (((1,), (1,)), ((), ())), preferred_element_type=F32
        )
        maps[0, n] = jnp.broadcast_to(row, (8, d.face))
        maps[1, n] = back.astype(jnp.int32)


def tables(d, nodes, weights, chaos, bonds, basis, masks):
    points = nodes[...]
    layer = lax.axis_index("sub")
    lane = lax.broadcasted_iota(jnp.int32, (d.height, bonds.shape[-1]), 1)

    def at(axis, x, z):
        picked = jnp.where(lane == z, bonds[axis, x].astype(F32), 0.0)
        return jnp.sum(picked, axis=1, keepdims=True)

    along = [[at(axis, x, layer) for x in range(d.breadth)] for axis in range(3)]
    under = [at(2, x, layer - 1) for x in range(d.breadth)]
    for n in range(d.subs):
        y, x = divmod(n, d.breadth)
        columns = [
            (along[0][(x - 1) % d.breadth], y),
            (along[0][x], y),
            (along[1][x], (y - 1) % d.height),
            (along[1][x], y),
            (under[x], y),
            (along[2][x], y),
        ]
        for which, (column, at_y) in enumerate(columns):
            masks[which, n] = jnp.broadcast_to(column[at_y : at_y + 1], (8, 128))
    one = jnp.sqrt(3.0) * points
    two = jnp.sqrt(5.0) * (1.5 * points * points - 0.5)
    three = jnp.sqrt(7.0) * (2.5 * points * points * points - 1.5 * points)
    total = jnp.ones((d.samples, d.terms), F32)
    for k in range(points.shape[1]):
        c = chaos[k : k + 1, :]
        high = jnp.where(c == 3, three[:, k : k + 1], two[:, k : k + 1])
        low = jnp.where(c == 1, one[:, k : k + 1], 1.0)
        total = total * jnp.where(c >= 2, high, low)
    square = (d.samples, d.samples)
    diagonal = lax.broadcasted_iota(jnp.int32, square, 0) == lax.broadcasted_iota(
        jnp.int32, square, 1
    )
    column = jnp.sum(jnp.where(diagonal, weights[...], 0.0), axis=1, keepdims=True)
    basis[...] = (column * total).T.astype(BF16)


def payloads(d, low, high, maps, on_chip, off_chip):
    even = lax.rem(lax.axis_index("sub"), 2) == 0
    for n in range(d.subs):
        back = maps[1, n]
        for start in range(n * d.samples, (n + 1) * d.samples, 8):
            rows = slice(start, start + 8)
            minus = low[rows]
            pushed = jnp.take_along_axis(high[rows], back, axis=1, mode="promise_in_bounds")
            on_chip[rows, :] = jnp.where(even, pushed, minus)
            off_chip[rows, :] = jnp.where(even, minus, pushed)


def part_of(d, shift):
    here = lax.axis_index("smp")
    return lax.rem(here - shift + d.parts, d.parts)


def combine(d, mod, part, first, second, field):
    width = field.shape[1]
    for n in range(d.subs):
        own = d.own(n, part)
        field[own, :] = (
            wide(mod[0, own, :], width) * first[d.group(n), :]
            + wide(mod[1, own, :], width) * second[d.group(n), :]
        )


def first_z(d, *refs):
    others = refs[: d.parts - 1]
    lam, mu, mod, maps, own_lam, own_mu, field, on_chip, off_chip = refs[d.parts - 1 :]
    at = slice(d.plane, d.width)
    combine(d, mod, lax.axis_index("smp"), own_lam.at[:, at], own_mu.at[:, at], field)
    for shift, other in enumerate(others, 1):
        rows = other[...]
        combine(d, mod, part_of(d, shift), dot(rows, lam[:, at]), dot(rows, mu[:, at]), field)
    payloads(d, field[:, : d.face], field[:, d.face :], maps, on_chip, off_chip)


def plane_jumps(d, field, masks, out):
    def mask(which, n):
        return jnp.concatenate([masks[which, n]] * (d.samples // 8), axis=0)

    for n in range(d.subs):
        y, x = divmod(n, d.breadth)
        left = y * d.breadth + (x - 1) % d.breadth
        right = y * d.breadth + (x + 1) % d.breadth
        front = (y - 1) % d.height * d.breadth + x
        behind = (y + 1) % d.height * d.breadth + x

        def face(which, m):
            return field[d.block(m), which * d.face : (which + 1) * d.face]

        out(0, n, mask(0, n) * (face(0, n) - face(1, left)))
        out(1, n, mask(1, n) * (face(1, n) - face(0, right)))
        out(2, n, mask(2, n) * (face(2, n) - face(3, front)))
        out(3, n, mask(3, n) * (face(3, n) - face(2, behind)))


def z_jumps(d, field, from_off, from_chip, maps, masks, out):
    layer = lax.axis_index("sub")
    even = lax.rem(layer, 2) == 0
    inside = jnp.logical_and(layer > 0, layer < lax.axis_size("sub") - 1)
    for n in range(d.subs):
        for start in range(n * d.samples, (n + 1) * d.samples, 8):
            rows = slice(start, start + 8)
            near, far = from_chip[rows, :], jnp.where(inside, from_off[rows, :], 0.0)
            above = jnp.where(even, near, far)
            below = jnp.where(even, far, near)
            matched = jnp.take_along_axis(above, maps[0, n], axis=1, mode="promise_in_bounds")
            out(0, rows, masks[4, n] * (field[rows, : d.face] - below))
            out(1, rows, masks[5, n] * (field[rows, d.face :] - matched))


def first_plane(d, *refs):
    others = refs[: d.parts - 1]
    lam, mu, mod, own_lam, own_mu, masks, jumps, part_lam, part_mu, field = refs[d.parts - 1 :]
    at = slice(0, d.plane)
    combine(d, mod, lax.axis_index("smp"), own_lam.at[:, at], own_mu.at[:, at], field)
    for shift, other in enumerate(others, 1):
        rows = other[...]
        combine(d, mod, part_of(d, shift), dot(rows, lam[:, at]), dot(rows, mu[:, at]), field)

    def put(which, n, value):
        jumps[d.block(n), which * d.face : (which + 1) * d.face] = value.astype(BF16)

    plane_jumps(d, field, masks, put)
    part_lam[...] = dot(jumps[...], lam[: d.plane, d.plane :])
    part_mu[...] = dot(jumps[...], mu[: d.plane, d.plane :])


def second_z(
    d, field, from_off, from_chip, maps, masks, mod, lam, mu, part_lam, part_mu,
    jumps, result, on_chip, off_chip, held,
):
    def put(which, rows, value):
        held[rows, which * d.face : (which + 1) * d.face] = value

    z_jumps(d, field, from_off, from_chip, maps, masks, put)
    rounded = held[...].astype(BF16)
    jumps[...] = rounded
    one = part_lam[...] + dot(rounded, lam[d.plane :, d.plane :])
    two = part_mu[...] + dot(rounded, mu[d.plane :, d.plane :])
    result[...] = wide(mod[0], 2 * d.face) * one + wide(mod[1], 2 * d.face) * two
    payloads(d, result[:, : d.face], result[:, d.face :], maps, on_chip, off_chip)


def second_plane(d, plane, zed, lam, mu, mod, masks, jumps):
    one = dot(plane[...], lam[: d.plane, : d.plane]) + dot(zed[...], lam[d.plane :, : d.plane])
    two = dot(plane[...], mu[: d.plane, : d.plane]) + dot(zed[...], mu[d.plane :, : d.plane])
    field = wide(mod[0], d.plane) * one + wide(mod[1], d.plane) * two

    def put(which, n, value):
        jumps[d.block(n), which * d.face : (which + 1) * d.face] = value.astype(BF16)

    plane_jumps(d, field, masks, put)


def last_z(d, field, from_off, from_chip, maps, masks, plane, jumps, held):
    def put(which, rows, value):
        held[rows, which * d.face : (which + 1) * d.face] = value

    z_jumps(d, field, from_off, from_chip, maps, masks, put)
    jumps[:, : d.plane] = plane[...]
    jumps[:, d.plane :] = held[...].astype(BF16)


def project_rows(d, picks, lanes, basis, out, rows_out, sem):
    width = lanes.stop - lanes.start
    group = max(g for g in (1, 2, 3, 6) if d.subs % g == 0 and g * width <= 768)
    for n in range(0, d.subs, group):
        right = picks[n : n + group]
        right = right[0] if group == 1 else jnp.concatenate(right, axis=1)
        for start in range(0, d.terms, CHUNK):
            rows = slice(start, min(start + CHUNK, d.terms))
            value = dot(basis[rows, :], right)
            for m in range(group):
                y, x = divmod(n + m, d.breadth)
                rows_out[y, x, rows, :] = value[:, m * width : (m + 1) * width].astype(BF16)
                pltpu.make_async_copy(
                    rows_out.at[y, x, rows, :], out.at[0, y, x, rows, lanes], sem
                ).start()
    pltpu.make_async_copy(rows_out, out.at[0, :, :, :, lanes], sem).wait()


def project_early(d, plane, basis, out, rows_out, sem):
    start = pl.multiple_of(lax.axis_index("smp") * d.share, 128)
    picks = [plane[d.block(n), pl.ds(start, d.face)] for n in range(d.subs)]
    project_rows(d, picks, slice(0, d.face), basis, out, rows_out, sem)


def project_late(
    d, field, from_off, from_chip, maps, masks, plane, basis, early, out, held, jumps, rows_out, sem
):
    last_z(d, field, from_off, from_chip, maps, masks, plane, jumps, held)
    width = d.share - d.face
    start = pl.multiple_of(lax.axis_index("smp") * d.share + d.face, 128)
    picks = [jumps[d.block(n), pl.ds(start, width)] for n in range(d.subs)]
    project_rows(d, picks, slice(d.face, d.share), basis, out, rows_out, sem)


def project_share(d, jumps, basis, out, rows_out, sem):
    picks = [jumps[d.block(n), :] for n in range(d.subs)]
    project_rows(d, picks, slice(0, d.share), basis, out, rows_out, sem)


def per_device(
    trial, stiff_lam, stiff_mu, log_modes, nodes, quad_weights, chaos_index, bonds, face_map
):
    parts = lax.axis_size("smp")
    layers = lax.axis_size("sub")
    d = Sizes(trial, chaos_index.shape[0], parts)
    rows, face = d.rows, d.face
    own = trial.reshape(d.subs * d.here, d.width)
    others = [
        lax.ppermute(own, "smp", [(i, (i + shift) % parts) for i in range(parts)])
        for shift in range(1, parts)
    ]
    pairs = [(i, i ^ 1) for i in range(layers)]
    partner = {i: i + 1 if i % 2 else i - 1 for i in range(1, layers - 1)}
    across = [
        (i * parts + s, partner[i] * parts + s if i in partner else i * parts + (s + 1) % parts)
        for i in range(layers)
        for s in range(parts)
    ]

    def exchange(on_chip, off_chip):
        far = lax.ppermute(off_chip, ("sub", "smp"), across)
        return lax.ppermute(on_chip, "sub", pairs), far

    def run(body, *args, **options):
        return call(functools.partial(body, d), *args, **options)

    product = shaped((d.subs * d.here, d.width))
    lam, mu = run(
        load,
        [shaped(stiff_lam.shape, BF16), shaped(stiff_mu.shape, BF16)],
        [HBM] * 2,
        [stiff_lam, stiff_mu],
        scratch=[pltpu.SemaphoreType.DMA((2,))],
        grant=51 << 20,
    )
    mod, maps, own_lam, own_mu = run(
        prepare,
        [shaped((2, rows, 128)), shaped((2, d.subs, 8, face), jnp.int32), product, product],
        [VMEM] * 6,
        [
            own, lam, mu,
            log_modes.transpose(0, 1, 3, 2, 4), nodes, face_map.transpose(0, 2, 1, 3),
        ],
    )
    field, on_chip, off_chip = run(
        first_z,
        [shaped((rows, 2 * face)), shaped((rows, face)), shaped((rows, face))],
        [VMEM] * (parts + 5),
        [*others, lam, mu, mod, maps, own_lam, own_mu],
    )
    near, far = exchange(on_chip, off_chip)
    basis, masks = run(
        tables,
        [shaped((d.terms, d.samples), BF16), shaped((6, d.subs, 8, 128))],
        [VMEM] * 4,
        [nodes, quad_weights.reshape(1, -1), chaos_index.T, bonds.transpose(0, 3, 2, 1)],
    )
    jumps_plane, part_lam, part_mu = run(
        first_plane,
        [shaped((rows, d.plane), BF16), shaped((rows, 2 * face)), shaped((rows, 2 * face))],
        [VMEM] * (parts + 5),
        [*others, lam, mu, mod, own_lam, own_mu, masks],
        scratch=[pltpu.VMEM((rows, d.plane), F32)],
    )
    jumps_z, field, on_chip, off_chip = run(
        second_z,
        [
            shaped((rows, 2 * face), BF16),
            shaped((rows, 2 * face)),
            shaped((rows, face)),
            shaped((rows, face)),
        ],
        [VMEM] * 10,
        [field, far, near, maps, masks, mod, lam, mu, part_lam, part_mu],
        scratch=[pltpu.VMEM((rows, 2 * face), F32)],
    )
    near, far = exchange(on_chip, off_chip)
    (plane,) = run(
        second_plane,
        [shaped((rows, d.plane), BF16)],
        [VMEM] * 6,
        [jumps_plane, jumps_z, lam, mu, mod, masks],
    )
    last = [field, far, near, maps, masks, plane]
    held = pltpu.VMEM((rows, 2 * face), F32)
    result = [shaped((1, d.height, d.breadth, d.terms, d.share), BF16)]

    def buffers(width):
        return [
            pltpu.VMEM((d.height, d.breadth, d.terms, width), BF16),
            pltpu.SemaphoreType.DMA(()),
        ]

    if d.share == 3 * face:
        (early,) = run(
            project_early,
            result,
            [VMEM] * 2,
            [plane, basis],
            out_specs=[HBM],
            scratch=buffers(face),
        )
        (out,) = run(
            project_late,
            result,
            [VMEM] * 7 + [HBM],
            [*last, basis, early],
            out_specs=[HBM],
            scratch=[held, pltpu.VMEM((rows, d.width), BF16)] + buffers(2 * face),
            aliases={7: 0},
        )
    else:
        (jumps,) = run(last_z, [shaped((rows, d.width), BF16)], [VMEM] * 6, last, scratch=[held])
        start = lax.axis_index("smp") * d.share
        jumps = lax.dynamic_slice_in_dim(jumps, start, d.share, 1)
        (out,) = run(
            project_share, result, [VMEM] * 2, [jumps, basis], out_specs=[HBM], scratch=buffers(d.share)
        )
    return jnp.swapaxes(out, -1, -2)


def solution(mesh):
    return jax.shard_map(
        per_device,
        mesh=mesh,
        in_specs=(
            P("sub", None, None, "smp", None),
            P(),
            P(),
            P(None, "sub", None, None, None),
            P(),
            P(),
            P(),
            P(),
            P("sub", None, None, None),
        ),
        out_specs=P("sub", None, None, "smp", None),
        check_vma=False,
    )
```

```python
import functools

import jax
import jax.numpy as jnp
from jax import lax
from jax.experimental import pallas as pl
from jax.experimental.pallas import tpu as pltpu
from jax.sharding import PartitionSpec as P

F32 = jnp.float32
BF16 = jnp.bfloat16
VMEM = pl.BlockSpec(memory_space=pltpu.VMEM)
CHUNK = 144
HBM = pl.BlockSpec(memory_space=pltpu.HBM)


def shaped(shape, dtype=F32):
    return jax.ShapeDtypeStruct(shape, dtype)


def call(body, outs, specs, args, flops=0, scratch=(), out_specs=None, grant=24 << 20, aliases=None):
    return pl.pallas_call(
        body,
        out_shape=outs,
        in_specs=specs,
        out_specs=[VMEM] * len(outs) if out_specs is None else out_specs,
        scratch_shapes=list(scratch),
        input_output_aliases=aliases or {},
        cost_estimate=pl.CostEstimate(flops=flops, bytes_accessed=0, transcendentals=0),
        compiler_params=pltpu.CompilerParams(vmem_limit_bytes=grant),
    )(*args)


def dot(a, b):
    return jnp.dot(a, b, preferred_element_type=F32)


def wide(column, width):
    return jnp.concatenate([column] * (width // 128), axis=1)


class Sizes:
    def __init__(self, trial, basis_size, parts):
        _, self.height, self.breadth, self.here, self.width = trial.shape
        self.face = self.width // 6
        self.subs = self.height * self.breadth
        self.parts = parts
        self.samples = self.here * parts
        self.rows = self.subs * self.samples
        self.plane = 4 * self.face
        self.terms = basis_size
        self.share = self.width // parts

    def own(self, n, part):
        return pl.ds(pl.multiple_of(n * self.samples + part * self.here, 8), self.here)

    def block(self, n):
        return slice(n * self.samples, (n + 1) * self.samples)

    def group(self, n):
        return slice(n * self.here, (n + 1) * self.here)


def load(d, lam, mu, lam_here, mu_here, sems):
    copies = [
        pltpu.make_async_copy(lam, lam_here, sems.at[0]),
        pltpu.make_async_copy(mu, mu_here, sems.at[1]),
    ]
    for copy in copies:
        copy.start()
    for copy in copies:
        copy.wait()


def prepare(d, trial, lam, mu, modes, nodes, faces, mod, maps, first, second):
    first[...] = dot(trial[...], lam[...])
    second[...] = dot(trial[...], mu[...])
    points = nodes[...]
    for c in range(2):
        for n in range(d.subs):
            row = modes[c, 0, n % d.breadth, pl.ds(n // d.breadth, 1), :]
            total = jnp.exp(jnp.sum(points * row, axis=1, keepdims=True))
            mod[c, d.block(n), :] = jnp.broadcast_to(total, (d.samples, 128))
    target = lax.broadcasted_iota(jnp.int32, (d.face, d.face), 0)
    source = lax.broadcasted_iota(jnp.int32, (8, d.face), 1).astype(F32).astype(BF16)
    for n in range(d.subs):
        row = faces[0, n % d.breadth, pl.ds(n // d.breadth, 1), :]
        hit = jnp.where(row == target, 1.0, 0.0).astype(BF16)
        back = lax.dot_general(
            source, hit, (((1,), (1,)), ((), ())), preferred_element_type=F32
        )
        maps[0, n] = jnp.broadcast_to(row, (8, d.face))
        maps[1, n] = back.astype(jnp.int32)


def tables(d, nodes, weights, chaos, bonds, basis, masks):
    points = nodes[...]
    layer = lax.axis_index("sub")
    lane = lax.broadcasted_iota(jnp.int32, (d.height, bonds.shape[-1]), 1)

    def at(axis, x, z):
        picked = jnp.where(lane == z, bonds[axis, x].astype(F32), 0.0)
        return jnp.sum(picked, axis=1, keepdims=True)

    along = [[at(axis, x, layer) for x in range(d.breadth)] for axis in range(3)]
    under = [at(2, x, layer - 1) for x in range(d.breadth)]
    for n in range(d.subs):
        y, x = divmod(n, d.breadth)
        columns = [
            (along[0][(x - 1) % d.breadth], y),
            (along[0][x], y),
            (along[1][x], (y - 1) % d.height),
            (along[1][x], y),
            (under[x], y),
            (along[2][x], y),
        ]
        for which, (column, at_y) in enumerate(columns):
            masks[which, n] = jnp.broadcast_to(column[at_y : at_y + 1], (8, 128))
    one = jnp.sqrt(3.0) * points
    two = jnp.sqrt(5.0) * (1.5 * points * points - 0.5)
    three = jnp.sqrt(7.0) * (2.5 * points * points * points - 1.5 * points)
    total = jnp.ones((d.samples, d.terms), F32)
    for k in range(points.shape[1]):
        c = chaos[k : k + 1, :]
        high = jnp.where(c == 3, three[:, k : k + 1], two[:, k : k + 1])
        low = jnp.where(c == 1, one[:, k : k + 1], 1.0)
        total = total * jnp.where(c >= 2, high, low)
    square = (d.samples, d.samples)
    diagonal = lax.broadcasted_iota(jnp.int32, square, 0) == lax.broadcasted_iota(
        jnp.int32, square, 1
    )
    column = jnp.sum(jnp.where(diagonal, weights[...], 0.0), axis=1, keepdims=True)
    basis[...] = (column * total).T.astype(BF16)


def payloads(d, low, high, maps, on_chip, off_chip):
    even = lax.rem(lax.axis_index("sub"), 2) == 0
    for n in range(d.subs):
        back = maps[1, n]
        for start in range(n * d.samples, (n + 1) * d.samples, 8):
            rows = slice(start, start + 8)
            minus = low[rows]
            pushed = jnp.take_along_axis(high[rows], back, axis=1, mode="promise_in_bounds")
            on_chip[rows, :] = jnp.where(even, pushed, minus)
            off_chip[rows, :] = jnp.where(even, minus, pushed)


def part_of(d, shift):
    here = lax.axis_index("smp")
    return lax.rem(here - shift + d.parts, d.parts)


def combine(d, mod, part, first, second, field):
    width = field.shape[1]
    for n in range(d.subs):
        own = d.own(n, part)
        field[own, :] = (
            wide(mod[0, own, :], width) * first[d.group(n), :]
            + wide(mod[1, own, :], width) * second[d.group(n), :]
        )


def first_z(d, *refs):
    others = refs[: d.parts - 1]
    lam, mu, mod, maps, own_lam, own_mu, field, on_chip, off_chip = refs[d.parts - 1 :]
    at = slice(d.plane, d.width)
    combine(d, mod, lax.axis_index("smp"), own_lam.at[:, at], own_mu.at[:, at], field)
    for shift, other in enumerate(others, 1):
        rows = other[...]
        combine(d, mod, part_of(d, shift), dot(rows, lam[:, at]), dot(rows, mu[:, at]), field)
    payloads(d, field[:, : d.face], field[:, d.face :], maps, on_chip, off_chip)


def plane_jumps(d, field, masks, out):
    def mask(which, n):
        return jnp.concatenate([masks[which, n]] * (d.samples // 8), axis=0)

    for n in range(d.subs):
        y, x = divmod(n, d.breadth)
        left = y * d.breadth + (x - 1) % d.breadth
        right = y * d.breadth + (x + 1) % d.breadth
        front = (y - 1) % d.height * d.breadth + x
        behind = (y + 1) % d.height * d.breadth + x

        def face(which, m):
            return field[d.block(m), which * d.face : (which + 1) * d.face]

        out(0, n, mask(0, n) * (face(0, n) - face(1, left)))
        out(1, n, mask(1, n) * (face(1, n) - face(0, right)))
        out(2, n, mask(2, n) * (face(2, n) - face(3, front)))
        out(3, n, mask(3, n) * (face(3, n) - face(2, behind)))


def z_jumps(d, field, from_off, from_chip, maps, masks, out):
    layer = lax.axis_index("sub")
    even = lax.rem(layer, 2) == 0
    inside = jnp.logical_and(layer > 0, layer < lax.axis_size("sub") - 1)
    for n in range(d.subs):
        for start in range(n * d.samples, (n + 1) * d.samples, 8):
            rows = slice(start, start + 8)
            near, far = from_chip[rows, :], jnp.where(inside, from_off[rows, :], 0.0)
            above = jnp.where(even, near, far)
            below = jnp.where(even, far, near)
            matched = jnp.take_along_axis(above, maps[0, n], axis=1, mode="promise_in_bounds")
            out(0, rows, masks[4, n] * (field[rows, : d.face] - below))
            out(1, rows, masks[5, n] * (field[rows, d.face :] - matched))


def first_plane(d, *refs):
    others = refs[: d.parts - 1]
    lam, mu, mod, own_lam, own_mu, masks, jumps, part_lam, part_mu, field = refs[d.parts - 1 :]
    at = slice(0, d.plane)
    combine(d, mod, lax.axis_index("smp"), own_lam.at[:, at], own_mu.at[:, at], field)
    for shift, other in enumerate(others, 1):
        rows = other[...]
        combine(d, mod, part_of(d, shift), dot(rows, lam[:, at]), dot(rows, mu[:, at]), field)

    def put(which, n, value):
        jumps[d.block(n), which * d.face : (which + 1) * d.face] = value.astype(BF16)

    plane_jumps(d, field, masks, put)
    part_lam[...] = dot(jumps[...], lam[: d.plane, d.plane :])
    part_mu[...] = dot(jumps[...], mu[: d.plane, d.plane :])


def second_z(
    d, field, from_off, from_chip, maps, masks, mod, lam, mu, part_lam, part_mu,
    jumps, result, on_chip, off_chip, held,
):
    def put(which, rows, value):
        held[rows, which * d.face : (which + 1) * d.face] = value

    z_jumps(d, field, from_off, from_chip, maps, masks, put)
    rounded = held[...].astype(BF16)
    jumps[...] = rounded
    one = part_lam[...] + dot(rounded, lam[d.plane :, d.plane :])
    two = part_mu[...] + dot(rounded, mu[d.plane :, d.plane :])
    result[...] = wide(mod[0], 2 * d.face) * one + wide(mod[1], 2 * d.face) * two
    payloads(d, result[:, : d.face], result[:, d.face :], maps, on_chip, off_chip)


def second_plane(d, plane, zed, lam, mu, mod, masks, jumps):
    one = dot(plane[...], lam[: d.plane, : d.plane]) + dot(zed[...], lam[d.plane :, : d.plane])
    two = dot(plane[...], mu[: d.plane, : d.plane]) + dot(zed[...], mu[d.plane :, : d.plane])
    field = wide(mod[0], d.plane) * one + wide(mod[1], d.plane) * two

    def put(which, n, value):
        jumps[d.block(n), which * d.face : (which + 1) * d.face] = value.astype(BF16)

    plane_jumps(d, field, masks, put)


def last_z(d, field, from_off, from_chip, maps, masks, plane, jumps, held):
    def put(which, rows, value):
        held[rows, which * d.face : (which + 1) * d.face] = value

    z_jumps(d, field, from_off, from_chip, maps, masks, put)
    jumps[:, : d.plane] = plane[...]
    jumps[:, d.plane :] = held[...].astype(BF16)


def project_rows(d, picks, lanes, basis, out, rows_out, sem):
    width = lanes.stop - lanes.start
    group = max(g for g in (1, 2, 3, 6) if d.subs % g == 0 and g * width <= 768)
    for n in range(0, d.subs, group):
        right = picks[n : n + group]
        right = right[0] if group == 1 else jnp.concatenate(right, axis=1)
        for start in range(0, d.terms, CHUNK):
            rows = slice(start, min(start + CHUNK, d.terms))
            value = dot(basis[rows, :], right)
            for m in range(group):
                y, x = divmod(n + m, d.breadth)
                rows_out[y, x, rows, :] = value[:, m * width : (m + 1) * width].astype(BF16)
                pltpu.make_async_copy(
                    rows_out.at[y, x, rows, :], out.at[0, y, x, rows, lanes], sem
                ).start()
    pltpu.make_async_copy(rows_out, out.at[0, :, :, :, lanes], sem).wait()


def project_early(d, plane, basis, out, rows_out, sem):
    start = pl.multiple_of(lax.axis_index("smp") * d.share, 128)
    picks = [plane[d.block(n), pl.ds(start, d.face)] for n in range(d.subs)]
    project_rows(d, picks, slice(0, d.face), basis, out, rows_out, sem)


def project_late(
    d, field, from_off, from_chip, maps, masks, plane, basis, early, out, held, jumps, rows_out, sem
):
    last_z(d, field, from_off, from_chip, maps, masks, plane, jumps, held)
    width = d.share - d.face
    start = pl.multiple_of(lax.axis_index("smp") * d.share + d.face, 128)
    picks = [jumps[d.block(n), pl.ds(start, width)] for n in range(d.subs)]
    project_rows(d, picks, slice(d.face, d.share), basis, out, rows_out, sem)


def project_share(d, jumps, basis, out, rows_out, sem):
    picks = [jumps[d.block(n), :] for n in range(d.subs)]
    project_rows(d, picks, slice(0, d.share), basis, out, rows_out, sem)


def per_device(
    trial, stiff_lam, stiff_mu, log_modes, nodes, quad_weights, chaos_index, bonds, face_map
):
    parts = lax.axis_size("smp")
    layers = lax.axis_size("sub")
    d = Sizes(trial, chaos_index.shape[0], parts)
    rows, face = d.rows, d.face
    own = trial.reshape(d.subs * d.here, d.width)
    others = [
        lax.ppermute(own, "smp", [(i, (i + shift) % parts) for i in range(parts)])
        for shift in range(1, parts)
    ]
    pairs = [(i, i ^ 1) for i in range(layers)]
    partner = {i: i + 1 if i % 2 else i - 1 for i in range(1, layers - 1)}
    across = [
        (i * parts + s, partner[i] * parts + s if i in partner else i * parts + (s + 1) % parts)
        for i in range(layers)
        for s in range(parts)
    ]

    second = across
    if parts == 2 and layers >= 4:
        top = layers - 1
        steps = {(i, 1): (partner[i], 1) for i in partner}
        steps.update({(i, 0): (i ^ 1, 0) for i in range(2, layers - 2)})
        steps.update({(0, 1): (1, 0), (1, 0): (0, 0), (0, 0): (0, 1)})
        steps.update({(top, 1): (top - 1, 0), (top - 1, 0): (top, 0), (top, 0): (top, 1)})
        second = sorted((i * 2 + s, j * 2 + t) for (i, s), (j, t) in steps.items())

    def exchange(on_chip, off_chip, across):
        far = lax.ppermute(off_chip, ("sub", "smp"), across)
        return lax.ppermute(on_chip, "sub", pairs), far

    def run(body, *args, **options):
        return call(functools.partial(body, d), *args, **options)

    product = shaped((d.subs * d.here, d.width))
    lam, mu = run(
        load,
        [shaped(stiff_lam.shape, BF16), shaped(stiff_mu.shape, BF16)],
        [HBM] * 2,
        [stiff_lam, stiff_mu],
        scratch=[pltpu.SemaphoreType.DMA((2,))],
        grant=51 << 20,
    )
    mod, maps, own_lam, own_mu = run(
        prepare,
        [shaped((2, rows, 128)), shaped((2, d.subs, 8, face), jnp.int32), product, product],
        [VMEM] * 6,
        [
            own, lam, mu,
            log_modes.transpose(0, 1, 3, 2, 4), nodes, face_map.transpose(0, 2, 1, 3),
        ],
    )
    field, on_chip, off_chip = run(
        first_z,
        [shaped((rows, 2 * face)), shaped((rows, face)), shaped((rows, face))],
        [VMEM] * (parts + 5),
        [*others, lam, mu, mod, maps, own_lam, own_mu],
    )
    near, far = exchange(on_chip, off_chip, across)
    basis, masks = run(
        tables,
        [shaped((d.terms, d.samples), BF16), shaped((6, d.subs, 8, 128))],
        [VMEM] * 4,
        [nodes, quad_weights.reshape(1, -1), chaos_index.T, bonds.transpose(0, 3, 2, 1)],
    )
    jumps_plane, part_lam, part_mu = run(
        first_plane,
        [shaped((rows, d.plane), BF16), shaped((rows, 2 * face)), shaped((rows, 2 * face))],
        [VMEM] * (parts + 5),
        [*others, lam, mu, mod, own_lam, own_mu, masks],
        scratch=[pltpu.VMEM((rows, d.plane), F32)],
    )
    jumps_z, field, on_chip, off_chip = run(
        second_z,
        [
            shaped((rows, 2 * face), BF16),
            shaped((rows, 2 * face)),
            shaped((rows, face)),
            shaped((rows, face)),
        ],
        [VMEM] * 10,
        [field, far, near, maps, masks, mod, lam, mu, part_lam, part_mu],
        scratch=[pltpu.VMEM((rows, 2 * face), F32)],
    )
    near, far = exchange(on_chip, off_chip, second)
    (plane,) = run(
        second_plane,
        [shaped((rows, d.plane), BF16)],
        [VMEM] * 6,
        [jumps_plane, jumps_z, lam, mu, mod, masks],
    )
    last = [field, far, near, maps, masks, plane]
    held = pltpu.VMEM((rows, 2 * face), F32)
    result = [shaped((1, d.height, d.breadth, d.terms, d.share), BF16)]

    def buffers(width):
        return [
            pltpu.VMEM((d.height, d.breadth, d.terms, width), BF16),
            pltpu.SemaphoreType.DMA(()),
        ]

    if d.share == 3 * face:
        (early,) = run(
            project_early,
            result,
            [VMEM] * 2,
            [plane, basis],
            out_specs=[HBM],
            scratch=buffers(face),
        )
        (out,) = run(
            project_late,
            result,
            [VMEM] * 7 + [HBM],
            [*last, basis, early],
            out_specs=[HBM],
            scratch=[held, pltpu.VMEM((rows, d.width), BF16)] + buffers(2 * face),
            aliases={7: 0},
        )
    else:
        (jumps,) = run(last_z, [shaped((rows, d.width), BF16)], [VMEM] * 6, last, scratch=[held])
        start = lax.axis_index("smp") * d.share
        jumps = lax.dynamic_slice_in_dim(jumps, start, d.share, 1)
        (out,) = run(
            project_share, result, [VMEM] * 2, [jumps, basis], out_specs=[HBM], scratch=buffers(d.share)
        )
    return jnp.swapaxes(out, -1, -2)


def solution(mesh):
    return jax.shard_map(
        per_device,
        mesh=mesh,
        in_specs=(
            P("sub", None, None, "smp", None),
            P(),
            P(),
            P(None, "sub", None, None, None),
            P(),
            P(),
            P(),
            P(),
            P("sub", None, None, None),
        ),
        out_specs=P("sub", None, None, "smp", None),
        check_vma=False,
    )
```

```python
import functools

import jax
import jax.numpy as jnp
from jax import lax
from jax.experimental import pallas as pl
from jax.experimental.pallas import tpu as pltpu
from jax.sharding import PartitionSpec as P

F32 = jnp.float32
BF16 = jnp.bfloat16
VMEM = pl.BlockSpec(memory_space=pltpu.VMEM)
CHUNK = 144
PAD = 8
HBM = pl.BlockSpec(memory_space=pltpu.HBM)


def shaped(shape, dtype=F32):
    return jax.ShapeDtypeStruct(shape, dtype)


def call(body, outs, specs, args, flops=0, scratch=(), out_specs=None, grant=24 << 20, aliases=None):
    return pl.pallas_call(
        body,
        out_shape=outs,
        in_specs=specs,
        out_specs=[VMEM] * len(outs) if out_specs is None else out_specs,
        scratch_shapes=list(scratch),
        input_output_aliases=aliases or {},
        cost_estimate=pl.CostEstimate(flops=flops, bytes_accessed=0, transcendentals=0),
        compiler_params=pltpu.CompilerParams(vmem_limit_bytes=grant),
    )(*args)


def dot(a, b):
    return jnp.dot(a, b, preferred_element_type=F32)


def wide(column, width):
    return jnp.concatenate([column] * (width // 128), axis=1)


class Sizes:
    def __init__(self, trial, basis_size, parts):
        _, self.height, self.breadth, self.here, self.width = trial.shape
        self.face = self.width // 6
        self.subs = self.height * self.breadth
        self.parts = parts
        self.samples = self.here * parts
        self.rows = self.subs * self.samples
        self.plane = 4 * self.face
        self.terms = basis_size
        self.share = self.width // parts

    def own(self, n, part):
        return pl.ds(pl.multiple_of(n * self.samples + part * self.here, 8), self.here)

    def block(self, n):
        return slice(n * self.samples, (n + 1) * self.samples)

    def group(self, n):
        return slice(n * self.here, (n + 1) * self.here)


def load(d, lam, mu, lam_here, mu_here, sems):
    copies = [
        pltpu.make_async_copy(lam, lam_here, sems.at[0]),
        pltpu.make_async_copy(mu, mu_here, sems.at[1]),
    ]
    for copy in copies:
        copy.start()
    for copy in copies:
        copy.wait()


def prepare(d, trial, lam, mu, modes, nodes, faces, mod, maps, first, second):
    first[...] = dot(trial[...], lam[...])
    second[...] = dot(trial[...], mu[...])
    points = nodes[...]
    for c in range(2):
        for n in range(d.subs):
            row = modes[c, 0, n % d.breadth, pl.ds(n // d.breadth, 1), :]
            total = jnp.exp(jnp.sum(points * row, axis=1, keepdims=True))
            mod[c, d.block(n), :] = jnp.broadcast_to(total, (d.samples, 128))
    target = lax.broadcasted_iota(jnp.int32, (d.face, d.face), 0)
    source = lax.broadcasted_iota(jnp.int32, (8, d.face), 1).astype(F32).astype(BF16)
    for n in range(d.subs):
        row = faces[0, n % d.breadth, pl.ds(n // d.breadth, 1), :]
        hit = jnp.where(row == target, 1.0, 0.0).astype(BF16)
        back = lax.dot_general(
            source, hit, (((1,), (1,)), ((), ())), preferred_element_type=F32
        )
        maps[0, n] = jnp.broadcast_to(row, (8, d.face))
        maps[1, n] = back.astype(jnp.int32)


def tables(d, nodes, weights, chaos, bonds, basis, masks):
    points = nodes[...]
    layer = lax.axis_index("sub")
    lane = lax.broadcasted_iota(jnp.int32, (d.height, bonds.shape[-1]), 1)

    def at(axis, x, z):
        picked = jnp.where(lane == z, bonds[axis, x].astype(F32), 0.0)
        return jnp.sum(picked, axis=1, keepdims=True)

    along = [[at(axis, x, layer) for x in range(d.breadth)] for axis in range(3)]
    under = [at(2, x, layer - 1) for x in range(d.breadth)]
    for n in range(d.subs):
        y, x = divmod(n, d.breadth)
        columns = [
            (along[0][(x - 1) % d.breadth], y),
            (along[0][x], y),
            (along[1][x], (y - 1) % d.height),
            (along[1][x], y),
            (under[x], y),
            (along[2][x], y),
        ]
        for which, (column, at_y) in enumerate(columns):
            masks[which, n] = jnp.broadcast_to(column[at_y : at_y + 1], (8, 128))
    one = jnp.sqrt(3.0) * points
    two = jnp.sqrt(5.0) * (1.5 * points * points - 0.5)
    three = jnp.sqrt(7.0) * (2.5 * points * points * points - 1.5 * points)
    total = jnp.ones((d.samples, d.terms), F32)
    for k in range(points.shape[1]):
        c = chaos[k : k + 1, :]
        high = jnp.where(c == 3, three[:, k : k + 1], two[:, k : k + 1])
        low = jnp.where(c == 1, one[:, k : k + 1], 1.0)
        total = total * jnp.where(c >= 2, high, low)
    square = (d.samples, d.samples)
    diagonal = lax.broadcasted_iota(jnp.int32, square, 0) == lax.broadcasted_iota(
        jnp.int32, square, 1
    )
    column = jnp.sum(jnp.where(diagonal, weights[...], 0.0), axis=1, keepdims=True)
    basis[...] = (column * total).T.astype(BF16)


def payloads(d, low, high, maps, on_chip, off_chip):
    even = lax.rem(lax.axis_index("sub"), 2) == 0
    for n in range(d.subs):
        back = maps[1, n]
        for start in range(n * d.samples, (n + 1) * d.samples, 8):
            rows = slice(start, start + 8)
            minus = low[rows]
            pushed = jnp.take_along_axis(high[rows], back, axis=1, mode="promise_in_bounds")
            on_chip[rows, :] = jnp.where(even, pushed, minus)
            off_chip[rows, :] = jnp.where(even, minus, pushed)


def part_of(d, shift):
    here = lax.axis_index("smp")
    return lax.rem(here - shift + d.parts, d.parts)


def combine(d, mod, part, first, second, field):
    width = field.shape[1]
    for n in range(d.subs):
        own = d.own(n, part)
        field[own, :] = (
            wide(mod[0, own, :], width) * first[d.group(n), :]
            + wide(mod[1, own, :], width) * second[d.group(n), :]
        )


def first_z(d, *refs):
    others = refs[: d.parts - 1]
    lam, mu, mod, maps, own_lam, own_mu, field, on_chip, off_chip = refs[d.parts - 1 :]
    at = slice(d.plane, d.width)
    combine(d, mod, lax.axis_index("smp"), own_lam.at[:, at], own_mu.at[:, at], field)
    for shift, other in enumerate(others, 1):
        rows = other[...]
        combine(d, mod, part_of(d, shift), dot(rows, lam[:, at]), dot(rows, mu[:, at]), field)
    payloads(d, field[:, : d.face], field[:, d.face :], maps, on_chip, off_chip)


def plane_jumps(d, field, masks, out):
    def mask(which, n):
        return jnp.concatenate([masks[which, n]] * (d.samples // 8), axis=0)

    for n in range(d.subs):
        y, x = divmod(n, d.breadth)
        left = y * d.breadth + (x - 1) % d.breadth
        right = y * d.breadth + (x + 1) % d.breadth
        front = (y - 1) % d.height * d.breadth + x
        behind = (y + 1) % d.height * d.breadth + x

        def face(which, m):
            return field[d.block(m), which * d.face : (which + 1) * d.face]

        out(0, n, mask(0, n) * (face(0, n) - face(1, left)))
        out(1, n, mask(1, n) * (face(1, n) - face(0, right)))
        out(2, n, mask(2, n) * (face(2, n) - face(3, front)))
        out(3, n, mask(3, n) * (face(3, n) - face(2, behind)))


def z_jumps(d, field, from_off, from_chip, maps, masks, out):
    layer = lax.axis_index("sub")
    even = lax.rem(layer, 2) == 0
    inside = jnp.logical_and(layer > 0, layer < lax.axis_size("sub") - 1)
    for n in range(d.subs):
        for start in range(n * d.samples, (n + 1) * d.samples, 8):
            rows = slice(start, start + 8)
            near, far = from_chip[rows, :], jnp.where(inside, from_off[rows, :], 0.0)
            above = jnp.where(even, near, far)
            below = jnp.where(even, far, near)
            matched = jnp.take_along_axis(above, maps[0, n], axis=1, mode="promise_in_bounds")
            out(0, rows, masks[4, n] * (field[rows, : d.face] - below))
            out(1, rows, masks[5, n] * (field[rows, d.face :] - matched))


def side_jumps(d, near, field, taken, maps, masks, out):
    layer = lax.axis_index("sub")
    even = lax.rem(layer, 2) == 0
    up = even if near else jnp.logical_not(even)
    inside = jnp.logical_and(layer > 0, layer < lax.axis_size("sub") - 1)
    for n in range(d.subs):
        for start in range(n * d.samples, (n + 1) * d.samples, 8):
            rows = slice(start, start + 8)
            other = taken[rows, :] if near else jnp.where(inside, taken[rows, :], 0.0)
            matched = jnp.take_along_axis(other, maps[0, n], axis=1, mode="promise_in_bounds")
            above = masks[5, n] * (field[rows, d.face :] - matched)
            below = masks[4, n] * (field[rows, : d.face] - other)
            out[rows, :] = jnp.where(up, above, below)
    return pl.ds(pl.multiple_of(jnp.where(up, 2, 1) * d.face, 128), d.face)


def first_plane(d, *refs):
    others = refs[: d.parts - 1]
    lam, mu, mod, own_lam, own_mu, masks, jumps, part_lam, part_mu, field = refs[d.parts - 1 :]
    at = slice(0, d.plane)
    combine(d, mod, lax.axis_index("smp"), own_lam.at[:, at], own_mu.at[:, at], field)
    for shift, other in enumerate(others, 1):
        rows = other[...]
        combine(d, mod, part_of(d, shift), dot(rows, lam[:, at]), dot(rows, mu[:, at]), field)

    def put(which, n, value):
        jumps[d.block(n), which * d.face : (which + 1) * d.face] = value.astype(BF16)

    plane_jumps(d, field, masks, put)
    part_lam[...] = dot(jumps[...], lam[: d.plane, d.plane :])
    part_mu[...] = dot(jumps[...], mu[: d.plane, d.plane :])


def second_z(
    d, field, from_off, from_chip, maps, masks, mod, lam, mu, part_lam, part_mu,
    jumps, result, on_chip, off_chip, held,
):
    def put(which, rows, value):
        held[rows, which * d.face : (which + 1) * d.face] = value

    z_jumps(d, field, from_off, from_chip, maps, masks, put)
    rounded = held[...].astype(BF16)
    jumps[...] = rounded
    one = part_lam[...] + dot(rounded, lam[d.plane :, d.plane :])
    two = part_mu[...] + dot(rounded, mu[d.plane :, d.plane :])
    result[...] = wide(mod[0], 2 * d.face) * one + wide(mod[1], 2 * d.face) * two
    payloads(d, result[:, : d.face], result[:, d.face :], maps, on_chip, off_chip)
    off_chip[d.rows :, :] = jnp.zeros((PAD, d.face), F32)


def second_plane(d, plane, zed, lam, mu, mod, masks, jumps):
    one = dot(plane[...], lam[: d.plane, : d.plane]) + dot(zed[...], lam[d.plane :, : d.plane])
    two = dot(plane[...], mu[: d.plane, : d.plane]) + dot(zed[...], mu[d.plane :, : d.plane])
    field = wide(mod[0], d.plane) * one + wide(mod[1], d.plane) * two

    def put(which, n, value):
        jumps[d.block(n), which * d.face : (which + 1) * d.face] = value.astype(BF16)

    plane_jumps(d, field, masks, put)


def last_z(d, field, from_off, from_chip, maps, masks, plane, jumps, held):
    def put(which, rows, value):
        held[rows, which * d.face : (which + 1) * d.face] = value

    z_jumps(d, field, from_off, from_chip, maps, masks, put)
    jumps[:, : d.plane] = plane[...]
    jumps[:, d.plane :] = held[...].astype(BF16)


def project_rows(d, picks, lanes, basis, out, rows_out, sem):
    width = rows_out.shape[-1]
    group = max(g for g in (1, 2, 3, 6) if d.subs % g == 0 and g * width <= 768)
    for n in range(0, d.subs, group):
        right = picks[n : n + group]
        right = right[0] if group == 1 else jnp.concatenate(right, axis=1)
        for start in range(0, d.terms, CHUNK):
            rows = slice(start, min(start + CHUNK, d.terms))
            value = dot(basis[rows, :], right)
            for m in range(group):
                y, x = divmod(n + m, d.breadth)
                rows_out[y, x, rows, :] = value[:, m * width : (m + 1) * width].astype(BF16)
                if out is not None:
                    pltpu.make_async_copy(
                        rows_out.at[y, x, rows, :], out.at[0, y, x, rows, lanes], sem
                    ).start()
    if out is not None:
        return pltpu.make_async_copy(rows_out, out.at[0, :, :, :, lanes], sem)


def project_plane(d, plane, basis, out, plane_out, all_out, sem):
    part = lax.axis_index("smp")

    @pl.when(part == 0)
    def _():
        picks = [plane[d.block(n), : d.share] for n in range(d.subs)]
        project_rows(d, picks, slice(0, d.share), basis, out, all_out, sem).wait()

    @pl.when(part == 1)
    def _():
        picks = [plane[d.block(n), d.share :] for n in range(d.subs)]
        project_rows(d, picks, None, basis, None, plane_out, None)


def project_near(d, field, near, maps, masks, basis, plane_out, early, out, held, near_out, sems):
    @pl.when(lax.axis_index("smp") == 1)
    def _():
        at = slice(0, d.face)
        first = pltpu.make_async_copy(plane_out, out.at[0, :, :, :, at], sems.at[0])
        first.start()
        lanes = side_jumps(d, True, field, near, maps, masks, held)
        picks = [held[d.block(n), :].astype(BF16) for n in range(d.subs)]
        second = project_rows(d, picks, lanes, basis, out, near_out, sems.at[1])
        first.wait()
        second.wait()


def project_late(d, field, far, maps, masks, basis, early, out, held, far_out, sem):
    @pl.when(lax.axis_index("smp") == 1)
    def _():
        lanes = side_jumps(d, False, field, far, maps, masks, held)
        picks = [held[d.block(n), :].astype(BF16) for n in range(d.subs)]
        project_rows(d, picks, lanes, basis, out, far_out, sem).wait()


def project_share(d, jumps, basis, out, rows_out, sem):
    picks = [jumps[d.block(n), :] for n in range(d.subs)]
    project_rows(d, picks, slice(0, d.share), basis, out, rows_out, sem).wait()


def per_device(
    trial, stiff_lam, stiff_mu, log_modes, nodes, quad_weights, chaos_index, bonds, face_map
):
    parts = lax.axis_size("smp")
    layers = lax.axis_size("sub")
    d = Sizes(trial, chaos_index.shape[0], parts)
    rows, face = d.rows, d.face
    own = trial.reshape(d.subs * d.here, d.width)
    others = [
        lax.ppermute(own, "smp", [(i, (i + shift) % parts) for i in range(parts)])
        for shift in range(1, parts)
    ]
    pairs = [(i, i ^ 1) for i in range(layers)]
    partner = {i: i + 1 if i % 2 else i - 1 for i in range(1, layers - 1)}
    across = [
        (i * parts + s, partner[i] * parts + s if i in partner else i * parts + (s + 1) % parts)
        for i in range(layers)
        for s in range(parts)
    ]

    second = across
    if parts == 2 and layers >= 4:
        top = layers - 1
        steps = {(i, 1): (partner[i], 1) for i in partner}
        steps.update({(i, 0): (i ^ 1, 0) for i in range(2, layers - 2)})
        steps.update({(0, 1): (1, 0), (1, 0): (0, 0), (0, 0): (0, 1)})
        steps.update({(top, 1): (top - 1, 0), (top - 1, 0): (top, 0), (top, 0): (top, 1)})
        second = sorted((i * 2 + s, j * 2 + t) for (i, s), (j, t) in steps.items())

    def exchange(on_chip, off_chip, across):
        far = lax.ppermute(off_chip, ("sub", "smp"), across)
        return lax.ppermute(on_chip, "sub", pairs), far

    def run(body, *args, **options):
        return call(functools.partial(body, d), *args, **options)

    product = shaped((d.subs * d.here, d.width))
    lam, mu = run(
        load,
        [shaped(stiff_lam.shape, BF16), shaped(stiff_mu.shape, BF16)],
        [HBM] * 2,
        [stiff_lam, stiff_mu],
        scratch=[pltpu.SemaphoreType.DMA((2,))],
        grant=51 << 20,
    )
    mod, maps, own_lam, own_mu = run(
        prepare,
        [shaped((2, rows, 128)), shaped((2, d.subs, 8, face), jnp.int32), product, product],
        [VMEM] * 6,
        [
            own, lam, mu,
            log_modes.transpose(0, 1, 3, 2, 4), nodes, face_map.transpose(0, 2, 1, 3),
        ],
    )
    field, on_chip, off_chip = run(
        first_z,
        [shaped((rows, 2 * face)), shaped((rows, face)), shaped((rows, face))],
        [VMEM] * (parts + 5),
        [*others, lam, mu, mod, maps, own_lam, own_mu],
    )
    near, far = exchange(on_chip, off_chip, across)
    basis, masks = run(
        tables,
        [shaped((d.terms, d.samples), BF16), shaped((6, d.subs, 8, 128))],
        [VMEM] * 4,
        [nodes, quad_weights.reshape(1, -1), chaos_index.T, bonds.transpose(0, 3, 2, 1)],
    )
    jumps_plane, part_lam, part_mu = run(
        first_plane,
        [shaped((rows, d.plane), BF16), shaped((rows, 2 * face)), shaped((rows, 2 * face))],
        [VMEM] * (parts + 5),
        [*others, lam, mu, mod, own_lam, own_mu, masks],
        scratch=[pltpu.VMEM((rows, d.plane), F32)],
    )
    jumps_z, field, on_chip, off_chip = run(
        second_z,
        [
            shaped((rows, 2 * face), BF16),
            shaped((rows, 2 * face)),
            shaped((rows, face)),
            shaped((rows + PAD, face)),
        ],
        [VMEM] * 10,
        [field, far, near, maps, masks, mod, lam, mu, part_lam, part_mu],
        scratch=[pltpu.VMEM((rows, 2 * face), F32)],
    )
    near, far = exchange(on_chip, off_chip, second)
    (plane,) = run(
        second_plane,
        [shaped((rows, d.plane), BF16)],
        [VMEM] * 6,
        [jumps_plane, jumps_z, lam, mu, mod, masks],
    )
    result = [shaped((1, d.height, d.breadth, d.terms, d.share), BF16)]

    def rows_out(width):
        return pltpu.VMEM((d.height, d.breadth, d.terms, width), BF16)

    if parts == 2:
        held = pltpu.VMEM((rows, face), F32)
        early, plane_out = run(
            project_plane,
            result + [shaped((d.height, d.breadth, d.terms, face), BF16)],
            [VMEM] * 2,
            [plane, basis],
            out_specs=[HBM, VMEM],
            scratch=[rows_out(d.share), pltpu.SemaphoreType.DMA(())],
        )
        (early,) = run(
            project_near,
            result,
            [VMEM] * 6 + [HBM],
            [field, near, maps, masks, basis, plane_out, early],
            out_specs=[HBM],
            scratch=[held, rows_out(face), pltpu.SemaphoreType.DMA((2,))],
            aliases={6: 0},
        )
        (out,) = run(
            project_late,
            result,
            [VMEM] * 5 + [HBM],
            [field, far, maps, masks, basis, early],
            out_specs=[HBM],
            scratch=[held, rows_out(face), pltpu.SemaphoreType.DMA(())],
            aliases={5: 0},
        )
    else:
        last = [field, far, near, maps, masks, plane]
        held = pltpu.VMEM((rows, 2 * face), F32)
        (jumps,) = run(last_z, [shaped((rows, d.width), BF16)], [VMEM] * 6, last, scratch=[held])
        start = lax.axis_index("smp") * d.share
        jumps = lax.dynamic_slice_in_dim(jumps, start, d.share, 1)
        (out,) = run(
            project_share,
            result,
            [VMEM] * 2,
            [jumps, basis],
            out_specs=[HBM],
            scratch=[rows_out(d.share), pltpu.SemaphoreType.DMA(())],
        )
    return jnp.swapaxes(out, -1, -2)


def solution(mesh):
    return jax.shard_map(
        per_device,
        mesh=mesh,
        in_specs=(
            P("sub", None, None, "smp", None),
            P(),
            P(),
            P(None, "sub", None, None, None),
            P(),
            P(),
            P(),
            P(),
            P("sub", None, None, None),
        ),
        out_specs=P("sub", None, None, "smp", None),
        check_vma=False,
    )
```

```python
import functools

import jax
import jax.numpy as jnp
from jax import lax
from jax.experimental import pallas as pl
from jax.experimental.pallas import tpu as pltpu
from jax.sharding import PartitionSpec as P

F32 = jnp.float32
BF16 = jnp.bfloat16
VMEM = pl.BlockSpec(memory_space=pltpu.VMEM)
CHUNK = 144
PAD = 8
HBM = pl.BlockSpec(memory_space=pltpu.HBM)


def shaped(shape, dtype=F32):
    return jax.ShapeDtypeStruct(shape, dtype)


def call(body, outs, specs, args, flops=0, scratch=(), out_specs=None, grant=24 << 20, aliases=None):
    return pl.pallas_call(
        body,
        out_shape=outs,
        in_specs=specs,
        out_specs=[VMEM] * len(outs) if out_specs is None else out_specs,
        scratch_shapes=list(scratch),
        input_output_aliases=aliases or {},
        cost_estimate=pl.CostEstimate(flops=flops, bytes_accessed=0, transcendentals=0),
        compiler_params=pltpu.CompilerParams(vmem_limit_bytes=grant),
    )(*args)


def dot(a, b):
    return jnp.dot(a, b, preferred_element_type=F32)


def wide(column, width):
    return jnp.concatenate([column] * (width // 128), axis=1)


class Sizes:
    def __init__(self, trial, basis_size, parts):
        _, self.height, self.breadth, self.here, self.width = trial.shape
        self.face = self.width // 6
        self.subs = self.height * self.breadth
        self.parts = parts
        self.samples = self.here * parts
        self.rows = self.subs * self.samples
        self.plane = 4 * self.face
        self.terms = basis_size
        self.share = self.width // parts

    def own(self, n, part):
        return pl.ds(pl.multiple_of(n * self.samples + part * self.here, 8), self.here)

    def block(self, n):
        return slice(n * self.samples, (n + 1) * self.samples)

    def group(self, n):
        return slice(n * self.here, (n + 1) * self.here)


def load(d, lam, mu, lam_here, mu_here, sems):
    copies = [
        pltpu.make_async_copy(lam, lam_here, sems.at[0]),
        pltpu.make_async_copy(mu, mu_here, sems.at[1]),
    ]
    for copy in copies:
        copy.start()
    for copy in copies:
        copy.wait()


def prepare(d, trial, lam, mu, modes, nodes, faces, mod, maps, first, second):
    first[...] = dot(trial[...], lam[...])
    second[...] = dot(trial[...], mu[...])
    points = nodes[...]
    for c in range(2):
        for n in range(d.subs):
            row = modes[c, 0, n % d.breadth, pl.ds(n // d.breadth, 1), :]
            total = jnp.exp(jnp.sum(points * row, axis=1, keepdims=True))
            mod[c, d.block(n), :] = jnp.broadcast_to(total, (d.samples, 128))
    target = lax.broadcasted_iota(jnp.int32, (d.face, d.face), 0)
    source = lax.broadcasted_iota(jnp.int32, (8, d.face), 1).astype(F32).astype(BF16)
    for n in range(d.subs):
        row = faces[0, n % d.breadth, pl.ds(n // d.breadth, 1), :]
        hit = jnp.where(row == target, 1.0, 0.0).astype(BF16)
        back = lax.dot_general(
            source, hit, (((1,), (1,)), ((), ())), preferred_element_type=F32
        )
        maps[0, n] = jnp.broadcast_to(row, (8, d.face))
        maps[1, n] = back.astype(jnp.int32)


def tables(d, nodes, weights, chaos, bonds, basis, masks):
    points = nodes[...]
    layer = lax.axis_index("sub")
    lane = lax.broadcasted_iota(jnp.int32, (d.height, bonds.shape[-1]), 1)

    def at(axis, x, z):
        picked = jnp.where(lane == z, bonds[axis, x].astype(F32), 0.0)
        return jnp.sum(picked, axis=1, keepdims=True)

    along = [[at(axis, x, layer) for x in range(d.breadth)] for axis in range(3)]
    under = [at(2, x, layer - 1) for x in range(d.breadth)]
    for n in range(d.subs):
        y, x = divmod(n, d.breadth)
        columns = [
            (along[0][(x - 1) % d.breadth], y),
            (along[0][x], y),
            (along[1][x], (y - 1) % d.height),
            (along[1][x], y),
            (under[x], y),
            (along[2][x], y),
        ]
        for which, (column, at_y) in enumerate(columns):
            masks[which, n] = jnp.broadcast_to(column[at_y : at_y + 1], (8, 128))
    one = jnp.sqrt(3.0) * points
    two = jnp.sqrt(5.0) * (1.5 * points * points - 0.5)
    three = jnp.sqrt(7.0) * (2.5 * points * points * points - 1.5 * points)
    total = jnp.ones((d.samples, d.terms), F32)
    for k in range(points.shape[1]):
        c = chaos[k : k + 1, :]
        high = jnp.where(c == 3, three[:, k : k + 1], two[:, k : k + 1])
        low = jnp.where(c == 1, one[:, k : k + 1], 1.0)
        total = total * jnp.where(c >= 2, high, low)
    square = (d.samples, d.samples)
    diagonal = lax.broadcasted_iota(jnp.int32, square, 0) == lax.broadcasted_iota(
        jnp.int32, square, 1
    )
    column = jnp.sum(jnp.where(diagonal, weights[...], 0.0), axis=1, keepdims=True)
    basis[...] = (column * total).T.astype(BF16)


def payloads(d, low, high, maps, on_chip, off_chip):
    even = lax.rem(lax.axis_index("sub"), 2) == 0
    for n in range(d.subs):
        back = maps[1, n]
        for start in range(n * d.samples, (n + 1) * d.samples, 8):
            rows = slice(start, start + 8)
            minus = low[rows]
            pushed = jnp.take_along_axis(high[rows], back, axis=1, mode="promise_in_bounds")
            on_chip[rows, :] = jnp.where(even, pushed, minus)
            off_chip[rows, :] = jnp.where(even, minus, pushed)


def part_of(d, shift):
    here = lax.axis_index("smp")
    return lax.rem(here - shift + d.parts, d.parts)


def combine(d, mod, part, first, second, field):
    width = field.shape[1]
    for n in range(d.subs):
        own = d.own(n, part)
        field[own, :] = (
            wide(mod[0, own, :], width) * first[d.group(n), :]
            + wide(mod[1, own, :], width) * second[d.group(n), :]
        )


def first_z(d, *refs):
    others = refs[: d.parts - 1]
    lam, mu, mod, maps, own_lam, own_mu, field, on_chip, off_chip = refs[d.parts - 1 :]
    at = slice(d.plane, d.width)
    combine(d, mod, lax.axis_index("smp"), own_lam.at[:, at], own_mu.at[:, at], field)
    for shift, other in enumerate(others, 1):
        rows = other[...]
        combine(d, mod, part_of(d, shift), dot(rows, lam[:, at]), dot(rows, mu[:, at]), field)
    payloads(d, field[:, : d.face], field[:, d.face :], maps, on_chip, off_chip)


def plane_jumps(d, field, masks, out):
    def mask(which, n):
        return jnp.concatenate([masks[which, n]] * (d.samples // 8), axis=0)

    for n in range(d.subs):
        y, x = divmod(n, d.breadth)
        left = y * d.breadth + (x - 1) % d.breadth
        right = y * d.breadth + (x + 1) % d.breadth
        front = (y - 1) % d.height * d.breadth + x
        behind = (y + 1) % d.height * d.breadth + x

        def face(which, m):
            return field[d.block(m), which * d.face : (which + 1) * d.face]

        out(0, n, mask(0, n) * (face(0, n) - face(1, left)))
        out(1, n, mask(1, n) * (face(1, n) - face(0, right)))
        out(2, n, mask(2, n) * (face(2, n) - face(3, front)))
        out(3, n, mask(3, n) * (face(3, n) - face(2, behind)))


def z_jumps(d, field, from_off, from_chip, maps, masks, out):
    layer = lax.axis_index("sub")
    even = lax.rem(layer, 2) == 0
    inside = jnp.logical_and(layer > 0, layer < lax.axis_size("sub") - 1)
    for n in range(d.subs):
        for start in range(n * d.samples, (n + 1) * d.samples, 8):
            rows = slice(start, start + 8)
            near, far = from_chip[rows, :], jnp.where(inside, from_off[rows, :], 0.0)
            above = jnp.where(even, near, far)
            below = jnp.where(even, far, near)
            matched = jnp.take_along_axis(above, maps[0, n], axis=1, mode="promise_in_bounds")
            out(0, rows, masks[4, n] * (field[rows, : d.face] - below))
            out(1, rows, masks[5, n] * (field[rows, d.face :] - matched))


def side_jumps(d, near, field, taken, maps, masks, out):
    layer = lax.axis_index("sub")
    even = lax.rem(layer, 2) == 0
    up = even if near else jnp.logical_not(even)
    inside = jnp.logical_and(layer > 0, layer < lax.axis_size("sub") - 1)
    for n in range(d.subs):
        for start in range(n * d.samples, (n + 1) * d.samples, 8):
            rows = slice(start, start + 8)
            other = taken[rows, :] if near else jnp.where(inside, taken[rows, :], 0.0)
            matched = jnp.take_along_axis(other, maps[0, n], axis=1, mode="promise_in_bounds")
            above = masks[5, n] * (field[rows, d.face :] - matched)
            below = masks[4, n] * (field[rows, : d.face] - other)
            out[rows, :] = jnp.where(up, above, below)
    return pl.ds(pl.multiple_of(jnp.where(up, 2, 1) * d.face, 128), d.face)


def first_plane(d, *refs):
    others = refs[: d.parts - 1]
    lam, mu, mod, own_lam, own_mu, masks, jumps, part_lam, part_mu, field = refs[d.parts - 1 :]
    at = slice(0, d.plane)
    combine(d, mod, lax.axis_index("smp"), own_lam.at[:, at], own_mu.at[:, at], field)
    for shift, other in enumerate(others, 1):
        rows = other[...]
        combine(d, mod, part_of(d, shift), dot(rows, lam[:, at]), dot(rows, mu[:, at]), field)

    def put(which, n, value):
        jumps[d.block(n), which * d.face : (which + 1) * d.face] = value.astype(BF16)

    plane_jumps(d, field, masks, put)
    part_lam[...] = dot(jumps[...], lam[: d.plane, d.plane :])
    part_mu[...] = dot(jumps[...], mu[: d.plane, d.plane :])


def second_z(
    d, field, from_off, from_chip, maps, masks, mod, lam, mu, part_lam, part_mu,
    jumps, result, on_chip, off_chip, held,
):
    def put(which, rows, value):
        held[rows, which * d.face : (which + 1) * d.face] = value

    z_jumps(d, field, from_off, from_chip, maps, masks, put)
    rounded = held[...].astype(BF16)
    jumps[...] = rounded
    one = part_lam[...] + dot(rounded, lam[d.plane :, d.plane :])
    two = part_mu[...] + dot(rounded, mu[d.plane :, d.plane :])
    result[...] = wide(mod[0], 2 * d.face) * one + wide(mod[1], 2 * d.face) * two
    payloads(d, result[:, : d.face], result[:, d.face :], maps, on_chip, off_chip)
    off_chip[d.rows :, :] = jnp.zeros((PAD, d.face), F32)


def second_plane(d, plane, zed, lam, mu, mod, masks, jumps):
    one = dot(plane[...], lam[: d.plane, : d.plane]) + dot(zed[...], lam[d.plane :, : d.plane])
    two = dot(plane[...], mu[: d.plane, : d.plane]) + dot(zed[...], mu[d.plane :, : d.plane])
    field = wide(mod[0], d.plane) * one + wide(mod[1], d.plane) * two

    def put(which, n, value):
        jumps[d.block(n), which * d.face : (which + 1) * d.face] = value.astype(BF16)

    plane_jumps(d, field, masks, put)


def last_z(d, field, from_off, from_chip, maps, masks, plane, jumps, held):
    def put(which, rows, value):
        held[rows, which * d.face : (which + 1) * d.face] = value

    z_jumps(d, field, from_off, from_chip, maps, masks, put)
    jumps[:, : d.plane] = plane[...]
    jumps[:, d.plane :] = held[...].astype(BF16)


def project_rows(d, picks, lanes, basis, out, rows_out, sem):
    width = rows_out.shape[-1]
    group = max(g for g in (1, 2, 3, 6) if d.subs % g == 0 and g * width <= 768)
    for n in range(0, d.subs, group):
        right = picks[n : n + group]
        right = right[0] if group == 1 else jnp.concatenate(right, axis=1)
        for start in range(0, d.terms, CHUNK):
            rows = slice(start, min(start + CHUNK, d.terms))
            value = dot(basis[rows, :], right)
            for m in range(group):
                y, x = divmod(n + m, d.breadth)
                rows_out[y, x, rows, :] = value[:, m * width : (m + 1) * width].astype(BF16)
                if out is not None:
                    pltpu.make_async_copy(
                        rows_out.at[y, x, rows, :], out.at[0, y, x, rows, lanes], sem
                    ).start()
    if out is not None:
        return pltpu.make_async_copy(rows_out, out.at[0, :, :, :, lanes], sem)


def project_plane(d, plane, basis, out, plane_out, all_out, sem):
    part = lax.axis_index("smp")

    @pl.when(part == 0)
    def _():
        picks = [plane[d.block(n), : d.share] for n in range(d.subs)]
        project_rows(d, picks, slice(0, d.share), basis, out, all_out, sem).wait()

    @pl.when(part == 1)
    def _():
        picks = [plane[d.block(n), d.share :] for n in range(d.subs)]
        project_rows(d, picks, None, basis, None, plane_out, None)


def last_part(even):
    here = lax.rem(lax.axis_index("sub"), 2) == (0 if even else 1)
    return jnp.logical_and(lax.axis_index("smp") == 1, here)


def plane_copy(d, plane_out, out, sem):
    return pltpu.make_async_copy(plane_out, out.at[0, :, :, :, slice(0, d.face)], sem)


def project_near(d, field, near, maps, masks, basis, plane_out, early, out, near_out, held, sems):
    def picks():
        lanes = side_jumps(d, True, field, near, maps, masks, held)
        return [held[d.block(n), :].astype(BF16) for n in range(d.subs)], lanes

    @pl.when(last_part(True))
    def _():
        first = plane_copy(d, plane_out, out, sems.at[0])
        first.start()
        rows, lanes = picks()
        second = project_rows(d, rows, lanes, basis, out, near_out, sems.at[1])
        first.wait()
        second.wait()

    @pl.when(last_part(False))
    def _():
        project_rows(d, picks()[0], None, basis, None, near_out, None)


def project_late(
    d, field, far, maps, masks, basis, plane_out, near_out, early, out, held, far_out, sems
):
    def project_far():
        lanes = side_jumps(d, False, field, far, maps, masks, held)
        picks = [held[d.block(n), :].astype(BF16) for n in range(d.subs)]
        return project_rows(d, picks, lanes, basis, out, far_out, sems.at[0])

    @pl.when(last_part(True))
    def _():
        project_far().wait()

    @pl.when(last_part(False))
    def _():
        at = slice(d.face, 2 * d.face)
        first = plane_copy(d, plane_out, out, sems.at[1])
        second = pltpu.make_async_copy(near_out, out.at[0, :, :, :, at], sems.at[2])
        first.start()
        second.start()
        project_far().wait()
        first.wait()
        second.wait()


def project_share(d, jumps, basis, out, rows_out, sem):
    picks = [jumps[d.block(n), :] for n in range(d.subs)]
    project_rows(d, picks, slice(0, d.share), basis, out, rows_out, sem).wait()


def per_device(
    trial, stiff_lam, stiff_mu, log_modes, nodes, quad_weights, chaos_index, bonds, face_map
):
    parts = lax.axis_size("smp")
    layers = lax.axis_size("sub")
    d = Sizes(trial, chaos_index.shape[0], parts)
    rows, face = d.rows, d.face
    own = trial.reshape(d.subs * d.here, d.width)
    others = [
        lax.ppermute(own, "smp", [(i, (i + shift) % parts) for i in range(parts)])
        for shift in range(1, parts)
    ]
    pairs = [(i, i ^ 1) for i in range(layers)]
    partner = {i: i + 1 if i % 2 else i - 1 for i in range(1, layers - 1)}
    across = [
        (i * parts + s, partner[i] * parts + s if i in partner else i * parts + (s + 1) % parts)
        for i in range(layers)
        for s in range(parts)
    ]

    second = across
    if parts == 2 and layers >= 4:
        top = layers - 1
        steps = {(i, 1): (partner[i], 1) for i in partner}
        steps.update({(i, 0): (i ^ 1, 0) for i in range(2, layers - 2)})
        steps.update({(0, 1): (1, 0), (1, 0): (0, 0), (0, 0): (0, 1)})
        steps.update({(top, 1): (top - 1, 0), (top - 1, 0): (top, 0), (top, 0): (top, 1)})
        second = sorted((i * 2 + s, j * 2 + t) for (i, s), (j, t) in steps.items())

    def exchange(on_chip, off_chip, across):
        far = lax.ppermute(off_chip, ("sub", "smp"), across)
        return lax.ppermute(on_chip, "sub", pairs), far

    def run(body, *args, **options):
        return call(functools.partial(body, d), *args, **options)

    product = shaped((d.subs * d.here, d.width))
    lam, mu = run(
        load,
        [shaped(stiff_lam.shape, BF16), shaped(stiff_mu.shape, BF16)],
        [HBM] * 2,
        [stiff_lam, stiff_mu],
        scratch=[pltpu.SemaphoreType.DMA((2,))],
        grant=51 << 20,
    )
    mod, maps, own_lam, own_mu = run(
        prepare,
        [shaped((2, rows, 128)), shaped((2, d.subs, 8, face), jnp.int32), product, product],
        [VMEM] * 6,
        [
            own, lam, mu,
            log_modes.transpose(0, 1, 3, 2, 4), nodes, face_map.transpose(0, 2, 1, 3),
        ],
    )
    field, on_chip, off_chip = run(
        first_z,
        [shaped((rows, 2 * face)), shaped((rows, face)), shaped((rows, face))],
        [VMEM] * (parts + 5),
        [*others, lam, mu, mod, maps, own_lam, own_mu],
    )
    near, far = exchange(on_chip, off_chip, across)
    basis, masks = run(
        tables,
        [shaped((d.terms, d.samples), BF16), shaped((6, d.subs, 8, 128))],
        [VMEM] * 4,
        [nodes, quad_weights.reshape(1, -1), chaos_index.T, bonds.transpose(0, 3, 2, 1)],
    )
    jumps_plane, part_lam, part_mu = run(
        first_plane,
        [shaped((rows, d.plane), BF16), shaped((rows, 2 * face)), shaped((rows, 2 * face))],
        [VMEM] * (parts + 5),
        [*others, lam, mu, mod, own_lam, own_mu, masks],
        scratch=[pltpu.VMEM((rows, d.plane), F32)],
    )
    jumps_z, field, on_chip, off_chip = run(
        second_z,
        [
            shaped((rows, 2 * face), BF16),
            shaped((rows, 2 * face)),
            shaped((rows, face)),
            shaped((rows + PAD, face)),
        ],
        [VMEM] * 10,
        [field, far, near, maps, masks, mod, lam, mu, part_lam, part_mu],
        scratch=[pltpu.VMEM((rows, 2 * face), F32)],
    )
    near, far = exchange(on_chip, off_chip, second)
    (plane,) = run(
        second_plane,
        [shaped((rows, d.plane), BF16)],
        [VMEM] * 6,
        [jumps_plane, jumps_z, lam, mu, mod, masks],
    )
    result = [shaped((1, d.height, d.breadth, d.terms, d.share), BF16)]

    def rows_out(width):
        return pltpu.VMEM((d.height, d.breadth, d.terms, width), BF16)

    if parts == 2:
        held = pltpu.VMEM((rows, face), F32)
        early, plane_out = run(
            project_plane,
            result + [shaped((d.height, d.breadth, d.terms, face), BF16)],
            [VMEM] * 2,
            [plane, basis],
            out_specs=[HBM, VMEM],
            scratch=[rows_out(d.share), pltpu.SemaphoreType.DMA(())],
        )
        early, near_out = run(
            project_near,
            result + [shaped((d.height, d.breadth, d.terms, face), BF16)],
            [VMEM] * 6 + [HBM],
            [field, near, maps, masks, basis, plane_out, early],
            out_specs=[HBM, VMEM],
            scratch=[held, pltpu.SemaphoreType.DMA((2,))],
            aliases={6: 0},
        )
        (out,) = run(
            project_late,
            result,
            [VMEM] * 7 + [HBM],
            [field, far, maps, masks, basis, plane_out, near_out, early],
            out_specs=[HBM],
            scratch=[held, rows_out(face), pltpu.SemaphoreType.DMA((3,))],
            aliases={7: 0},
        )
    else:
        last = [field, far, near, maps, masks, plane]
        held = pltpu.VMEM((rows, 2 * face), F32)
        (jumps,) = run(last_z, [shaped((rows, d.width), BF16)], [VMEM] * 6, last, scratch=[held])
        start = lax.axis_index("smp") * d.share
        jumps = lax.dynamic_slice_in_dim(jumps, start, d.share, 1)
        (out,) = run(
            project_share,
            result,
            [VMEM] * 2,
            [jumps, basis],
            out_specs=[HBM],
            scratch=[rows_out(d.share), pltpu.SemaphoreType.DMA(())],
        )
    return jnp.swapaxes(out, -1, -2)


def solution(mesh):
    return jax.shard_map(
        per_device,
        mesh=mesh,
        in_specs=(
            P("sub", None, None, "smp", None),
            P(),
            P(),
            P(None, "sub", None, None, None),
            P(),
            P(),
            P(),
            P(),
            P("sub", None, None, None),
        ),
        out_specs=P("sub", None, None, "smp", None),
        check_vma=False,
    )
```

```python
import functools

import jax
import jax.numpy as jnp
from jax import lax
from jax.experimental import pallas as pl
from jax.experimental.pallas import tpu as pltpu
from jax.sharding import PartitionSpec as P

F32 = jnp.float32
BF16 = jnp.bfloat16
VMEM = pl.BlockSpec(memory_space=pltpu.VMEM)
CHUNK = 144
PAD = 8
HBM = pl.BlockSpec(memory_space=pltpu.HBM)


def shaped(shape, dtype=F32):
    return jax.ShapeDtypeStruct(shape, dtype)


def call(body, outs, specs, args, flops=0, scratch=(), out_specs=None, grant=24 << 20, aliases=None):
    return pl.pallas_call(
        body,
        out_shape=outs,
        in_specs=specs,
        out_specs=[VMEM] * len(outs) if out_specs is None else out_specs,
        scratch_shapes=list(scratch),
        input_output_aliases=aliases or {},
        cost_estimate=pl.CostEstimate(flops=flops, bytes_accessed=0, transcendentals=0),
        compiler_params=pltpu.CompilerParams(vmem_limit_bytes=grant),
    )(*args)


def dot(a, b):
    return jnp.dot(a, b, preferred_element_type=F32)


def wide(column, width):
    return jnp.concatenate([column] * (width // 128), axis=1)


class Sizes:
    def __init__(self, trial, basis_size, parts):
        _, self.height, self.breadth, self.here, self.width = trial.shape
        self.face = self.width // 6
        self.subs = self.height * self.breadth
        self.parts = parts
        self.samples = self.here * parts
        self.rows = self.subs * self.samples
        self.plane = 4 * self.face
        self.terms = basis_size
        self.share = self.width // parts

    def own(self, n, part):
        return pl.ds(pl.multiple_of(n * self.samples + part * self.here, 8), self.here)

    def block(self, n):
        return slice(n * self.samples, (n + 1) * self.samples)

    def group(self, n):
        return slice(n * self.here, (n + 1) * self.here)


def load(d, lam, mu, lam_here, mu_here, sems):
    copies = [
        pltpu.make_async_copy(lam, lam_here, sems.at[0]),
        pltpu.make_async_copy(mu, mu_here, sems.at[1]),
    ]
    for copy in copies:
        copy.start()
    for copy in copies:
        copy.wait()


def prepare(d, trial, lam, mu, modes, nodes, faces, mod, maps, first, second):
    first[...] = dot(trial[...], lam[...])
    second[...] = dot(trial[...], mu[...])
    points = nodes[...]
    for c in range(2):
        for n in range(d.subs):
            row = modes[c, 0, n % d.breadth, pl.ds(n // d.breadth, 1), :]
            total = jnp.exp(jnp.sum(points * row, axis=1, keepdims=True))
            mod[c, d.block(n), :] = jnp.broadcast_to(total, (d.samples, 128))
    target = lax.broadcasted_iota(jnp.int32, (d.face, d.face), 0)
    source = lax.broadcasted_iota(jnp.int32, (8, d.face), 1).astype(F32).astype(BF16)
    for n in range(d.subs):
        row = faces[0, n % d.breadth, pl.ds(n // d.breadth, 1), :]
        hit = jnp.where(row == target, 1.0, 0.0).astype(BF16)
        back = lax.dot_general(
            source, hit, (((1,), (1,)), ((), ())), preferred_element_type=F32
        )
        maps[0, n] = jnp.broadcast_to(row, (8, d.face))
        maps[1, n] = back.astype(jnp.int32)


def tables(d, nodes, weights, chaos, bonds, basis, masks):
    points = nodes[...]
    layer = lax.axis_index("sub")
    lane = lax.broadcasted_iota(jnp.int32, (d.height, bonds.shape[-1]), 1)

    def at(axis, x, z):
        picked = jnp.where(lane == z, bonds[axis, x].astype(F32), 0.0)
        return jnp.sum(picked, axis=1, keepdims=True)

    along = [[at(axis, x, layer) for x in range(d.breadth)] for axis in range(3)]
    under = [at(2, x, layer - 1) for x in range(d.breadth)]
    for n in range(d.subs):
        y, x = divmod(n, d.breadth)
        columns = [
            (along[0][(x - 1) % d.breadth], y),
            (along[0][x], y),
            (along[1][x], (y - 1) % d.height),
            (along[1][x], y),
            (under[x], y),
            (along[2][x], y),
        ]
        for which, (column, at_y) in enumerate(columns):
            masks[which, n] = jnp.broadcast_to(column[at_y : at_y + 1], (8, 128))
    one = jnp.sqrt(3.0) * points
    two = jnp.sqrt(5.0) * (1.5 * points * points - 0.5)
    three = jnp.sqrt(7.0) * (2.5 * points * points * points - 1.5 * points)
    total = jnp.ones((d.samples, d.terms), F32)
    for k in range(points.shape[1]):
        c = chaos[k : k + 1, :]
        high = jnp.where(c == 3, three[:, k : k + 1], two[:, k : k + 1])
        low = jnp.where(c == 1, one[:, k : k + 1], 1.0)
        total = total * jnp.where(c >= 2, high, low)
    square = (d.samples, d.samples)
    diagonal = lax.broadcasted_iota(jnp.int32, square, 0) == lax.broadcasted_iota(
        jnp.int32, square, 1
    )
    column = jnp.sum(jnp.where(diagonal, weights[...], 0.0), axis=1, keepdims=True)
    basis[...] = (column * total).T.astype(BF16)


def payloads(d, low, high, maps, on_chip, off_chip):
    even = lax.rem(lax.axis_index("sub"), 2) == 0
    for n in range(d.subs):
        back = maps[1, n]
        for start in range(n * d.samples, (n + 1) * d.samples, 8):
            rows = slice(start, start + 8)
            minus = low[rows]
            pushed = jnp.take_along_axis(high[rows], back, axis=1, mode="promise_in_bounds")
            on_chip[rows, :] = jnp.where(even, pushed, minus)
            off_chip[rows, :] = jnp.where(even, minus, pushed)


def part_of(d, shift):
    here = lax.axis_index("smp")
    return lax.rem(here - shift + d.parts, d.parts)


def combine(d, mod, part, first, second, field):
    width = field.shape[1]
    for n in range(d.subs):
        own = d.own(n, part)
        field[own, :] = (
            wide(mod[0, own, :], width) * first[d.group(n), :]
            + wide(mod[1, own, :], width) * second[d.group(n), :]
        )


def first_z(d, *refs):
    others = refs[: d.parts - 1]
    lam, mu, mod, maps, own_lam, own_mu, field, on_chip, off_chip = refs[d.parts - 1 :]
    at = slice(d.plane, d.width)
    even = lax.rem(lax.axis_index("sub"), 2) == 0

    def finish(part, first, second):
        for n in range(d.subs):
            for start in range(0, d.here, 8):
                group = slice(n * d.here + start, n * d.here + start + 8)
                place = n * d.samples + part * d.here + start
                rows = pl.ds(pl.multiple_of(place, 8), 8)
                value = (
                    wide(mod[0, rows, :], 2 * d.face) * first[group, :]
                    + wide(mod[1, rows, :], 2 * d.face) * second[group, :]
                )
                field[rows, :] = value
                minus, high = value[:, : d.face], value[:, d.face :]
                pushed = jnp.take_along_axis(high, maps[1, n], axis=1, mode="promise_in_bounds")
                on_chip[rows, :] = jnp.where(even, pushed, minus)
                off_chip[rows, :] = jnp.where(even, minus, pushed)

    finish(lax.axis_index("smp"), own_lam[:, at], own_mu[:, at])
    for shift, other in enumerate(others, 1):
        rows = other[...]
        finish(part_of(d, shift), dot(rows, lam[:, at]), dot(rows, mu[:, at]))


def plane_jumps(d, field, masks, out):
    def mask(which, n):
        return jnp.concatenate([masks[which, n]] * (d.samples // 8), axis=0)

    for n in range(d.subs):
        y, x = divmod(n, d.breadth)
        left = y * d.breadth + (x - 1) % d.breadth
        right = y * d.breadth + (x + 1) % d.breadth
        front = (y - 1) % d.height * d.breadth + x
        behind = (y + 1) % d.height * d.breadth + x

        def face(which, m):
            return field[d.block(m), which * d.face : (which + 1) * d.face]

        out(0, n, mask(0, n) * (face(0, n) - face(1, left)))
        out(1, n, mask(1, n) * (face(1, n) - face(0, right)))
        out(2, n, mask(2, n) * (face(2, n) - face(3, front)))
        out(3, n, mask(3, n) * (face(3, n) - face(2, behind)))


def z_jumps(d, field, from_off, from_chip, maps, masks, out):
    layer = lax.axis_index("sub")
    even = lax.rem(layer, 2) == 0
    inside = jnp.logical_and(layer > 0, layer < lax.axis_size("sub") - 1)
    for n in range(d.subs):
        for start in range(n * d.samples, (n + 1) * d.samples, 8):
            rows = slice(start, start + 8)
            near, far = from_chip[rows, :], jnp.where(inside, from_off[rows, :], 0.0)
            above = jnp.where(even, near, far)
            below = jnp.where(even, far, near)
            matched = jnp.take_along_axis(above, maps[0, n], axis=1, mode="promise_in_bounds")
            out(0, rows, masks[4, n] * (field[rows, : d.face] - below))
            out(1, rows, masks[5, n] * (field[rows, d.face :] - matched))


def side_jumps(d, near, field, taken, maps, masks, out):
    layer = lax.axis_index("sub")
    even = lax.rem(layer, 2) == 0
    up = even if near else jnp.logical_not(even)
    inside = jnp.logical_and(layer > 0, layer < lax.axis_size("sub") - 1)
    for n in range(d.subs):
        for start in range(n * d.samples, (n + 1) * d.samples, 8):
            rows = slice(start, start + 8)
            other = taken[rows, :] if near else jnp.where(inside, taken[rows, :], 0.0)
            matched = jnp.take_along_axis(other, maps[0, n], axis=1, mode="promise_in_bounds")
            above = masks[5, n] * (field[rows, d.face :] - matched)
            below = masks[4, n] * (field[rows, : d.face] - other)
            out[rows, :] = jnp.where(up, above, below)
    return pl.ds(pl.multiple_of(jnp.where(up, 2, 1) * d.face, 128), d.face)


def first_plane(d, *refs):
    others = refs[: d.parts - 1]
    lam, mu, mod, own_lam, own_mu, masks, jumps, part_lam, part_mu, field = refs[d.parts - 1 :]
    at = slice(0, d.plane)
    combine(d, mod, lax.axis_index("smp"), own_lam.at[:, at], own_mu.at[:, at], field)
    for shift, other in enumerate(others, 1):
        rows = other[...]
        combine(d, mod, part_of(d, shift), dot(rows, lam[:, at]), dot(rows, mu[:, at]), field)

    def put(which, n, value):
        jumps[d.block(n), which * d.face : (which + 1) * d.face] = value.astype(BF16)

    plane_jumps(d, field, masks, put)
    part_lam[...] = dot(jumps[...], lam[: d.plane, d.plane :])
    part_mu[...] = dot(jumps[...], mu[: d.plane, d.plane :])


def second_z(
    d, field, from_off, from_chip, maps, masks, mod, lam, mu, part_lam, part_mu,
    jumps, result, on_chip, off_chip, held,
):
    def put(which, rows, value):
        held[rows, which * d.face : (which + 1) * d.face] = value

    z_jumps(d, field, from_off, from_chip, maps, masks, put)
    rounded = held[...].astype(BF16)
    jumps[...] = rounded
    one = part_lam[...] + dot(rounded, lam[d.plane :, d.plane :])
    two = part_mu[...] + dot(rounded, mu[d.plane :, d.plane :])
    result[...] = wide(mod[0], 2 * d.face) * one + wide(mod[1], 2 * d.face) * two
    payloads(d, result[:, : d.face], result[:, d.face :], maps, on_chip, off_chip)
    off_chip[d.rows :, :] = jnp.zeros((PAD, d.face), F32)


def second_plane(d, plane, zed, lam, mu, mod, masks, jumps):
    one = dot(plane[...], lam[: d.plane, : d.plane]) + dot(zed[...], lam[d.plane :, : d.plane])
    two = dot(plane[...], mu[: d.plane, : d.plane]) + dot(zed[...], mu[d.plane :, : d.plane])
    field = wide(mod[0], d.plane) * one + wide(mod[1], d.plane) * two

    def put(which, n, value):
        jumps[d.block(n), which * d.face : (which + 1) * d.face] = value.astype(BF16)

    plane_jumps(d, field, masks, put)


def last_z(d, field, from_off, from_chip, maps, masks, plane, jumps, held):
    def put(which, rows, value):
        held[rows, which * d.face : (which + 1) * d.face] = value

    z_jumps(d, field, from_off, from_chip, maps, masks, put)
    jumps[:, : d.plane] = plane[...]
    jumps[:, d.plane :] = held[...].astype(BF16)


def project_rows(d, picks, lanes, basis, out, rows_out, sem):
    width = rows_out.shape[-1]
    group = max(g for g in (1, 2, 3, 6) if d.subs % g == 0 and g * width <= 768)
    for n in range(0, d.subs, group):
        right = picks[n : n + group]
        right = right[0] if group == 1 else jnp.concatenate(right, axis=1)
        for start in range(0, d.terms, CHUNK):
            rows = slice(start, min(start + CHUNK, d.terms))
            value = dot(basis[rows, :], right)
            for m in range(group):
                y, x = divmod(n + m, d.breadth)
                rows_out[y, x, rows, :] = value[:, m * width : (m + 1) * width].astype(BF16)
                if out is not None:
                    pltpu.make_async_copy(
                        rows_out.at[y, x, rows, :], out.at[0, y, x, rows, lanes], sem
                    ).start()
    if out is not None:
        return pltpu.make_async_copy(rows_out, out.at[0, :, :, :, lanes], sem)


def project_plane(d, plane, basis, out, plane_out, all_out, sem):
    part = lax.axis_index("smp")

    @pl.when(part == 0)
    def _():
        picks = [plane[d.block(n), : d.share] for n in range(d.subs)]
        project_rows(d, picks, slice(0, d.share), basis, out, all_out, sem).wait()

    @pl.when(part == 1)
    def _():
        picks = [plane[d.block(n), d.share :] for n in range(d.subs)]
        project_rows(d, picks, None, basis, None, plane_out, None)


def last_part(even):
    here = lax.rem(lax.axis_index("sub"), 2) == (0 if even else 1)
    return jnp.logical_and(lax.axis_index("smp") == 1, here)


def plane_copy(d, plane_out, out, sem):
    return pltpu.make_async_copy(plane_out, out.at[0, :, :, :, slice(0, d.face)], sem)


def project_near(d, field, near, maps, masks, basis, plane_out, early, out, near_out, held, sems):
    def picks():
        lanes = side_jumps(d, True, field, near, maps, masks, held)
        return [held[d.block(n), :].astype(BF16) for n in range(d.subs)], lanes

    @pl.when(last_part(True))
    def _():
        first = plane_copy(d, plane_out, out, sems.at[0])
        first.start()
        rows, lanes = picks()
        second = project_rows(d, rows, lanes, basis, out, near_out, sems.at[1])
        first.wait()
        second.wait()

    @pl.when(last_part(False))
    def _():
        project_rows(d, picks()[0], None, basis, None, near_out, None)


def project_late(
    d, field, far, maps, masks, basis, plane_out, near_out, early, out, held, far_out, sems
):
    def project_far():
        lanes = side_jumps(d, False, field, far, maps, masks, held)
        picks = [held[d.block(n), :].astype(BF16) for n in range(d.subs)]
        return project_rows(d, picks, lanes, basis, out, far_out, sems.at[0])

    @pl.when(last_part(True))
    def _():
        project_far().wait()

    @pl.when(last_part(False))
    def _():
        at = slice(d.face, 2 * d.face)
        first = plane_copy(d, plane_out, out, sems.at[1])
        second = pltpu.make_async_copy(near_out, out.at[0, :, :, :, at], sems.at[2])
        first.start()
        second.start()
        project_far().wait()
        first.wait()
        second.wait()


def project_share(d, jumps, basis, out, rows_out, sem):
    picks = [jumps[d.block(n), :] for n in range(d.subs)]
    project_rows(d, picks, slice(0, d.share), basis, out, rows_out, sem).wait()


def per_device(
    trial, stiff_lam, stiff_mu, log_modes, nodes, quad_weights, chaos_index, bonds, face_map
):
    parts = lax.axis_size("smp")
    layers = lax.axis_size("sub")
    d = Sizes(trial, chaos_index.shape[0], parts)
    rows, face = d.rows, d.face
    own = trial.reshape(d.subs * d.here, d.width)
    others = [
        lax.ppermute(own, "smp", [(i, (i + shift) % parts) for i in range(parts)])
        for shift in range(1, parts)
    ]
    pairs = [(i, i ^ 1) for i in range(layers)]
    partner = {i: i + 1 if i % 2 else i - 1 for i in range(1, layers - 1)}
    across = [
        (i * parts + s, partner[i] * parts + s if i in partner else i * parts + (s + 1) % parts)
        for i in range(layers)
        for s in range(parts)
    ]

    second = across
    if parts == 2 and layers >= 4:
        top = layers - 1
        steps = {(i, 1): (partner[i], 1) for i in partner}
        steps.update({(i, 0): (i ^ 1, 0) for i in range(2, layers - 2)})
        steps.update({(0, 1): (1, 0), (1, 0): (0, 0), (0, 0): (0, 1)})
        steps.update({(top, 1): (top - 1, 0), (top - 1, 0): (top, 0), (top, 0): (top, 1)})
        second = sorted((i * 2 + s, j * 2 + t) for (i, s), (j, t) in steps.items())

    def exchange(on_chip, off_chip, across):
        far = lax.ppermute(off_chip, ("sub", "smp"), across)
        return lax.ppermute(on_chip, "sub", pairs), far

    def run(body, *args, **options):
        return call(functools.partial(body, d), *args, **options)

    product = shaped((d.subs * d.here, d.width))
    lam, mu = run(
        load,
        [shaped(stiff_lam.shape, BF16), shaped(stiff_mu.shape, BF16)],
        [HBM] * 2,
        [stiff_lam, stiff_mu],
        scratch=[pltpu.SemaphoreType.DMA((2,))],
        grant=51 << 20,
    )
    mod, maps, own_lam, own_mu = run(
        prepare,
        [shaped((2, rows, 128)), shaped((2, d.subs, 8, face), jnp.int32), product, product],
        [VMEM] * 6,
        [
            own, lam, mu,
            log_modes.transpose(0, 1, 3, 2, 4), nodes, face_map.transpose(0, 2, 1, 3),
        ],
    )
    field, on_chip, off_chip = run(
        first_z,
        [shaped((rows, 2 * face)), shaped((rows, face)), shaped((rows, face))],
        [VMEM] * (parts + 5),
        [*others, lam, mu, mod, maps, own_lam, own_mu],
    )
    near, far = exchange(on_chip, off_chip, across)
    basis, masks = run(
        tables,
        [shaped((d.terms, d.samples), BF16), shaped((6, d.subs, 8, 128))],
        [VMEM] * 4,
        [nodes, quad_weights.reshape(1, -1), chaos_index.T, bonds.transpose(0, 3, 2, 1)],
    )
    jumps_plane, part_lam, part_mu = run(
        first_plane,
        [shaped((rows, d.plane), BF16), shaped((rows, 2 * face)), shaped((rows, 2 * face))],
        [VMEM] * (parts + 5),
        [*others, lam, mu, mod, own_lam, own_mu, masks],
        scratch=[pltpu.VMEM((rows, d.plane), F32)],
    )
    jumps_z, field, on_chip, off_chip = run(
        second_z,
        [
            shaped((rows, 2 * face), BF16),
            shaped((rows, 2 * face)),
            shaped((rows, face)),
            shaped((rows + PAD, face)),
        ],
        [VMEM] * 10,
        [field, far, near, maps, masks, mod, lam, mu, part_lam, part_mu],
        scratch=[pltpu.VMEM((rows, 2 * face), F32)],
    )
    near, far = exchange(on_chip, off_chip, second)
    (plane,) = run(
        second_plane,
        [shaped((rows, d.plane), BF16)],
        [VMEM] * 6,
        [jumps_plane, jumps_z, lam, mu, mod, masks],
    )
    result = [shaped((1, d.height, d.breadth, d.terms, d.share), BF16)]

    def rows_out(width):
        return pltpu.VMEM((d.height, d.breadth, d.terms, width), BF16)

    if parts == 2:
        held = pltpu.VMEM((rows, face), F32)
        early, plane_out = run(
            project_plane,
            result + [shaped((d.height, d.breadth, d.terms, face), BF16)],
            [VMEM] * 2,
            [plane, basis],
            out_specs=[HBM, VMEM],
            scratch=[rows_out(d.share), pltpu.SemaphoreType.DMA(())],
        )
        early, near_out = run(
            project_near,
            result + [shaped((d.height, d.breadth, d.terms, face), BF16)],
            [VMEM] * 6 + [HBM],
            [field, near, maps, masks, basis, plane_out, early],
            out_specs=[HBM, VMEM],
            scratch=[held, pltpu.SemaphoreType.DMA((2,))],
            aliases={6: 0},
        )
        (out,) = run(
            project_late,
            result,
            [VMEM] * 7 + [HBM],
            [field, far, maps, masks, basis, plane_out, near_out, early],
            out_specs=[HBM],
            scratch=[held, rows_out(face), pltpu.SemaphoreType.DMA((3,))],
            aliases={7: 0},
        )
    else:
        last = [field, far, near, maps, masks, plane]
        held = pltpu.VMEM((rows, 2 * face), F32)
        (jumps,) = run(last_z, [shaped((rows, d.width), BF16)], [VMEM] * 6, last, scratch=[held])
        start = lax.axis_index("smp") * d.share
        jumps = lax.dynamic_slice_in_dim(jumps, start, d.share, 1)
        (out,) = run(
            project_share,
            result,
            [VMEM] * 2,
            [jumps, basis],
            out_specs=[HBM],
            scratch=[rows_out(d.share), pltpu.SemaphoreType.DMA(())],
        )
    return jnp.swapaxes(out, -1, -2)


def solution(mesh):
    return jax.shard_map(
        per_device,
        mesh=mesh,
        in_specs=(
            P("sub", None, None, "smp", None),
            P(),
            P(),
            P(None, "sub", None, None, None),
            P(),
            P(),
            P(),
            P(),
            P("sub", None, None, None),
        ),
        out_specs=P("sub", None, None, "smp", None),
        check_vma=False,
    )
```

```python
import functools

import jax
import jax.numpy as jnp
from jax import lax
from jax.experimental import pallas as pl
from jax.experimental.pallas import tpu as pltpu
from jax.sharding import PartitionSpec as P

F32 = jnp.float32
BF16 = jnp.bfloat16
VMEM = pl.BlockSpec(memory_space=pltpu.VMEM)
CHUNK = 144
PAD = 8
HBM = pl.BlockSpec(memory_space=pltpu.HBM)


def shaped(shape, dtype=F32):
    return jax.ShapeDtypeStruct(shape, dtype)


def call(body, outs, specs, args, flops=0, scratch=(), out_specs=None, grant=24 << 20, aliases=None):
    return pl.pallas_call(
        body,
        out_shape=outs,
        in_specs=specs,
        out_specs=[VMEM] * len(outs) if out_specs is None else out_specs,
        scratch_shapes=list(scratch),
        input_output_aliases=aliases or {},
        cost_estimate=pl.CostEstimate(flops=flops, bytes_accessed=0, transcendentals=0),
        compiler_params=pltpu.CompilerParams(vmem_limit_bytes=grant),
    )(*args)


def dot(a, b):
    return jnp.dot(a, b, preferred_element_type=F32)


def wide(column, width):
    return jnp.concatenate([column] * (width // 128), axis=1)


class Sizes:
    def __init__(self, trial, basis_size, parts):
        _, self.height, self.breadth, self.here, self.width = trial.shape
        self.face = self.width // 6
        self.subs = self.height * self.breadth
        self.parts = parts
        self.samples = self.here * parts
        self.rows = self.subs * self.samples
        self.plane = 4 * self.face
        self.terms = basis_size
        self.share = self.width // parts

    def own(self, n, part):
        return pl.ds(pl.multiple_of(n * self.samples + part * self.here, 8), self.here)

    def block(self, n):
        return slice(n * self.samples, (n + 1) * self.samples)

    def group(self, n):
        return slice(n * self.here, (n + 1) * self.here)


def load(d, lam, mu, lam_here, mu_here, sems):
    copies = [
        pltpu.make_async_copy(lam, lam_here, sems.at[0]),
        pltpu.make_async_copy(mu, mu_here, sems.at[1]),
    ]
    for copy in copies:
        copy.start()
    for copy in copies:
        copy.wait()


def prepare(d, trial, lam, mu, modes, nodes, faces, mod, maps, first, second):
    first[...] = dot(trial[...], lam[...])
    second[...] = dot(trial[...], mu[...])
    points = nodes[...]
    for c in range(2):
        for n in range(d.subs):
            row = modes[c, 0, n % d.breadth, pl.ds(n // d.breadth, 1), :]
            total = jnp.exp(jnp.sum(points * row, axis=1, keepdims=True))
            mod[c, d.block(n), :] = jnp.broadcast_to(total, (d.samples, 128))
    target = lax.broadcasted_iota(jnp.int32, (d.face, d.face), 0)
    source = lax.broadcasted_iota(jnp.int32, (8, d.face), 1).astype(F32).astype(BF16)
    for n in range(d.subs):
        row = faces[0, n % d.breadth, pl.ds(n // d.breadth, 1), :]
        hit = jnp.where(row == target, 1.0, 0.0).astype(BF16)
        back = lax.dot_general(
            source, hit, (((1,), (1,)), ((), ())), preferred_element_type=F32
        )
        maps[0, n] = jnp.broadcast_to(row, (8, d.face))
        maps[1, n] = back.astype(jnp.int32)


def tables(d, nodes, weights, chaos, bonds, basis, masks):
    points = nodes[...]
    layer = lax.axis_index("sub")
    lane = lax.broadcasted_iota(jnp.int32, (d.height, bonds.shape[-1]), 1)

    def at(axis, x, z):
        picked = jnp.where(lane == z, bonds[axis, x].astype(F32), 0.0)
        return jnp.sum(picked, axis=1, keepdims=True)

    along = [[at(axis, x, layer) for x in range(d.breadth)] for axis in range(3)]
    under = [at(2, x, layer - 1) for x in range(d.breadth)]
    for n in range(d.subs):
        y, x = divmod(n, d.breadth)
        columns = [
            (along[0][(x - 1) % d.breadth], y),
            (along[0][x], y),
            (along[1][x], (y - 1) % d.height),
            (along[1][x], y),
            (under[x], y),
            (along[2][x], y),
        ]
        for which, (column, at_y) in enumerate(columns):
            masks[which, n] = jnp.broadcast_to(column[at_y : at_y + 1], (8, 128))
    one = jnp.sqrt(3.0) * points
    two = jnp.sqrt(5.0) * (1.5 * points * points - 0.5)
    three = jnp.sqrt(7.0) * (2.5 * points * points * points - 1.5 * points)
    total = jnp.ones((d.samples, d.terms), F32)
    for k in range(points.shape[1]):
        c = chaos[k : k + 1, :]
        high = jnp.where(c == 3, three[:, k : k + 1], two[:, k : k + 1])
        low = jnp.where(c == 1, one[:, k : k + 1], 1.0)
        total = total * jnp.where(c >= 2, high, low)
    square = (d.samples, d.samples)
    diagonal = lax.broadcasted_iota(jnp.int32, square, 0) == lax.broadcasted_iota(
        jnp.int32, square, 1
    )
    column = jnp.sum(jnp.where(diagonal, weights[...], 0.0), axis=1, keepdims=True)
    basis[...] = (column * total).T.astype(BF16)


def payloads(d, low, high, maps, on_chip, off_chip):
    even = lax.rem(lax.axis_index("sub"), 2) == 0
    for n in range(d.subs):
        back = maps[1, n]
        for start in range(n * d.samples, (n + 1) * d.samples, 8):
            rows = slice(start, start + 8)
            minus = low[rows]
            pushed = jnp.take_along_axis(high[rows], back, axis=1, mode="promise_in_bounds")
            on_chip[rows, :] = jnp.where(even, pushed, minus)
            off_chip[rows, :] = jnp.where(even, minus, pushed)


def part_of(d, shift):
    here = lax.axis_index("smp")
    return lax.rem(here - shift + d.parts, d.parts)


def combine(d, mod, part, first, second, field):
    width = field.shape[1]
    for n in range(d.subs):
        own = d.own(n, part)
        field[own, :] = (
            wide(mod[0, own, :], width) * first[d.group(n), :]
            + wide(mod[1, own, :], width) * second[d.group(n), :]
        )


def first_z(d, *refs):
    others = refs[: d.parts - 1]
    lam, mu, mod, maps, own_lam, own_mu, field, on_chip, off_chip = refs[d.parts - 1 :]
    at = slice(d.plane, d.width)
    even = lax.rem(lax.axis_index("sub"), 2) == 0

    def finish(part, first, second):
        for n in range(d.subs):
            for start in range(0, d.here, 8):
                group = slice(n * d.here + start, n * d.here + start + 8)
                place = n * d.samples + part * d.here + start
                rows = pl.ds(pl.multiple_of(place, 8), 8)
                value = (
                    wide(mod[0, rows, :], 2 * d.face) * first[group, :]
                    + wide(mod[1, rows, :], 2 * d.face) * second[group, :]
                )
                field[rows, :] = value
                minus, high = value[:, : d.face], value[:, d.face :]
                pushed = jnp.take_along_axis(high, maps[1, n], axis=1, mode="promise_in_bounds")
                on_chip[rows, :] = jnp.where(even, pushed, minus)
                off_chip[rows, :] = jnp.where(even, minus, pushed)

    finish(lax.axis_index("smp"), own_lam[:, at], own_mu[:, at])
    for shift, other in enumerate(others, 1):
        rows = other[...]
        finish(part_of(d, shift), dot(rows, lam[:, at]), dot(rows, mu[:, at]))


def plane_jumps(d, field, masks, out):
    def mask(which, n):
        return jnp.concatenate([masks[which, n]] * (d.samples // 8), axis=0)

    for n in range(d.subs):
        y, x = divmod(n, d.breadth)
        left = y * d.breadth + (x - 1) % d.breadth
        right = y * d.breadth + (x + 1) % d.breadth
        front = (y - 1) % d.height * d.breadth + x
        behind = (y + 1) % d.height * d.breadth + x

        def face(which, m):
            return field[d.block(m), which * d.face : (which + 1) * d.face]

        out(0, n, mask(0, n) * (face(0, n) - face(1, left)))
        out(1, n, mask(1, n) * (face(1, n) - face(0, right)))
        out(2, n, mask(2, n) * (face(2, n) - face(3, front)))
        out(3, n, mask(3, n) * (face(3, n) - face(2, behind)))


def z_jumps(d, field, from_off, from_chip, maps, masks, out):
    layer = lax.axis_index("sub")
    even = lax.rem(layer, 2) == 0
    inside = jnp.logical_and(layer > 0, layer < lax.axis_size("sub") - 1)
    for n in range(d.subs):
        for start in range(n * d.samples, (n + 1) * d.samples, 8):
            rows = slice(start, start + 8)
            near, far = from_chip[rows, :], jnp.where(inside, from_off[rows, :], 0.0)
            above = jnp.where(even, near, far)
            below = jnp.where(even, far, near)
            matched = jnp.take_along_axis(above, maps[0, n], axis=1, mode="promise_in_bounds")
            out(0, rows, masks[4, n] * (field[rows, : d.face] - below))
            out(1, rows, masks[5, n] * (field[rows, d.face :] - matched))


def side_jumps(d, near, field, taken, maps, masks, out):
    layer = lax.axis_index("sub")
    even = lax.rem(layer, 2) == 0
    up = even if near else jnp.logical_not(even)
    inside = jnp.logical_and(layer > 0, layer < lax.axis_size("sub") - 1)
    for n in range(d.subs):
        for start in range(n * d.samples, (n + 1) * d.samples, 8):
            rows = slice(start, start + 8)
            other = taken[rows, :] if near else jnp.where(inside, taken[rows, :], 0.0)
            matched = jnp.take_along_axis(other, maps[0, n], axis=1, mode="promise_in_bounds")
            above = masks[5, n] * (field[rows, d.face :] - matched)
            below = masks[4, n] * (field[rows, : d.face] - other)
            out[rows, :] = jnp.where(up, above, below)
    return pl.ds(pl.multiple_of(jnp.where(up, 2, 1) * d.face, 128), d.face)


def first_plane(d, *refs):
    others = refs[: d.parts - 1]
    lam, mu, mod, own_lam, own_mu, masks, jumps, part_lam, part_mu, field = refs[d.parts - 1 :]
    at = slice(0, d.plane)
    combine(d, mod, lax.axis_index("smp"), own_lam.at[:, at], own_mu.at[:, at], field)
    for shift, other in enumerate(others, 1):
        rows = other[...]
        combine(d, mod, part_of(d, shift), dot(rows, lam[:, at]), dot(rows, mu[:, at]), field)

    def put(which, n, value):
        jumps[d.block(n), which * d.face : (which + 1) * d.face] = value.astype(BF16)

    plane_jumps(d, field, masks, put)
    part_lam[...] = dot(jumps[...], lam[: d.plane, d.plane :])
    part_mu[...] = dot(jumps[...], mu[: d.plane, d.plane :])


def second_z(
    d, field, from_off, from_chip, maps, masks, mod, lam, mu, part_lam, part_mu,
    jumps, result, on_chip, off_chip,
):
    faces = ([], [])
    z_jumps(
        d, field, from_off, from_chip, maps, masks,
        lambda which, rows, value: faces[which].append(value),
    )
    minus, plus = (jnp.concatenate(face, axis=0) for face in faces)
    rounded = jnp.concatenate([minus, plus], axis=1).astype(BF16)
    jumps[...] = rounded
    one = part_lam[...] + dot(rounded, lam[d.plane :, d.plane :])
    two = part_mu[...] + dot(rounded, mu[d.plane :, d.plane :])
    value = wide(mod[0], 2 * d.face) * one + wide(mod[1], 2 * d.face) * two
    result[...] = value
    payloads(d, value[:, : d.face], value[:, d.face :], maps, on_chip, off_chip)
    off_chip[d.rows :, :] = jnp.zeros((PAD, d.face), F32)


def second_plane(d, plane, zed, lam, mu, mod, masks, jumps):
    one = dot(plane[...], lam[: d.plane, : d.plane]) + dot(zed[...], lam[d.plane :, : d.plane])
    two = dot(plane[...], mu[: d.plane, : d.plane]) + dot(zed[...], mu[d.plane :, : d.plane])
    field = wide(mod[0], d.plane) * one + wide(mod[1], d.plane) * two

    def put(which, n, value):
        jumps[d.block(n), which * d.face : (which + 1) * d.face] = value.astype(BF16)

    plane_jumps(d, field, masks, put)


def last_z(d, field, from_off, from_chip, maps, masks, plane, jumps, held):
    def put(which, rows, value):
        held[rows, which * d.face : (which + 1) * d.face] = value

    z_jumps(d, field, from_off, from_chip, maps, masks, put)
    jumps[:, : d.plane] = plane[...]
    jumps[:, d.plane :] = held[...].astype(BF16)


def project_rows(d, picks, lanes, basis, out, rows_out, sem):
    width = rows_out.shape[-1]
    group = max(g for g in (1, 2, 3, 6) if d.subs % g == 0 and g * width <= 768)
    for n in range(0, d.subs, group):
        right = picks[n : n + group]
        right = right[0] if group == 1 else jnp.concatenate(right, axis=1)
        for start in range(0, d.terms, CHUNK):
            rows = slice(start, min(start + CHUNK, d.terms))
            value = dot(basis[rows, :], right)
            for m in range(group):
                y, x = divmod(n + m, d.breadth)
                rows_out[y, x, rows, :] = value[:, m * width : (m + 1) * width].astype(BF16)
                if out is not None:
                    pltpu.make_async_copy(
                        rows_out.at[y, x, rows, :], out.at[0, y, x, rows, lanes], sem
                    ).start()
    if out is not None:
        return pltpu.make_async_copy(rows_out, out.at[0, :, :, :, lanes], sem)


def project_plane(d, plane, basis, out, plane_out, all_out, sem):
    part = lax.axis_index("smp")

    @pl.when(part == 0)
    def _():
        picks = [plane[d.block(n), : d.share] for n in range(d.subs)]
        project_rows(d, picks, slice(0, d.share), basis, out, all_out, sem).wait()

    @pl.when(part == 1)
    def _():
        picks = [plane[d.block(n), d.share :] for n in range(d.subs)]
        project_rows(d, picks, None, basis, None, plane_out, None)


def last_part(even):
    here = lax.rem(lax.axis_index("sub"), 2) == (0 if even else 1)
    return jnp.logical_and(lax.axis_index("smp") == 1, here)


def plane_copy(d, plane_out, out, sem):
    return pltpu.make_async_copy(plane_out, out.at[0, :, :, :, slice(0, d.face)], sem)


def project_near(d, field, near, maps, masks, basis, plane_out, early, out, near_out, held, sems):
    def picks():
        lanes = side_jumps(d, True, field, near, maps, masks, held)
        return [held[d.block(n), :].astype(BF16) for n in range(d.subs)], lanes

    @pl.when(last_part(True))
    def _():
        first = plane_copy(d, plane_out, out, sems.at[0])
        first.start()
        rows, lanes = picks()
        second = project_rows(d, rows, lanes, basis, out, near_out, sems.at[1])
        first.wait()
        second.wait()

    @pl.when(last_part(False))
    def _():
        project_rows(d, picks()[0], None, basis, None, near_out, None)


def project_late(
    d, field, far, maps, masks, basis, plane_out, near_out, early, out, held, far_out, sems
):
    def project_far():
        lanes = side_jumps(d, False, field, far, maps, masks, held)
        picks = [held[d.block(n), :].astype(BF16) for n in range(d.subs)]
        return project_rows(d, picks, lanes, basis, out, far_out, sems.at[0])

    @pl.when(last_part(True))
    def _():
        project_far().wait()

    @pl.when(last_part(False))
    def _():
        at = slice(d.face, 2 * d.face)
        first = plane_copy(d, plane_out, out, sems.at[1])
        second = pltpu.make_async_copy(near_out, out.at[0, :, :, :, at], sems.at[2])
        first.start()
        second.start()
        project_far().wait()
        first.wait()
        second.wait()


def project_share(d, jumps, basis, out, rows_out, sem):
    picks = [jumps[d.block(n), :] for n in range(d.subs)]
    project_rows(d, picks, slice(0, d.share), basis, out, rows_out, sem).wait()


def per_device(
    trial, stiff_lam, stiff_mu, log_modes, nodes, quad_weights, chaos_index, bonds, face_map
):
    parts = lax.axis_size("smp")
    layers = lax.axis_size("sub")
    d = Sizes(trial, chaos_index.shape[0], parts)
    rows, face = d.rows, d.face
    own = trial.reshape(d.subs * d.here, d.width)
    others = [
        lax.ppermute(own, "smp", [(i, (i + shift) % parts) for i in range(parts)])
        for shift in range(1, parts)
    ]
    pairs = [(i, i ^ 1) for i in range(layers)]
    partner = {i: i + 1 if i % 2 else i - 1 for i in range(1, layers - 1)}
    across = [
        (i * parts + s, partner[i] * parts + s if i in partner else i * parts + (s + 1) % parts)
        for i in range(layers)
        for s in range(parts)
    ]

    second = across
    if parts == 2 and layers >= 4:
        top = layers - 1
        steps = {(i, 1): (partner[i], 1) for i in partner}
        steps.update({(i, 0): (i ^ 1, 0) for i in range(2, layers - 2)})
        steps.update({(0, 1): (1, 0), (1, 0): (0, 0), (0, 0): (0, 1)})
        steps.update({(top, 1): (top - 1, 0), (top - 1, 0): (top, 0), (top, 0): (top, 1)})
        second = sorted((i * 2 + s, j * 2 + t) for (i, s), (j, t) in steps.items())

    def exchange(on_chip, off_chip, across):
        far = lax.ppermute(off_chip, ("sub", "smp"), across)
        return lax.ppermute(on_chip, "sub", pairs), far

    def run(body, *args, **options):
        return call(functools.partial(body, d), *args, **options)

    product = shaped((d.subs * d.here, d.width))
    lam, mu = run(
        load,
        [shaped(stiff_lam.shape, BF16), shaped(stiff_mu.shape, BF16)],
        [HBM] * 2,
        [stiff_lam, stiff_mu],
        scratch=[pltpu.SemaphoreType.DMA((2,))],
        grant=51 << 20,
    )
    mod, maps, own_lam, own_mu = run(
        prepare,
        [shaped((2, rows, 128)), shaped((2, d.subs, 8, face), jnp.int32), product, product],
        [VMEM] * 6,
        [
            own, lam, mu,
            log_modes.transpose(0, 1, 3, 2, 4), nodes, face_map.transpose(0, 2, 1, 3),
        ],
    )
    field, on_chip, off_chip = run(
        first_z,
        [shaped((rows, 2 * face)), shaped((rows, face)), shaped((rows, face))],
        [VMEM] * (parts + 5),
        [*others, lam, mu, mod, maps, own_lam, own_mu],
    )
    near, far = exchange(on_chip, off_chip, across)
    basis, masks = run(
        tables,
        [shaped((d.terms, d.samples), BF16), shaped((6, d.subs, 8, 128))],
        [VMEM] * 4,
        [nodes, quad_weights.reshape(1, -1), chaos_index.T, bonds.transpose(0, 3, 2, 1)],
    )
    jumps_plane, part_lam, part_mu = run(
        first_plane,
        [shaped((rows, d.plane), BF16), shaped((rows, 2 * face)), shaped((rows, 2 * face))],
        [VMEM] * (parts + 5),
        [*others, lam, mu, mod, own_lam, own_mu, masks],
        scratch=[pltpu.VMEM((rows, d.plane), F32)],
    )
    jumps_z, field, on_chip, off_chip = run(
        second_z,
        [
            shaped((rows, 2 * face), BF16),
            shaped((rows, 2 * face)),
            shaped((rows, face)),
            shaped((rows + PAD, face)),
        ],
        [VMEM] * 10,
        [field, far, near, maps, masks, mod, lam, mu, part_lam, part_mu],
    )
    near, far = exchange(on_chip, off_chip, second)
    (plane,) = run(
        second_plane,
        [shaped((rows, d.plane), BF16)],
        [VMEM] * 6,
        [jumps_plane, jumps_z, lam, mu, mod, masks],
    )
    result = [shaped((1, d.height, d.breadth, d.terms, d.share), BF16)]

    def rows_out(width):
        return pltpu.VMEM((d.height, d.breadth, d.terms, width), BF16)

    if parts == 2:
        held = pltpu.VMEM((rows, face), F32)
        early, plane_out = run(
            project_plane,
            result + [shaped((d.height, d.breadth, d.terms, face), BF16)],
            [VMEM] * 2,
            [plane, basis],
            out_specs=[HBM, VMEM],
            scratch=[rows_out(d.share), pltpu.SemaphoreType.DMA(())],
        )
        early, near_out = run(
            project_near,
            result + [shaped((d.height, d.breadth, d.terms, face), BF16)],
            [VMEM] * 6 + [HBM],
            [field, near, maps, masks, basis, plane_out, early],
            out_specs=[HBM, VMEM],
            scratch=[held, pltpu.SemaphoreType.DMA((2,))],
            aliases={6: 0},
        )
        (out,) = run(
            project_late,
            result,
            [VMEM] * 7 + [HBM],
            [field, far, maps, masks, basis, plane_out, near_out, early],
            out_specs=[HBM],
            scratch=[held, rows_out(face), pltpu.SemaphoreType.DMA((3,))],
            aliases={7: 0},
        )
    else:
        last = [field, far, near, maps, masks, plane]
        held = pltpu.VMEM((rows, 2 * face), F32)
        (jumps,) = run(last_z, [shaped((rows, d.width), BF16)], [VMEM] * 6, last, scratch=[held])
        start = lax.axis_index("smp") * d.share
        jumps = lax.dynamic_slice_in_dim(jumps, start, d.share, 1)
        (out,) = run(
            project_share,
            result,
            [VMEM] * 2,
            [jumps, basis],
            out_specs=[HBM],
            scratch=[rows_out(d.share), pltpu.SemaphoreType.DMA(())],
        )
    return jnp.swapaxes(out, -1, -2)


def solution(mesh):
    return jax.shard_map(
        per_device,
        mesh=mesh,
        in_specs=(
            P("sub", None, None, "smp", None),
            P(),
            P(),
            P(None, "sub", None, None, None),
            P(),
            P(),
            P(),
            P(),
            P("sub", None, None, None),
        ),
        out_specs=P("sub", None, None, "smp", None),
        check_vma=False,
    )
```
